512 devices in a mesh: seq: 16 (over y, core), leaf: 32 (over x, z).
Axes of the slice: x: 4, y: 8, z: 8, core: 2. Of those that a mesh axis runs over, the one named last changes fastest.
Arguments:
- queries: bfloat16 [256, 4, 4096], P('leaf'), may hold values from -32 to 32
- prompt_kv: bfloat16 [2, 20480, 512], P(None, 'seq'), may hold values from -8 to 8
- node_kv: bfloat16 [2, 512, 256, 512], P(None, 'leaf', 'seq'), may hold values from -8 to 8
- node_lengths: int32 [512], P('leaf'), may hold values from 128 to 256, as said below
- ancestors: int32 [256, 10], P('leaf'), may hold values from -1 to 511, as said below
Outputs:
- attended: bfloat16 [256, 4, 4096], P('leaf', None, 'seq')
The draws below stay inside these ranges and needn't reach their ends.
Inputs may be any that keep to these rules, and one draw needn't show every extreme that they name: `ancestors`: each entry is -1 or a node id, owner * 16 + slot, whose owner is an index of leaf. The last entry of every row is the leaf's own node, owned by the index of leaf that holds the leaf. A node whose owner is not the index of leaf holding the leaf sits in slot 15 of its owner, and each owner holds one such node at most. `node_lengths`: multiples of 128.
All inputs are finite; a program needn't handle non-finite values.
Results may differ from the reference program's by a relative error of at most 0.0028.
Values may be sent and summed in bfloat16 or wider, within the bound.
No kernel may reach another device: no remote copies, remote signals or barrier semaphores. Data moves between devices by JAX's collectives and lax.ppermute only.
A program may use at most 64 MiB of HBM per device.

```python
import math
import jax
import jax.numpy as jnp
from jax import lax

HEADS = 16
KV_HEADS = 2
HEAD_DIM = 256
STEPS = 4
DEPTH = 10
BLOCK = 128
NODE_LEN = 256
LEAF_DEV = 8
P_DEV = 1280
LEAVES = 256
PROMPT = 20480
NODE_DEV = 16
NODES = 512
TOK_SEQ = 16
N_SEQ = 16


def draw_queries(key, part):
    key = jax.random.fold_in(key, 1)
    entries = jnp.clip(1.25 * jax.random.normal(key, (LEAVES, STEPS, HEADS * HEAD_DIM), jnp.float32), -6.0, 6.0)
    return entries.astype(jnp.bfloat16)


def draw_prompt_kv(key, part):
    key = jax.random.fold_in(key, 2)
    entries = jnp.clip(2.0 * jax.random.normal(key, (2, PROMPT, KV_HEADS * HEAD_DIM), jnp.float32), -8.0, 8.0)
    return entries.astype(jnp.bfloat16)


def draw_node_lengths(key, part):
    key = jax.random.fold_in(key, 3)
    block_counts = jax.random.randint(key, (NODES,), 1, NODE_LEN // BLOCK + 1)
    block_counts = block_counts.at[0].set(NODE_LEN // BLOCK).at[1].set(1)
    return (BLOCK * block_counts).astype(jnp.int32)


def draw_ancestors(key, part):
    key = jax.random.fold_in(key, 4)
    dev_count = LEAVES // LEAF_DEV
    lower_levels = LEAF_DEV.bit_length()
    upper_levels = DEPTH - lower_levels
    placed = jax.random.permutation(jax.random.fold_in(key, 1), dev_count).astype(jnp.int32)
    holder = jnp.zeros((dev_count,), jnp.int32).at[placed].set(jnp.arange(dev_count, dtype=jnp.int32))
    leaf_ids = jnp.arange(LEAVES, dtype=jnp.int32)
    device_ids = leaf_ids // LEAF_DEV
    local_ids = leaf_ids % LEAF_DEV
    position = placed[device_ids]
    bounds = jax.random.randint(jax.random.fold_in(key, 2), (dev_count,), 0, lower_levels)
    extra_depth = jax.random.randint(jax.random.fold_in(key, 3), (LEAVES,), 0, bounds[device_ids] + 1)
    extra_depth = jnp.where(local_ids == 0, lower_levels - 1, extra_depth)
    columns = []
    for level in range(DEPTH):
        if level < upper_levels:
            span_size = 2 ** (upper_levels - level)
            if span_size > dev_count:
                columns.append(jnp.full((LEAVES,), -1, jnp.int32))
            else:
                middle = position // span_size * span_size + span_size // 2
                columns.append(holder[middle] * NODE_DEV + NODE_DEV - 1)
        else:
            depth_local = level - upper_levels
            group_leaves = LEAF_DEV >> depth_local
            node_ids = device_ids * NODE_DEV + (2 ** depth_local - 1) + local_ids // group_leaves
            if depth_local < lower_levels - 1:
                node_ids = jnp.where(depth_local < extra_depth, node_ids, -1)
            columns.append(node_ids)
    return jnp.stack(columns, axis=1).astype(jnp.int32)


def shard_levels(rng, extent, pieces, smallest, high):
    gain, own = 1.0, jax.random.fold_in(rng, 6)
    for dim, shards_of in pieces:
        draws = jnp.exp(jax.random.uniform(jax.random.fold_in(own, dim), (shards_of,), jnp.float32, smallest / len(pieces), high / len(pieces)))
        gain = gain * jnp.repeat(draws, extent[dim] // shards_of).reshape([-1 if axis == dim else 1 for axis in range(len(extent))])
    return gain


def normal_values(own_key, shape, deviation, reach, shards=(), kind=jnp.bfloat16):
    array = jax.random.normal(own_key, shape, jnp.float32) * deviation
    if len(shards) > 0:
        array = shard_levels(own_key, shape, shards, -0.22, 0.18) * array
    return jnp.clip(array, min=-reach, max=reach).astype(kind)


def setup_inputs(seed: int = 0) -> dict:
    streams_of = jax.random.split(jax.random.key(seed), 6)
    return {
        "queries": draw_queries(jax.random.fold_in(streams_of[5], 71), 0),
        "prompt_kv": draw_prompt_kv(jax.random.fold_in(streams_of[5], 71), 0),
        "node_kv": normal_values(streams_of[2], (2, NODES, NODE_LEN, KV_HEADS * HEAD_DIM), 2.0, 8.0, ((1, 32), (2, 16))),
        "node_lengths": draw_node_lengths(jax.random.fold_in(streams_of[5], 71), 0),
        "ancestors": draw_ancestors(jax.random.fold_in(streams_of[5], 71), 0),
    }


def combine_parts(first_part, second_part):
    first_max, first_total, first_sum = first_part
    second_max, second_total, second_sum = second_part
    top_max = jnp.maximum(first_max, second_max)
    first_weight = jnp.exp(first_max - top_max)
    second_weight = jnp.exp(second_max - top_max)
    return (top_max, first_total * first_weight + second_total * second_weight, first_sum * first_weight[..., None] + second_sum * second_weight[..., None])

def block_parts(block_id, query_rows, prompt_kv, node_kv, node_lengths, ancestors):
    leaf_count, step_count = (query_rows.shape[0], query_rows.shape[1])
    score_scale = 1.0 / math.sqrt(HEAD_DIM)
    prompt_block = lax.dynamic_slice_in_dim(prompt_kv, (block_id * P_DEV).astype(jnp.int32), P_DEV, 1).astype(jnp.float32)
    prompt_keys = prompt_block[0].reshape(P_DEV, KV_HEADS, HEAD_DIM)
    prompt_values = prompt_block[1].reshape(P_DEV, KV_HEADS, HEAD_DIM)
    prompt_scores = jnp.einsum('lskgd,pkd->lskgp', query_rows, prompt_keys) * score_scale
    node_block = lax.dynamic_slice_in_dim(node_kv, (block_id * TOK_SEQ).astype(jnp.int32), TOK_SEQ, 2)
    safe_ids = jnp.maximum(ancestors, 0)
    picked = node_block[:, safe_ids].astype(jnp.float32)
    lengths = node_lengths[safe_ids]
    position = block_id * TOK_SEQ + jnp.arange(TOK_SEQ, dtype=jnp.int32)
    present = (ancestors >= 0)[:, :, None] & (position[None, None, :] < lengths[:, :, None])
    step_ids = jnp.arange(step_count, dtype=jnp.int32)
    own_limit = lengths[:, -1][:, None] - step_count + step_ids[None, :]
    last_level = jnp.arange(DEPTH, dtype=jnp.int32) == DEPTH - 1
    causal = jnp.logical_not(last_level)[None, None, :, None] | (position[None, None, None, :] <= own_limit[:, :, None, None])
    allowed = present[:, None] & causal
    node_keys = picked[0].reshape(leaf_count, DEPTH, TOK_SEQ, KV_HEADS, HEAD_DIM)
    node_values = picked[1].reshape(leaf_count, DEPTH, TOK_SEQ, KV_HEADS, HEAD_DIM)
    node_scores = jnp.einsum('lskgd,ljtkd->lskgjt', query_rows, node_keys) * score_scale
    node_scores = jnp.where(allowed[:, :, None, None], node_scores, -jnp.inf)
    block_max = jnp.maximum(lax.optimization_barrier(jnp.max(prompt_scores, axis=-1)), lax.optimization_barrier(jnp.max(node_scores, axis=(-2, -1))))
    prompt_weights = jnp.exp(prompt_scores - block_max[..., None])
    node_weights = jnp.exp(node_scores - block_max[..., None, None])
    block_total = lax.optimization_barrier(jnp.sum(prompt_weights, axis=-1)) + lax.optimization_barrier(jnp.sum(node_weights, axis=(-2, -1)))
    prompt_rounded = lax.optimization_barrier(prompt_weights.astype(jnp.bfloat16)).astype(jnp.float32)
    node_rounded = lax.optimization_barrier(node_weights.astype(jnp.bfloat16)).astype(jnp.float32)
    block_sum = jnp.einsum('lskgp,pkd->lskgd', prompt_rounded, prompt_values)
    block_sum = block_sum + jnp.einsum('lskgjt,ljtkd->lskgd', node_rounded, node_values)
    return (block_max, block_total, block_sum)

def reference(queries, prompt_kv, node_kv, node_lengths, ancestors):
    leaf_count, step_count, feat_width = queries.shape
    group_size = HEADS // KV_HEADS
    query_rows = queries.astype(jnp.float32).reshape(leaf_count, step_count, KV_HEADS, group_size, HEAD_DIM)

    def visit_block(carry, block_id):
        block_part = block_parts(block_id, query_rows, prompt_kv, node_kv, node_lengths, ancestors)
        return (combine_parts(carry, block_part), None)
    row_shape = (leaf_count, step_count, KV_HEADS, group_size)
    start_carry = (jnp.full(row_shape, -jnp.inf, jnp.float32), jnp.zeros(row_shape, jnp.float32), jnp.zeros(row_shape + (HEAD_DIM,), jnp.float32))
    final_carry, _ = lax.scan(visit_block, start_carry, jnp.arange(N_SEQ, dtype=jnp.int32))
    denominator = final_carry[1]
    numerator = final_carry[2]
    return (numerator / denominator[..., None]).reshape(leaf_count, step_count, feat_width).astype(jnp.bfloat16)
```

```python
import functools

import jax
import jax.numpy as jnp
from jax import lax
from jax.experimental import pallas as pl
from jax.experimental.pallas import tpu as pltpu
from jax.sharding import PartitionSpec as P

HEADS = 16
KV_HEADS = 2
HEAD_DIM = 256
GROUP = HEADS // KV_HEADS
CHUNK = 256
LANES = 128
INVALID_KEY = 256.0


def fold(x, combine):
    parts = [x[:, i : i + LANES] for i in range(0, x.shape[1], LANES)]
    return functools.reduce(combine, parts)


def node_counts(anc, ids, levels):
    counts = jnp.zeros((anc.shape[0], ids.shape[1]), jnp.float32)
    for level in levels:
        counts = counts + jnp.where(anc[:, level : level + 1] == ids, 1.0, 0.0)
    return counts


def tall(mask, reps):
    return jnp.concatenate([mask] * reps, axis=0)


def attend_kernel(
    steps, place_ref, lengths_ref, anc_ref, q_ref, prompt_ref, node_ref, shared_ref, out_ref, s_ref
):
    leaf_count, level_count = anc_ref.shape
    node_slots = lengths_ref.shape[0]
    owners = shared_ref.shape[0]
    node_cols = node_ref.shape[1]
    tokens = node_cols // node_slots
    prompt_cols = prompt_ref.shape[1]
    shared_cols = owners * tokens
    rows = steps * leaf_count
    first_pos = place_ref[0] * tokens
    device = place_ref[1]
    anc = anc_ref[...]

    lane = lax.broadcasted_iota(jnp.int32, (1, node_cols), 1)
    slot = lane // tokens
    position = first_pos + lane % tokens
    length = jnp.zeros((1, node_cols), jnp.int32)
    for n in range(node_slots):
        length = jnp.where(slot == n, lengths_ref[n], length)
    ids = device * node_slots + slot
    upper = node_counts(anc, ids, range(level_count - 1))
    own = node_counts(anc, ids, [level_count - 1])
    local_mult = []
    for step in range(steps):
        causal = jnp.where(position <= length - steps + step, 1.0, 0.0)
        local_mult.append(jnp.where(position < length, upper + own * causal, 0.0))
    local_mult = jnp.concatenate(local_mult, axis=0)

    lane = lax.broadcasted_iota(jnp.int32, (1, shared_cols), 1)
    owner = lane // tokens
    shared_count = node_counts(anc, owner * node_slots + node_slots - 1, range(level_count - 1))
    shared_count = jnp.where(owner == device, 0.0, shared_count)

    for k in range(KV_HEADS):
        cols = slice(k * HEAD_DIM, (k + 1) * HEAD_DIM)
        query = jnp.concatenate(
            [q_ref[:, (k * GROUP + h) * HEAD_DIM : (k * GROUP + h + 1) * HEAD_DIM] for h in range(GROUP)], axis=0
        )
        query = query * jnp.bfloat16(1.0 / 16.0)

        def scores(keys):
            return lax.dot_general(query, keys, (((1,), (1,)), ((), ())), preferred_element_type=jnp.float32)

        top = None
        for start in range(0, prompt_cols, CHUNK):
            s = scores(prompt_ref[0, start : start + CHUNK, cols])
            s_ref[:, start : start + CHUNK] = s
            part = fold(s, jnp.maximum)
            top = part if top is None else jnp.maximum(top, part)
        s = scores(node_ref[0, :, cols])
        s = jnp.where(tall(local_mult, GROUP) > 0.0, s, -jnp.inf)
        s_ref[:, prompt_cols : prompt_cols + node_cols] = s
        top = jnp.maximum(top, fold(s, jnp.maximum))
        shared_keys = shared_ref[:, 0:tokens, cols].reshape(shared_cols, HEAD_DIM)
        flags = lax.dot_general(
            jnp.where(lax.broadcasted_iota(jnp.int32, (8, HEAD_DIM), 1) == 0, 1.0, 0.0).astype(jnp.bfloat16),
            shared_keys,
            (((1,), (1,)), ((), ())),
            preferred_element_type=jnp.float32,
        )
        shared_mult = jnp.where(flags[0:1] < INVALID_KEY / 2, shared_count, 0.0)
        shared_mult = tall(shared_mult, steps)
        s = scores(shared_keys)
        s = jnp.where(tall(shared_mult, GROUP) > 0.0, s, -jnp.inf)
        s_ref[:, prompt_cols + node_cols : prompt_cols + node_cols + shared_cols] = s
        top = jnp.maximum(top, fold(s, jnp.maximum))
        block_max = jnp.max(top, axis=1, keepdims=True)

        total = jnp.zeros((GROUP * rows, LANES), jnp.float32)
        acc = jnp.zeros((GROUP * rows, HEAD_DIM), jnp.float32)
        for start in range(0, prompt_cols, CHUNK):
            w = jnp.exp(s_ref[:, start : start + CHUNK] - block_max)
            total = total + fold(w, jnp.add)
            acc = acc + jnp.dot(
                w.astype(jnp.bfloat16), prompt_ref[1, start : start + CHUNK, cols], preferred_element_type=jnp.float32
            )
        w = jnp.exp(s_ref[:, prompt_cols : prompt_cols + node_cols] - block_max) * tall(local_mult, GROUP)
        total = total + fold(w, jnp.add)
        acc = acc + jnp.dot(w.astype(jnp.bfloat16), node_ref[1, :, cols], preferred_element_type=jnp.float32)
        w = jnp.exp(
            s_ref[:, prompt_cols + node_cols : prompt_cols + node_cols + shared_cols] - block_max
        ) * tall(shared_mult, GROUP)
        total = total + fold(w, jnp.add)
        shared_values = shared_ref[:, tokens : 2 * tokens, cols].reshape(shared_cols, HEAD_DIM)
        acc = acc + jnp.dot(w.astype(jnp.bfloat16), shared_values, preferred_element_type=jnp.float32)
        total = jnp.sum(total, axis=1, keepdims=True)

        half = rows // 2
        lane = lax.broadcasted_iota(jnp.int32, (GROUP * rows, LANES), 1)
        stats = jnp.where(lane == 0, block_max, jnp.where(lane == 1, total, 0.0))
        for h in range(GROUP):
            for part in range(2):
                first = h * rows + part * half
                out_ref[k * GROUP + h, :, part * HEAD_DIM : (part + 1) * HEAD_DIM] = acc[first : first + half]
            low, high = stats[h * rows : h * rows + half], stats[h * rows + half : (h + 1) * rows]
            out_ref[k * GROUP + h, :, 2 * HEAD_DIM :] = jnp.where(
                lane[:half] < LANES // 2, low, pltpu.roll(high, LANES // 2, 1)
            )


def merge_kernel(parts_ref, out_ref):
    blocks, half, _ = parts_ref.shape
    leaf_count, steps, _ = out_ref.shape
    for part in range(2):
        first = part * LANES // 2
        stats = [parts_ref[b, :, 2 * HEAD_DIM :] for b in range(blocks)]
        tops = [st[:, first : first + 1] for st in stats]
        row_max = functools.reduce(jnp.maximum, tops)
        denominator = jnp.zeros((half, 1), jnp.float32)
        numerator = jnp.zeros((half, HEAD_DIM), jnp.float32)
        for b in range(blocks):
            scale = jnp.exp(tops[b] - row_max)
            denominator = denominator + scale * stats[b][:, first + 1 : first + 2]
            numerator = numerator + scale * parts_ref[b, :, part * HEAD_DIM : (part + 1) * HEAD_DIM]
        merged = (numerator / denominator).astype(jnp.bfloat16)
        for i in range(half // leaf_count):
            out_ref[:, part * half // leaf_count + i, :] = merged[i * leaf_count : (i + 1) * leaf_count]


def shards(queries, prompt_kv, node_kv, node_lengths, ancestors):
    leaf_count, steps, feat_width = queries.shape
    node_slots, tokens = node_kv.shape[1:3]
    width = KV_HEADS * HEAD_DIM
    rows = steps * leaf_count
    blocks = lax.axis_size("seq")
    owners = lax.axis_size("leaf")
    place = jnp.stack([lax.axis_index("seq"), lax.axis_index("leaf")]).astype(jnp.int32)

    present = lax.axis_index("seq") * tokens < node_lengths[node_slots - 1]
    last = node_kv[:, node_slots - 1]
    last = jnp.stack([jnp.where(present, last[0], jnp.bfloat16(INVALID_KEY)), last[1]])
    last = jnp.broadcast_to(last.reshape(1, 2 * tokens, width), (owners, 2 * tokens, width))
    shared = lax.all_to_all(last, "leaf", 0, 0, tiled=True)

    query_rows = queries.transpose(1, 0, 2).reshape(rows, feat_width)
    cols = prompt_kv.shape[1] + node_slots * tokens + owners * tokens
    vmem = pl.BlockSpec(memory_space=pltpu.VMEM)
    smem = pl.BlockSpec(memory_space=pltpu.SMEM)
    parts = pl.pallas_call(
        functools.partial(attend_kernel, steps),
        out_shape=jax.ShapeDtypeStruct((HEADS, rows // 2, 2 * HEAD_DIM + LANES), jnp.float32),
        in_specs=[smem, smem, vmem, vmem, vmem, vmem, vmem],
        out_specs=vmem,
        scratch_shapes=[pltpu.VMEM((GROUP * rows, cols), jnp.float32)],
        compiler_params=pltpu.CompilerParams(vmem_limit_bytes=32 * 1024 * 1024),
    )(
        place,
        node_lengths,
        ancestors,
        query_rows,
        prompt_kv,
        node_kv.reshape(2, node_slots * tokens, width),
        shared,
    )
    parts = lax.all_to_all(parts, "seq", 0, 0, tiled=True)
    return pl.pallas_call(
        merge_kernel,
        out_shape=jax.ShapeDtypeStruct((leaf_count, steps, HEAD_DIM), jnp.bfloat16),
        in_specs=[vmem],
        out_specs=vmem,
        compiler_params=pltpu.CompilerParams(vmem_limit_bytes=32 * 1024 * 1024),
    )(parts)


def solution(mesh):
    placed = (
        P("leaf", None, None),
        P(None, "seq", None),
        P(None, "leaf", "seq", None),
        P("leaf"),
        P("leaf", None),
    )
    return jax.shard_map(
        shards, mesh=mesh, in_specs=placed, out_specs=P("leaf", None, "seq"), check_vma=False
    )
```

```python
import functools

import jax
import jax.numpy as jnp
from jax import lax
from jax.experimental import pallas as pl
from jax.experimental.pallas import tpu as pltpu
from jax.sharding import PartitionSpec as P

HEADS = 16
KV_HEADS = 2
HEAD_DIM = 256
GROUP = HEADS // KV_HEADS
CHUNK = 256
LANES = 128
Z = 8
INVALID_KEY = 256.0
TOP = 32767.0
POINTS = (2.0**18, 2.0**26, 2.0**23)

VMEM = pl.BlockSpec(memory_space=pltpu.VMEM)
SMEM = pl.BlockSpec(memory_space=pltpu.SMEM)


def params(mib):
    return pltpu.CompilerParams(vmem_limit_bytes=mib * 1024 * 1024)


def fold(x, combine):
    parts = [x[:, i : i + LANES] for i in range(0, x.shape[1], LANES)]
    return functools.reduce(combine, parts)


def tall(x, reps):
    return jnp.concatenate([x] * reps, axis=0)


def node_counts(anc, ids, levels):
    counts = jnp.zeros((anc.shape[0], ids.shape[1]), jnp.float32)
    for level in levels:
        counts = counts + jnp.where(anc[:, level : level + 1] == ids, 1.0, 0.0)
    return counts


def group_query(q_ref, k):
    heads = range(k * GROUP, (k + 1) * GROUP)
    query = jnp.concatenate([q_ref[:, h * HEAD_DIM : (h + 1) * HEAD_DIM] for h in heads], axis=0)
    return query * jnp.bfloat16(1.0 / 16.0)


def dot_nt(a, b):
    return lax.dot_general(a, b, (((1,), (1,)), ((), ())), preferred_element_type=jnp.float32)


def post_kernel(lengths_ref, node_ref, out_ref):
    node_slots = lengths_ref.shape[0]
    tokens = node_ref.shape[2]
    present = lax.axis_index("seq") * tokens < lengths_ref[node_slots - 1]
    keys = jnp.where(present, node_ref[0, 0], jnp.bfloat16(INVALID_KEY))
    values = node_ref[1, 0]
    for copy in range(out_ref.shape[0]):
        out_ref[copy, 0:tokens] = keys
        out_ref[copy, tokens : 2 * tokens] = values


def early_kernel(steps, lengths_ref, anc_ref, q_ref, prompt_ref, node_ref, w_ref, max_ref, total_ref):
    leaf_count, level_count = anc_ref.shape
    node_slots = lengths_ref.shape[0]
    node_cols = node_ref.shape[1]
    tokens = node_cols // node_slots
    prompt_cols = prompt_ref.shape[1]
    anc = anc_ref[...]

    lane = lax.broadcasted_iota(jnp.int32, (1, node_cols), 1)
    slot = lane // tokens
    position = lax.axis_index("seq") * tokens + lane % tokens
    length = jnp.zeros((1, node_cols), jnp.int32)
    for n in range(node_slots):
        length = jnp.where(slot == n, lengths_ref[n], length)
    ids = lax.axis_index("leaf") * node_slots + slot
    upper = node_counts(anc, ids, range(level_count - 1))
    own = node_counts(anc, ids, [level_count - 1])
    mult = []
    for step in range(steps):
        causal = jnp.where(position <= length - steps + step, 1.0, 0.0)
        mult.append(jnp.where(position < length, upper + own * causal, 0.0))
    mult = tall(jnp.concatenate(mult, axis=0), GROUP)

    for k in range(KV_HEADS):
        cols = slice(k * HEAD_DIM, (k + 1) * HEAD_DIM)
        query = group_query(q_ref, k)
        top = None
        for start in range(0, prompt_cols, CHUNK):
            s = dot_nt(query, prompt_ref[0, start : start + CHUNK, cols])
            w_ref[k, :, start : start + CHUNK] = s
            part = fold(s, jnp.maximum)
            top = part if top is None else jnp.maximum(top, part)
        s = dot_nt(query, node_ref[0, :, cols])
        s = jnp.where(mult > 0.0, s, -jnp.inf)
        w_ref[k, :, prompt_cols:] = s
        top = jnp.max(jnp.maximum(top, fold(s, jnp.maximum)), axis=1, keepdims=True)
        total = jnp.zeros((s.shape[0], LANES), jnp.float32)
        for start in range(0, prompt_cols, CHUNK):
            w = jnp.exp(w_ref[k, :, start : start + CHUNK] - top)
            w_ref[k, :, start : start + CHUNK] = w
            total = total + fold(w, jnp.add)
        w = jnp.exp(w_ref[k, :, prompt_cols:] - top) * mult
        w_ref[k, :, prompt_cols:] = w
        total = total + fold(w, jnp.add)
        total_ref[k] = jnp.broadcast_to(jnp.sum(total, axis=1, keepdims=True), total.shape)
        max_ref[k] = jnp.broadcast_to(top, total.shape)


def late_kernel(
    steps, node_slots, anc_ref, q_ref, shared_ref, w_ref, max_ref, total_ref, prompt_ref, node_ref, out_ref
):
    leaf_count, level_count = anc_ref.shape
    owners = shared_ref.shape[0]
    tokens = shared_ref.shape[1] // 2
    prompt_cols = prompt_ref.shape[1]
    shared_cols = owners * tokens
    rows = steps * leaf_count
    half = rows // 2

    lane = lax.broadcasted_iota(jnp.int32, (1, shared_cols), 1)
    owner = lane // tokens
    count = node_counts(anc_ref[...], owner * node_slots + node_slots - 1, range(level_count - 1))
    count = jnp.where(owner == lax.axis_index("leaf"), 0.0, count)
    pick = jnp.where(lax.broadcasted_iota(jnp.int32, (8, HEAD_DIM), 1) == 0, 1.0, 0.0).astype(jnp.bfloat16)

    for k in range(KV_HEADS):
        cols = slice(k * HEAD_DIM, (k + 1) * HEAD_DIM)
        keys = shared_ref[:, 0:tokens, cols].reshape(shared_cols, HEAD_DIM)
        values = shared_ref[:, tokens : 2 * tokens, cols].reshape(shared_cols, HEAD_DIM)
        marks = dot_nt(pick, keys)[0:1]
        mult = tall(jnp.where(marks < INVALID_KEY / 2, count, 0.0), steps * GROUP)
        s = dot_nt(group_query(q_ref, k), keys)
        s = jnp.where(mult > 0.0, s, -jnp.inf)
        early_max = max_ref[k]
        block_max = jnp.maximum(jnp.max(fold(s, jnp.maximum), axis=1, keepdims=True), early_max)
        scale = jnp.exp(early_max - block_max)
        w = jnp.exp(s - block_max[:, 0:1]) * mult
        total = jnp.sum(fold(w, jnp.add), axis=1, keepdims=True) + total_ref[k] * scale
        acc = jnp.dot(w.astype(jnp.bfloat16), values, preferred_element_type=jnp.float32)
        wide = jnp.concatenate([scale, scale], axis=1)
        for start in range(0, prompt_cols, CHUNK):
            w = (w_ref[k, :, start : start + CHUNK] * wide).astype(jnp.bfloat16)
            acc = acc + jnp.dot(w, prompt_ref[0, start : start + CHUNK, cols], preferred_element_type=jnp.float32)
        w = (w_ref[k, :, prompt_cols:] * wide).astype(jnp.bfloat16)
        acc = acc + jnp.dot(w, node_ref[0, :, cols], preferred_element_type=jnp.float32)

        reach = jnp.maximum(jnp.max(fold(jnp.abs(acc), jnp.maximum), axis=1, keepdims=True), 1e-30)
        data = jnp.round(acc * (TOP / reach)).astype(jnp.int32).astype(jnp.int16)
        fixed = [
            jnp.round(value * point).astype(jnp.int32)
            for value, point in zip((block_max, jnp.log(total), jnp.log(reach)), POINTS)
        ]
        lane = lax.broadcasted_iota(jnp.int32, (GROUP * rows, LANES), 1)
        stats = jnp.zeros((GROUP * rows, LANES), jnp.int32)
        for i, value in enumerate(fixed):
            stats = jnp.where(lane == 2 * i, value >> 16, stats)
            stats = jnp.where(lane == 2 * i + 1, (value & 0xFFFF) - 0x8000, stats)
        lane = lane[:half]
        for h in range(GROUP):
            first = h * rows
            for part in range(2):
                lanes = slice(part * HEAD_DIM, (part + 1) * HEAD_DIM)
                out_ref[k * GROUP + h, :, lanes] = data[first + part * half : first + (part + 1) * half]
            low, high = stats[first : first + half], stats[first + half : first + rows]
            both = jnp.where(lane < LANES // 2, low, pltpu.roll(high, LANES // 2, 1))
            out_ref[k * GROUP + h, :, 2 * HEAD_DIM :] = both.astype(jnp.int16)


def merge_kernel(parts_ref, out_ref):
    blocks, half, _ = parts_ref.shape
    leaf_count = out_ref.shape[0]
    stats = [parts_ref[b, :, 2 * HEAD_DIM :].astype(jnp.int32) for b in range(blocks)]
    for part in range(2):
        first = part * LANES // 2

        def value(b, i):
            high = stats[b][:, first + 2 * i : first + 2 * i + 1]
            low = stats[b][:, first + 2 * i + 1 : first + 2 * i + 2] + 0x8000
            return ((high << 16) + low).astype(jnp.float32) * (1.0 / POINTS[i])

        tops = [value(b, 0) for b in range(blocks)]
        row_max = functools.reduce(jnp.maximum, tops)
        denominator = jnp.zeros((half, 1), jnp.float32)
        numerator = jnp.zeros((half, HEAD_DIM), jnp.float32)
        for b in range(blocks):
            shift = tops[b] - row_max
            denominator = denominator + jnp.exp(shift + value(b, 1))
            data = parts_ref[b, :, part * HEAD_DIM : (part + 1) * HEAD_DIM].astype(jnp.int32).astype(jnp.float32)
            numerator = numerator + jnp.exp(shift + value(b, 2)) * data
        merged = (numerator / (denominator * TOP)).astype(jnp.bfloat16)
        for i in range(half // leaf_count):
            out_ref[:, part * half // leaf_count + i, :] = merged[i * leaf_count : (i + 1) * leaf_count]


def gather_shared(own, owners):
    along_z = [list(range(x, x + Z)) for x in range(0, owners, Z)]
    along_x = [list(range(z, owners, Z)) for z in range(Z)]
    plane = lax.all_to_all(own, "leaf", 0, 0, tiled=True, axis_index_groups=along_z)
    plane = jnp.broadcast_to(plane[None], (owners // Z,) + plane.shape)
    shared = lax.all_to_all(plane, "leaf", 0, 0, tiled=True, axis_index_groups=along_x)
    return shared.reshape((owners,) + own.shape[1:])


def shards(queries, prompt_kv, node_kv, node_lengths, ancestors):
    leaf_count, steps, feat_width = queries.shape
    node_slots, tokens = node_kv.shape[1:3]
    prompt_cols = prompt_kv.shape[1]
    width = KV_HEADS * HEAD_DIM
    rows = steps * leaf_count
    owners = lax.axis_size("leaf")

    own = pl.pallas_call(
        post_kernel,
        out_shape=jax.ShapeDtypeStruct((Z, 2 * tokens, width), jnp.bfloat16),
        grid=(1,),
        in_specs=[SMEM, pl.BlockSpec((2, 1, tokens, width), lambda i: (0, node_slots - 1, 0, 0))],
        out_specs=VMEM,
        compiler_params=params(8),
    )(node_lengths, node_kv)
    shared = gather_shared(own, owners)

    query_rows = queries.transpose(1, 0, 2).reshape(rows, feat_width)
    nodes = node_kv.reshape(2, node_slots * tokens, width)
    cols = prompt_cols + node_slots * tokens
    keys_of = lambda n: pl.BlockSpec((1, n, width), lambda i: (0, 0, 0))
    values_of = lambda n: pl.BlockSpec((1, n, width), lambda i: (1, 0, 0))
    row_shape = jax.ShapeDtypeStruct((KV_HEADS, GROUP * rows, LANES), jnp.float32)
    early, early_max, early_total = pl.pallas_call(
        functools.partial(early_kernel, steps),
        out_shape=(jax.ShapeDtypeStruct((KV_HEADS, GROUP * rows, cols), jnp.float32), row_shape, row_shape),
        grid=(1,),
        in_specs=[SMEM, VMEM, VMEM, keys_of(prompt_cols), keys_of(node_slots * tokens)],
        out_specs=(VMEM, VMEM, VMEM),
        compiler_params=params(16),
        cost_estimate=pl.CostEstimate(flops=500_000_000, bytes_accessed=6_000_000, transcendentals=800_000),
    )(node_lengths, ancestors, query_rows, prompt_kv, nodes)

    parts = pl.pallas_call(
        functools.partial(late_kernel, steps, node_slots),
        out_shape=jax.ShapeDtypeStruct((HEADS, rows // 2, 2 * HEAD_DIM + LANES), jnp.int16),
        grid=(1,),
        in_specs=[VMEM, VMEM, VMEM, VMEM, VMEM, VMEM, values_of(prompt_cols), values_of(node_slots * tokens)],
        out_specs=VMEM,
        compiler_params=params(16),
    )(ancestors, query_rows, shared, early, early_max, early_total, prompt_kv, nodes)

    parts = lax.all_to_all(parts, "seq", 0, 0, tiled=True)
    return pl.pallas_call(
        merge_kernel,
        out_shape=jax.ShapeDtypeStruct((leaf_count, steps, HEAD_DIM), jnp.bfloat16),
        in_specs=[VMEM],
        out_specs=VMEM,
        compiler_params=params(8),
    )(parts)


def solution(mesh):
    placed = (
        P("leaf", None, None),
        P(None, "seq", None),
        P(None, "leaf", "seq", None),
        P("leaf"),
        P("leaf", None),
    )
    return jax.shard_map(
        shards, mesh=mesh, in_specs=placed, out_specs=P("leaf", None, "seq"), check_vma=False
    )
```

```python
import functools

import jax
import jax.numpy as jnp
from jax import lax
from jax.experimental import pallas as pl
from jax.experimental.pallas import tpu as pltpu
from jax.sharding import PartitionSpec as P

HEADS = 16
KV_HEADS = 2
HEAD_DIM = 256
GROUP = HEADS // KV_HEADS
CHUNK = 256
LANES = 128
Z = 8
INVALID_KEY = 256.0
TOP = 32767.0
POINTS = (2.0**18, 2.0**26, 2.0**23)

VMEM = pl.BlockSpec(memory_space=pltpu.VMEM)
HBM = pl.BlockSpec(memory_space=pltpu.HBM)


def in_hbm(*arrays):
    return [pltpu.with_memory_space_constraint(array, pltpu.HBM) for array in arrays]


def params(mib):
    return pltpu.CompilerParams(vmem_limit_bytes=mib * 1024 * 1024)


def fold(x, combine):
    parts = [x[:, i : i + LANES] for i in range(0, x.shape[1], LANES)]
    return functools.reduce(combine, parts)


def tall(x, reps):
    return jnp.concatenate([x] * reps, axis=0)


def node_counts(anc, ids, levels):
    counts = jnp.zeros((anc.shape[0], ids.shape[1]), jnp.float32)
    for level in levels:
        counts = counts + jnp.where(anc[:, level : level + 1] == ids, 1.0, 0.0)
    return counts


def group_query(q_ref, k):
    heads = range(k * GROUP, (k + 1) * GROUP)
    query = jnp.concatenate([q_ref[:, h * HEAD_DIM : (h + 1) * HEAD_DIM] for h in heads], axis=0)
    return query * jnp.bfloat16(1.0 / 16.0)


def dot_nt(a, b):
    return lax.dot_general(a, b, (((1,), (1,)), ((), ())), preferred_element_type=jnp.float32)


def fetch(pairs, sems):
    copies = [pltpu.make_async_copy(src, dst, sems.at[i]) for i, (src, dst) in enumerate(pairs)]
    for copy in copies:
        copy.start()
    return copies


def post_kernel(lengths_hbm, node_hbm, out_ref, node_ref, lengths_ref, sems):
    node_slots = lengths_hbm.shape[0]
    tokens = node_ref.shape[1]
    for copy in fetch([(node_hbm.at[:, node_slots - 1], node_ref), (lengths_hbm, lengths_ref)], sems):
        copy.wait()
    present = lax.axis_index("seq") * tokens < lengths_ref[node_slots - 1]
    keys = jnp.where(present, node_ref[0], jnp.bfloat16(INVALID_KEY))
    values = node_ref[1]
    for copy in range(out_ref.shape[0]):
        out_ref[copy, 0:tokens] = keys
        out_ref[copy, tokens : 2 * tokens] = values


def copies_kernel(plane_ref, out_ref):
    for copy in range(out_ref.shape[0]):
        out_ref[copy] = plane_ref[...]


def early_kernel(
    steps,
    lengths_hbm,
    anc_hbm,
    prompt_hbm,
    node_hbm,
    q_ref,
    w_ref,
    max_ref,
    total_ref,
    query_ref,
    count_ref,
    prompt_values_ref,
    node_values_ref,
    lengths_ref,
    anc_ref,
    prompt_ref,
    node_ref,
    sems,
):
    copies = fetch(
        [
            (lengths_hbm, lengths_ref),
            (anc_hbm, anc_ref),
            (node_hbm.at[0], node_ref),
            (prompt_hbm.at[0], prompt_ref),
            (node_hbm.at[1], node_values_ref),
            (prompt_hbm.at[1], prompt_values_ref),
        ],
        sems,
    )
    leaf_count, level_count = anc_ref.shape
    node_slots, tokens, width = node_ref.shape
    node_cols = node_slots * tokens
    prompt_cols = prompt_ref.shape[0]
    shared_cols = count_ref.shape[1]
    for k in range(KV_HEADS):
        query_ref[k] = group_query(q_ref, k)
    copies[0].wait()
    copies[1].wait()
    anc = anc_ref[...]

    lane = lax.broadcasted_iota(jnp.int32, (1, shared_cols), 1)
    owner = lane // tokens
    count = node_counts(anc, owner * node_slots + node_slots - 1, range(level_count - 1))
    count_ref[...] = jnp.where(owner == lax.axis_index("leaf"), 0.0, count)

    lane = lax.broadcasted_iota(jnp.int32, (1, node_cols), 1)
    slot = lane // tokens
    position = lax.axis_index("seq") * tokens + lane % tokens
    length = jnp.zeros((1, node_cols), jnp.int32)
    for n in range(node_slots):
        length = jnp.where(slot == n, lengths_ref[n], length)
    ids = lax.axis_index("leaf") * node_slots + slot
    upper = node_counts(anc, ids, range(level_count - 1))
    own = node_counts(anc, ids, [level_count - 1])
    mult = []
    for step in range(steps):
        causal = jnp.where(position <= length - steps + step, 1.0, 0.0)
        mult.append(jnp.where(position < length, upper + own * causal, 0.0))
    mult = tall(jnp.concatenate(mult, axis=0), GROUP)
    copies[2].wait()
    copies[3].wait()

    for k in range(KV_HEADS):
        cols = slice(k * HEAD_DIM, (k + 1) * HEAD_DIM)
        query = query_ref[k]
        top = None
        for start in range(0, prompt_cols, CHUNK):
            s = dot_nt(query, prompt_ref[start : start + CHUNK, cols])
            w_ref[k, :, start : start + CHUNK] = s
            part = fold(s, jnp.maximum)
            top = part if top is None else jnp.maximum(top, part)
        s = dot_nt(query, node_ref[:, :, cols].reshape(node_cols, HEAD_DIM))
        s = jnp.where(mult > 0.0, s, -jnp.inf)
        w_ref[k, :, prompt_cols:] = s
        top = jnp.max(jnp.maximum(top, fold(s, jnp.maximum)), axis=1, keepdims=True)
        total = jnp.zeros((s.shape[0], LANES), jnp.float32)
        for start in range(0, prompt_cols, CHUNK):
            w = jnp.exp(w_ref[k, :, start : start + CHUNK] - top)
            w_ref[k, :, start : start + CHUNK] = w
            total = total + fold(w, jnp.add)
        w = jnp.exp(w_ref[k, :, prompt_cols:] - top) * mult
        w_ref[k, :, prompt_cols:] = w
        total = total + fold(w, jnp.add)
        total_ref[k] = jnp.broadcast_to(jnp.sum(total, axis=1, keepdims=True), total.shape)
        max_ref[k] = jnp.broadcast_to(top, total.shape)
    copies[4].wait()
    copies[5].wait()


def late_kernel(query_ref, shared_ref, w_ref, max_ref, total_ref, count_ref, prompt_ref, node_ref, out_ref):
    owners = shared_ref.shape[0]
    tokens = shared_ref.shape[1] // 2
    prompt_cols = prompt_ref.shape[0]
    node_cols = node_ref.shape[0] * node_ref.shape[1]
    shared_cols = owners * tokens
    rows = query_ref.shape[1] // GROUP
    half = rows // 2
    count = count_ref[...]
    reps = GROUP * rows // count.shape[0]
    pick = jnp.where(lax.broadcasted_iota(jnp.int32, (8, HEAD_DIM), 1) == 0, 1.0, 0.0).astype(jnp.bfloat16)

    for k in range(KV_HEADS):
        cols = slice(k * HEAD_DIM, (k + 1) * HEAD_DIM)
        keys = shared_ref[:, 0:tokens, cols].reshape(shared_cols, HEAD_DIM)
        values = shared_ref[:, tokens : 2 * tokens, cols].reshape(shared_cols, HEAD_DIM)
        marks = dot_nt(pick, keys)[0:1]
        mult = tall(jnp.where(marks < INVALID_KEY / 2, count, 0.0), reps)
        s = dot_nt(query_ref[k], keys)
        s = jnp.where(mult > 0.0, s, -jnp.inf)
        early_max = max_ref[k]
        block_max = jnp.maximum(jnp.max(fold(s, jnp.maximum), axis=1, keepdims=True), early_max)
        scale = jnp.exp(early_max - block_max)
        w = jnp.exp(s - block_max[:, 0:1]) * mult
        total = jnp.sum(fold(w, jnp.add), axis=1, keepdims=True) + total_ref[k] * scale
        acc = jnp.dot(w.astype(jnp.bfloat16), values, preferred_element_type=jnp.float32)
        wide = jnp.concatenate([scale, scale], axis=1)
        for start in range(0, prompt_cols, CHUNK):
            w = (w_ref[k, :, start : start + CHUNK] * wide).astype(jnp.bfloat16)
            acc = acc + jnp.dot(w, prompt_ref[start : start + CHUNK, cols], preferred_element_type=jnp.float32)
        w = (w_ref[k, :, prompt_cols:] * wide).astype(jnp.bfloat16)
        node_values = node_ref[:, :, cols].reshape(node_cols, HEAD_DIM)
        acc = acc + jnp.dot(w, node_values, preferred_element_type=jnp.float32)

        reach = jnp.maximum(jnp.max(fold(jnp.abs(acc), jnp.maximum), axis=1, keepdims=True), 1e-30)
        data = jnp.round(acc * (TOP / reach)).astype(jnp.int32).astype(jnp.int16)
        fixed = [
            jnp.round(value * point).astype(jnp.int32)
            for value, point in zip((block_max, jnp.log(total), jnp.log(reach)), POINTS)
        ]
        lane = lax.broadcasted_iota(jnp.int32, (GROUP * rows, LANES), 1)
        stats = jnp.zeros((GROUP * rows, LANES), jnp.int32)
        for i, value in enumerate(fixed):
            stats = jnp.where(lane == 2 * i, value >> 16, stats)
            stats = jnp.where(lane == 2 * i + 1, (value & 0xFFFF) - 0x8000, stats)
        lane = lane[:half]
        for h in range(GROUP):
            first = h * rows
            for part in range(2):
                lanes = slice(part * HEAD_DIM, (part + 1) * HEAD_DIM)
                out_ref[k * GROUP + h, :, lanes] = data[first + part * half : first + (part + 1) * half]
            low, high = stats[first : first + half], stats[first + half : first + rows]
            both = jnp.where(lane < LANES // 2, low, pltpu.roll(high, LANES // 2, 1))
            out_ref[k * GROUP + h, :, 2 * HEAD_DIM :] = both.astype(jnp.int16)


def merge_kernel(parts_ref, out_ref):
    blocks, half, _ = parts_ref.shape
    leaf_count = out_ref.shape[0]
    stats = [parts_ref[b, :, 2 * HEAD_DIM :].astype(jnp.int32) for b in range(blocks)]
    for part in range(2):
        first = part * LANES // 2

        def value(b, i):
            high = stats[b][:, first + 2 * i : first + 2 * i + 1]
            low = stats[b][:, first + 2 * i + 1 : first + 2 * i + 2] + 0x8000
            return ((high << 16) + low).astype(jnp.float32) * (1.0 / POINTS[i])

        tops = [value(b, 0) for b in range(blocks)]
        row_max = functools.reduce(jnp.maximum, tops)
        denominator = jnp.zeros((half, 1), jnp.float32)
        numerator = jnp.zeros((half, HEAD_DIM), jnp.float32)
        for b in range(blocks):
            shift = tops[b] - row_max
            denominator = denominator + jnp.exp(shift + value(b, 1))
            data = parts_ref[b, :, part * HEAD_DIM : (part + 1) * HEAD_DIM].astype(jnp.int32).astype(jnp.float32)
            numerator = numerator + jnp.exp(shift + value(b, 2)) * data
        merged = (numerator / (denominator * TOP)).astype(jnp.bfloat16)
        for i in range(half // leaf_count):
            out_ref[:, part * half // leaf_count + i, :] = merged[i * leaf_count : (i + 1) * leaf_count]


def gather_shared(own, owners):
    along_z = [list(range(x, x + Z)) for x in range(0, owners, Z)]
    along_x = [list(range(z, owners, Z)) for z in range(Z)]
    plane = lax.all_to_all(own, "leaf", 0, 0, tiled=True, axis_index_groups=along_z)
    plane = pl.pallas_call(
        copies_kernel,
        out_shape=jax.ShapeDtypeStruct((owners // Z,) + plane.shape, plane.dtype),
        in_specs=[VMEM],
        out_specs=VMEM,
        compiler_params=params(8),
    )(plane)
    shared = lax.all_to_all(plane, "leaf", 0, 0, tiled=True, axis_index_groups=along_x)
    return shared.reshape((owners,) + own.shape[1:])


def shards(queries, prompt_kv, node_kv, node_lengths, ancestors):
    leaf_count, steps, feat_width = queries.shape
    node_slots, tokens = node_kv.shape[1:3]
    prompt_cols = prompt_kv.shape[1]
    width = KV_HEADS * HEAD_DIM
    rows = steps * leaf_count
    owners = lax.axis_size("leaf")

    own = pl.pallas_call(
        post_kernel,
        out_shape=jax.ShapeDtypeStruct((Z, 2 * tokens, width), jnp.bfloat16),
        in_specs=[HBM, HBM],
        out_specs=VMEM,
        scratch_shapes=[
            pltpu.VMEM((2, tokens, width), jnp.bfloat16),
            pltpu.SMEM((node_slots,), jnp.int32),
            pltpu.SemaphoreType.DMA((2,)),
        ],
        compiler_params=params(8),
    )(*in_hbm(node_lengths, node_kv))
    shared = gather_shared(own, owners)

    query_rows = queries.transpose(1, 0, 2).reshape(rows, feat_width)
    cols = prompt_cols + node_slots * tokens
    row_shape = jax.ShapeDtypeStruct((KV_HEADS, GROUP * rows, LANES), jnp.float32)
    weights, early_max, early_total, query, count, prompt_values, node_values = pl.pallas_call(
        functools.partial(early_kernel, steps),
        out_shape=(
            jax.ShapeDtypeStruct((KV_HEADS, GROUP * rows, cols), jnp.float32),
            row_shape,
            row_shape,
            jax.ShapeDtypeStruct((KV_HEADS, GROUP * rows, HEAD_DIM), jnp.bfloat16),
            jax.ShapeDtypeStruct((leaf_count, owners * tokens), jnp.float32),
            jax.ShapeDtypeStruct((prompt_cols, width), jnp.bfloat16),
            jax.ShapeDtypeStruct((node_slots, tokens, width), jnp.bfloat16),
        ),
        in_specs=[HBM, HBM, HBM, HBM, VMEM],
        out_specs=(VMEM,) * 7,
        scratch_shapes=[
            pltpu.SMEM((node_slots,), jnp.int32),
            pltpu.VMEM(ancestors.shape, jnp.int32),
            pltpu.VMEM((prompt_cols, width), jnp.bfloat16),
            pltpu.VMEM((node_slots, tokens, width), jnp.bfloat16),
            pltpu.SemaphoreType.DMA((6,)),
        ],
        compiler_params=params(16),
        cost_estimate=pl.CostEstimate(flops=500_000_000, bytes_accessed=6_000_000, transcendentals=800_000),
    )(*in_hbm(node_lengths, ancestors, prompt_kv, node_kv), query_rows)

    parts = pl.pallas_call(
        late_kernel,
        out_shape=jax.ShapeDtypeStruct((HEADS, rows // 2, 2 * HEAD_DIM + LANES), jnp.int16),
        in_specs=[VMEM] * 8,
        out_specs=VMEM,
        compiler_params=params(16),
    )(query, shared, weights, early_max, early_total, count, prompt_values, node_values)

    parts = lax.all_to_all(parts, "seq", 0, 0, tiled=True)
    return pl.pallas_call(
        merge_kernel,
        out_shape=jax.ShapeDtypeStruct((leaf_count, steps, HEAD_DIM), jnp.bfloat16),
        in_specs=[VMEM],
        out_specs=VMEM,
        compiler_params=params(8),
    )(parts)


def solution(mesh):
    placed = (
        P("leaf", None, None),
        P(None, "seq", None),
        P(None, "leaf", "seq", None),
        P("leaf"),
        P("leaf", None),
    )
    return jax.shard_map(
        shards, mesh=mesh, in_specs=placed, out_specs=P("leaf", None, "seq"), check_vma=False
    )
```

```python
import functools

import jax
import jax.numpy as jnp
from jax import lax
from jax.experimental import pallas as pl
from jax.experimental.pallas import tpu as pltpu
from jax.sharding import PartitionSpec as P

HEADS = 16
KV_HEADS = 2
HEAD_DIM = 256
GROUP = HEADS // KV_HEADS
CHUNK = 256
LANES = 128
Z = 8
INVALID_KEY = 256.0
TOP = 32767.0
POINTS = (2.0**18, 2.0**26, 2.0**23)

VMEM = pl.BlockSpec(memory_space=pltpu.VMEM)
HBM = pl.BlockSpec(memory_space=pltpu.HBM)


def in_hbm(*arrays):
    return [pltpu.with_memory_space_constraint(array, pltpu.HBM) for array in arrays]


def params(mib):
    return pltpu.CompilerParams(vmem_limit_bytes=mib * 1024 * 1024)


def fold(x, combine):
    parts = [x[:, i : i + LANES] for i in range(0, x.shape[1], LANES)]
    return functools.reduce(combine, parts)


def tall(x, reps):
    return jnp.concatenate([x] * reps, axis=0)


def node_counts(anc, ids, levels):
    counts = jnp.zeros((anc.shape[0], ids.shape[1]), jnp.float32)
    for level in levels:
        counts = counts + jnp.where(anc[:, level : level + 1] == ids, 1.0, 0.0)
    return counts


def group_query(q_ref, k):
    heads = range(k * GROUP, (k + 1) * GROUP)
    query = jnp.concatenate([q_ref[:, h * HEAD_DIM : (h + 1) * HEAD_DIM] for h in heads], axis=0)
    return query * jnp.bfloat16(1.0 / 16.0)


def dot_nt(a, b):
    return lax.dot_general(a, b, (((1,), (1,)), ((), ())), preferred_element_type=jnp.float32)


def fetch(pairs, sems):
    copies = [pltpu.make_async_copy(src, dst, sems.at[i]) for i, (src, dst) in enumerate(pairs)]
    for copy in copies:
        copy.start()
    return copies


def post_kernel(lengths_hbm, node_hbm, out_ref, node_ref, lengths_ref, sems):
    node_slots = lengths_hbm.shape[0]
    tokens = node_ref.shape[1]
    for copy in fetch([(node_hbm.at[:, node_slots - 1], node_ref), (lengths_hbm, lengths_ref)], sems):
        copy.wait()
    present = lax.axis_index("seq") * tokens < lengths_ref[node_slots - 1]
    keys = jnp.where(present, node_ref[0], jnp.bfloat16(INVALID_KEY))
    values = node_ref[1]
    for copy in range(out_ref.shape[0]):
        out_ref[copy, 0:tokens] = keys
        out_ref[copy, tokens : 2 * tokens] = values


def copies_kernel(plane_ref, out_hbm, sems):
    for copy in fetch([(plane_ref, out_hbm.at[i]) for i in range(out_hbm.shape[0])], sems):
        copy.wait()


def early_kernel(
    steps,
    lengths_hbm,
    anc_hbm,
    prompt_hbm,
    node_hbm,
    q_ref,
    w_hbm,
    max_ref,
    total_ref,
    query_ref,
    count_ref,
    prompt_values_ref,
    node_values_ref,
    lengths_ref,
    anc_ref,
    prompt_ref,
    node_ref,
    w_ref,
    sems,
    w_sems,
):
    copies = fetch(
        [
            (lengths_hbm, lengths_ref),
            (anc_hbm, anc_ref),
            (node_hbm.at[0], node_ref),
            (prompt_hbm.at[0], prompt_ref),
            (node_hbm.at[1], node_values_ref),
            (prompt_hbm.at[1], prompt_values_ref),
        ],
        sems,
    )
    leaf_count, level_count = anc_ref.shape
    node_slots, tokens, width = node_ref.shape
    node_cols = node_slots * tokens
    prompt_cols = prompt_ref.shape[0]
    shared_cols = count_ref.shape[1]
    for k in range(KV_HEADS):
        query_ref[k] = group_query(q_ref, k)
    copies[0].wait()
    copies[1].wait()
    anc = anc_ref[...]

    lane = lax.broadcasted_iota(jnp.int32, (1, shared_cols), 1)
    owner = lane // tokens
    count = node_counts(anc, owner * node_slots + node_slots - 1, range(level_count - 1))
    count_ref[...] = jnp.where(owner == lax.axis_index("leaf"), 0.0, count)

    lane = lax.broadcasted_iota(jnp.int32, (1, node_cols), 1)
    slot = lane // tokens
    position = lax.axis_index("seq") * tokens + lane % tokens
    length = jnp.zeros((1, node_cols), jnp.int32)
    for n in range(node_slots):
        length = jnp.where(slot == n, lengths_ref[n], length)
    ids = lax.axis_index("leaf") * node_slots + slot
    upper = node_counts(anc, ids, range(level_count - 1))
    own = node_counts(anc, ids, [level_count - 1])
    mult = []
    for step in range(steps):
        causal = jnp.where(position <= length - steps + step, 1.0, 0.0)
        mult.append(jnp.where(position < length, upper + own * causal, 0.0))
    mult = tall(jnp.concatenate(mult, axis=0), GROUP)
    copies[2].wait()
    copies[3].wait()

    for k in range(KV_HEADS):
        cols = slice(k * HEAD_DIM, (k + 1) * HEAD_DIM)
        query = query_ref[k]
        top = None
        for start in range(0, prompt_cols, CHUNK):
            s = dot_nt(query, prompt_ref[start : start + CHUNK, cols])
            w_ref[k, start // CHUNK] = s
            part = fold(s, jnp.maximum)
            top = part if top is None else jnp.maximum(top, part)
        s = dot_nt(query, node_ref[:, :, cols].reshape(node_cols, HEAD_DIM))
        s = jnp.where(mult > 0.0, s, -jnp.inf)
        w_ref[k, prompt_cols // CHUNK] = s
        top = jnp.max(jnp.maximum(top, fold(s, jnp.maximum)), axis=1, keepdims=True)
        total = jnp.zeros((s.shape[0], LANES), jnp.float32)
        for start in range(0, prompt_cols, CHUNK):
            w = jnp.exp(w_ref[k, start // CHUNK] - top)
            w_ref[k, start // CHUNK] = w
            total = total + fold(w, jnp.add)
        w = jnp.exp(w_ref[k, prompt_cols // CHUNK] - top) * mult
        w_ref[k, prompt_cols // CHUNK] = w
        copies += fetch([(w_ref.at[k], w_hbm.at[k])], w_sems.at[pl.ds(k, 1)])
        total = total + fold(w, jnp.add)
        total_ref[k] = jnp.broadcast_to(jnp.sum(total, axis=1, keepdims=True), total.shape)
        max_ref[k] = jnp.broadcast_to(top, total.shape)
    for copy in copies[4:]:
        copy.wait()


def late_kernel(
    query_ref, shared_ref, w_hbm, max_ref, total_ref, count_ref, prompt_ref, node_ref, out_ref, w_ref, sems
):
    chunks = w_ref.shape[1]
    places = [(k, c) for k in range(KV_HEADS) for c in range(chunks)]
    copies = fetch([(w_hbm.at[k, c], w_ref.at[k, c]) for k, c in places], sems)
    owners = shared_ref.shape[0]
    tokens = shared_ref.shape[1] // 2
    prompt_cols = prompt_ref.shape[0]
    node_cols = node_ref.shape[0] * node_ref.shape[1]
    shared_cols = owners * tokens
    rows = query_ref.shape[1] // GROUP
    half = rows // 2
    count = count_ref[...]
    reps = GROUP * rows // count.shape[0]
    pick = jnp.where(lax.broadcasted_iota(jnp.int32, (8, HEAD_DIM), 1) == 0, 1.0, 0.0).astype(jnp.bfloat16)

    for k in range(KV_HEADS):
        cols = slice(k * HEAD_DIM, (k + 1) * HEAD_DIM)
        keys = shared_ref[:, 0:tokens, cols].reshape(shared_cols, HEAD_DIM)
        values = shared_ref[:, tokens : 2 * tokens, cols].reshape(shared_cols, HEAD_DIM)
        marks = dot_nt(pick, keys)[0:1]
        mult = tall(jnp.where(marks < INVALID_KEY / 2, count, 0.0), reps)
        s = dot_nt(query_ref[k], keys)
        s = jnp.where(mult > 0.0, s, -jnp.inf)
        early_max = max_ref[k]
        block_max = jnp.maximum(jnp.max(fold(s, jnp.maximum), axis=1, keepdims=True), early_max)
        scale = jnp.exp(early_max - block_max)
        w = jnp.exp(s - block_max[:, 0:1]) * mult
        total = jnp.sum(fold(w, jnp.add), axis=1, keepdims=True) + total_ref[k] * scale
        acc = jnp.dot(w.astype(jnp.bfloat16), values, preferred_element_type=jnp.float32)
        wide = jnp.concatenate([scale, scale], axis=1)
        for start in range(0, prompt_cols, CHUNK):
            copies[k * chunks + start // CHUNK].wait()
            w = (w_ref[k, start // CHUNK] * wide).astype(jnp.bfloat16)
            acc = acc + jnp.dot(w, prompt_ref[start : start + CHUNK, cols], preferred_element_type=jnp.float32)
        copies[k * chunks + chunks - 1].wait()
        w = (w_ref[k, chunks - 1] * wide).astype(jnp.bfloat16)
        node_values = node_ref[:, :, cols].reshape(node_cols, HEAD_DIM)
        acc = acc + jnp.dot(w, node_values, preferred_element_type=jnp.float32)

        reach = jnp.maximum(jnp.max(fold(jnp.abs(acc), jnp.maximum), axis=1, keepdims=True), 1e-30)
        data = jnp.round(acc * (TOP / reach)).astype(jnp.int32).astype(jnp.int16)
        fixed = [
            jnp.round(value * point).astype(jnp.int32)
            for value, point in zip((block_max, jnp.log(total), jnp.log(reach)), POINTS)
        ]
        lane = lax.broadcasted_iota(jnp.int32, (GROUP * rows, LANES), 1)
        stats = jnp.zeros((GROUP * rows, LANES), jnp.int32)
        for i, value in enumerate(fixed):
            stats = jnp.where(lane == 2 * i, value >> 16, stats)
            stats = jnp.where(lane == 2 * i + 1, (value & 0xFFFF) - 0x8000, stats)
        lane = lane[:half]
        for h in range(GROUP):
            first = h * rows
            for part in range(2):
                lanes = slice(part * HEAD_DIM, (part + 1) * HEAD_DIM)
                out_ref[k * GROUP + h, :, lanes] = data[first + part * half : first + (part + 1) * half]
            low, high = stats[first : first + half], stats[first + half : first + rows]
            both = jnp.where(lane < LANES // 2, low, pltpu.roll(high, LANES // 2, 1))
            out_ref[k * GROUP + h, :, 2 * HEAD_DIM :] = both.astype(jnp.int16)


def merge_kernel(parts_ref, out_ref):
    blocks, half, _ = parts_ref.shape
    leaf_count = out_ref.shape[0]
    stats = [parts_ref[b, :, 2 * HEAD_DIM :].astype(jnp.int32) for b in range(blocks)]
    for part in range(2):
        first = part * LANES // 2

        def value(b, i):
            high = stats[b][:, first + 2 * i : first + 2 * i + 1]
            low = stats[b][:, first + 2 * i + 1 : first + 2 * i + 2] + 0x8000
            return ((high << 16) + low).astype(jnp.float32) * (1.0 / POINTS[i])

        tops = [value(b, 0) for b in range(blocks)]
        row_max = functools.reduce(jnp.maximum, tops)
        denominator = jnp.zeros((half, 1), jnp.float32)
        numerator = jnp.zeros((half, HEAD_DIM), jnp.float32)
        for b in range(blocks):
            shift = tops[b] - row_max
            denominator = denominator + jnp.exp(shift + value(b, 1))
            data = parts_ref[b, :, part * HEAD_DIM : (part + 1) * HEAD_DIM].astype(jnp.int32).astype(jnp.float32)
            numerator = numerator + jnp.exp(shift + value(b, 2)) * data
        merged = (numerator / (denominator * TOP)).astype(jnp.bfloat16)
        for i in range(half // leaf_count):
            out_ref[:, part * half // leaf_count + i, :] = merged[i * leaf_count : (i + 1) * leaf_count]


def gather_shared(own, owners):
    along_z = [list(range(x, x + Z)) for x in range(0, owners, Z)]
    along_x = [list(range(z, owners, Z)) for z in range(Z)]
    plane = lax.all_to_all(own, "leaf", 0, 0, tiled=True, axis_index_groups=along_z)
    plane = pl.pallas_call(
        copies_kernel,
        out_shape=pltpu.HBM((owners // Z,) + plane.shape, plane.dtype),
        in_specs=[VMEM],
        out_specs=HBM,
        scratch_shapes=[pltpu.SemaphoreType.DMA((owners // Z,))],
        compiler_params=params(8),
    )(plane)
    shared = lax.all_to_all(plane, "leaf", 0, 0, tiled=True, axis_index_groups=along_x)
    return shared.reshape((owners,) + own.shape[1:])


def shards(queries, prompt_kv, node_kv, node_lengths, ancestors):
    leaf_count, steps, feat_width = queries.shape
    node_slots, tokens = node_kv.shape[1:3]
    prompt_cols = prompt_kv.shape[1]
    width = KV_HEADS * HEAD_DIM
    rows = steps * leaf_count
    owners = lax.axis_size("leaf")

    own = pl.pallas_call(
        post_kernel,
        out_shape=jax.ShapeDtypeStruct((Z, 2 * tokens, width), jnp.bfloat16),
        in_specs=[HBM, HBM],
        out_specs=VMEM,
        scratch_shapes=[
            pltpu.VMEM((2, tokens, width), jnp.bfloat16),
            pltpu.SMEM((node_slots,), jnp.int32),
            pltpu.SemaphoreType.DMA((2,)),
        ],
        compiler_params=params(8),
    )(*in_hbm(node_lengths, node_kv))
    shared = gather_shared(own, owners)

    query_rows = queries.transpose(1, 0, 2).reshape(rows, feat_width)
    assert prompt_cols % CHUNK == 0 and node_slots * tokens == CHUNK
    weights_shape = (KV_HEADS, prompt_cols // CHUNK + 1, GROUP * rows, CHUNK)
    row_shape = jax.ShapeDtypeStruct((KV_HEADS, GROUP * rows, LANES), jnp.float32)
    weights, early_max, early_total, query, count, prompt_values, node_values = pl.pallas_call(
        functools.partial(early_kernel, steps),
        out_shape=(
            pltpu.HBM(weights_shape, jnp.float32),
            row_shape,
            row_shape,
            jax.ShapeDtypeStruct((KV_HEADS, GROUP * rows, HEAD_DIM), jnp.bfloat16),
            jax.ShapeDtypeStruct((leaf_count, owners * tokens), jnp.float32),
            jax.ShapeDtypeStruct((prompt_cols, width), jnp.bfloat16),
            jax.ShapeDtypeStruct((node_slots, tokens, width), jnp.bfloat16),
        ),
        in_specs=[HBM, HBM, HBM, HBM, VMEM],
        out_specs=(HBM,) + (VMEM,) * 6,
        scratch_shapes=[
            pltpu.SMEM((node_slots,), jnp.int32),
            pltpu.VMEM(ancestors.shape, jnp.int32),
            pltpu.VMEM((prompt_cols, width), jnp.bfloat16),
            pltpu.VMEM((node_slots, tokens, width), jnp.bfloat16),
            pltpu.VMEM(weights_shape, jnp.float32),
            pltpu.SemaphoreType.DMA((6,)),
            pltpu.SemaphoreType.DMA((KV_HEADS,)),
        ],
        compiler_params=params(16),
        cost_estimate=pl.CostEstimate(flops=500_000_000, bytes_accessed=6_000_000, transcendentals=800_000),
    )(*in_hbm(node_lengths, ancestors, prompt_kv, node_kv), query_rows)

    parts = pl.pallas_call(
        late_kernel,
        out_shape=jax.ShapeDtypeStruct((HEADS, rows // 2, 2 * HEAD_DIM + LANES), jnp.int16),
        in_specs=[VMEM, VMEM, HBM] + [VMEM] * 5,
        out_specs=VMEM,
        scratch_shapes=[
            pltpu.VMEM(weights_shape, jnp.float32),
            pltpu.SemaphoreType.DMA((weights_shape[0] * weights_shape[1],)),
        ],
        compiler_params=params(16),
    )(query, shared, *in_hbm(weights), early_max, early_total, count, prompt_values, node_values)

    parts = lax.all_to_all(parts, "seq", 0, 0, tiled=True)
    return pl.pallas_call(
        merge_kernel,
        out_shape=jax.ShapeDtypeStruct((leaf_count, steps, HEAD_DIM), jnp.bfloat16),
        in_specs=[VMEM],
        out_specs=VMEM,
        compiler_params=params(8),
    )(parts)


def solution(mesh):
    placed = (
        P("leaf", None, None),
        P(None, "seq", None),
        P(None, "leaf", "seq", None),
        P("leaf"),
        P("leaf", None),
    )
    return jax.shard_map(
        shards, mesh=mesh, in_specs=placed, out_specs=P("leaf", None, "seq"), check_vma=False
    )
```

```python
import functools

import jax
import jax.numpy as jnp
from jax import lax
from jax.experimental import pallas as pl
from jax.experimental.pallas import tpu as pltpu
from jax.sharding import PartitionSpec as P

HEADS = 16
KV_HEADS = 2
HEAD_DIM = 256
GROUP = HEADS // KV_HEADS
CHUNK = 256
LANES = 128
Z = 8
INVALID_KEY = 256.0
TOP = 32767.0
POINTS = (2.0**18, 2.0**26, 2.0**23)

VMEM = pl.BlockSpec(memory_space=pltpu.VMEM)
HBM = pl.BlockSpec(memory_space=pltpu.HBM)


def in_hbm(*arrays):
    return [pltpu.with_memory_space_constraint(array, pltpu.HBM) for array in arrays]


def params(mib):
    return pltpu.CompilerParams(vmem_limit_bytes=mib * 1024 * 1024)


def fold(x, combine):
    parts = [x[:, i : i + LANES] for i in range(0, x.shape[1], LANES)]
    return functools.reduce(combine, parts)


def tall(x, reps):
    return jnp.concatenate([x] * reps, axis=0)


def node_counts(anc, ids, levels):
    counts = jnp.zeros((anc.shape[0], ids.shape[1]), jnp.float32)
    for level in levels:
        counts = counts + jnp.where(anc[:, level : level + 1] == ids, 1.0, 0.0)
    return counts


def group_query(q_ref, k):
    heads = range(k * GROUP, (k + 1) * GROUP)
    query = jnp.concatenate([q_ref[:, h * HEAD_DIM : (h + 1) * HEAD_DIM] for h in heads], axis=0)
    return query * jnp.bfloat16(1.0 / 16.0)


def dot_nt(a, b):
    return lax.dot_general(a, b, (((1,), (1,)), ((), ())), preferred_element_type=jnp.float32)


def fetch(pairs, sems):
    copies = [pltpu.make_async_copy(src, dst, sems.at[i]) for i, (src, dst) in enumerate(pairs)]
    for copy in copies:
        copy.start()
    return copies


def post_kernel(lengths_hbm, node_hbm, out_ref, node_ref, lengths_ref, sems):
    node_slots = lengths_hbm.shape[0]
    tokens = node_ref.shape[1]
    for copy in fetch([(node_hbm.at[:, node_slots - 1], node_ref), (lengths_hbm, lengths_ref)], sems):
        copy.wait()
    present = lax.axis_index("seq") * tokens < lengths_ref[node_slots - 1]
    keys = jnp.where(present, node_ref[0], jnp.bfloat16(INVALID_KEY))
    values = node_ref[1]
    for copy in range(out_ref.shape[0]):
        out_ref[copy, 0:tokens] = keys
        out_ref[copy, tokens : 2 * tokens] = values


def copies_kernel(plane_ref, early_ref, out_ref):
    del early_ref
    for copy in range(out_ref.shape[0]):
        out_ref[copy] = plane_ref[...]


def early_kernel(
    steps,
    lengths_hbm,
    anc_hbm,
    prompt_hbm,
    node_hbm,
    q_ref,
    w_ref,
    max_ref,
    total_ref,
    query_ref,
    count_ref,
    prompt_values_ref,
    node_values_ref,
    lengths_ref,
    anc_ref,
    prompt_ref,
    node_ref,
    sems,
):
    copies = fetch(
        [
            (lengths_hbm, lengths_ref),
            (anc_hbm, anc_ref),
            (node_hbm.at[0], node_ref),
            (prompt_hbm.at[0], prompt_ref),
            (node_hbm.at[1], node_values_ref),
            (prompt_hbm.at[1], prompt_values_ref),
        ],
        sems,
    )
    leaf_count, level_count = anc_ref.shape
    node_slots, tokens, width = node_ref.shape
    node_cols = node_slots * tokens
    prompt_cols = prompt_ref.shape[0]
    shared_cols = count_ref.shape[1]
    for k in range(KV_HEADS):
        query_ref[k] = group_query(q_ref, k)
    copies[0].wait()
    copies[1].wait()
    anc = anc_ref[...]

    lane = lax.broadcasted_iota(jnp.int32, (1, shared_cols), 1)
    owner = lane // tokens
    count = node_counts(anc, owner * node_slots + node_slots - 1, range(level_count - 1))
    count_ref[...] = jnp.where(owner == lax.axis_index("leaf"), 0.0, count)

    lane = lax.broadcasted_iota(jnp.int32, (1, node_cols), 1)
    slot = lane // tokens
    position = lax.axis_index("seq") * tokens + lane % tokens
    length = jnp.zeros((1, node_cols), jnp.int32)
    for n in range(node_slots):
        length = jnp.where(slot == n, lengths_ref[n], length)
    ids = lax.axis_index("leaf") * node_slots + slot
    upper = node_counts(anc, ids, range(level_count - 1))
    own = node_counts(anc, ids, [level_count - 1])
    mult = []
    for step in range(steps):
        causal = jnp.where(position <= length - steps + step, 1.0, 0.0)
        mult.append(jnp.where(position < length, upper + own * causal, 0.0))
    mult = tall(jnp.concatenate(mult, axis=0), GROUP)
    copies[2].wait()
    copies[3].wait()

    for k in range(KV_HEADS):
        cols = slice(k * HEAD_DIM, (k + 1) * HEAD_DIM)
        query = query_ref[k]
        top = None
        for start in range(0, prompt_cols, CHUNK):
            s = dot_nt(query, prompt_ref[start : start + CHUNK, cols])
            w_ref[k, :, start : start + CHUNK] = s
            part = fold(s, jnp.maximum)
            top = part if top is None else jnp.maximum(top, part)
        s = dot_nt(query, node_ref[:, :, cols].reshape(node_cols, HEAD_DIM))
        s = jnp.where(mult > 0.0, s, -jnp.inf)
        w_ref[k, :, prompt_cols:] = s
        top = jnp.max(jnp.maximum(top, fold(s, jnp.maximum)), axis=1, keepdims=True)
        total = jnp.zeros((s.shape[0], LANES), jnp.float32)
        for start in range(0, prompt_cols, CHUNK):
            w = jnp.exp(w_ref[k, :, start : start + CHUNK] - top)
            w_ref[k, :, start : start + CHUNK] = w
            total = total + fold(w, jnp.add)
        w = jnp.exp(w_ref[k, :, prompt_cols:] - top) * mult
        w_ref[k, :, prompt_cols:] = w
        total = total + fold(w, jnp.add)
        total_ref[k] = jnp.broadcast_to(jnp.sum(total, axis=1, keepdims=True), total.shape)
        max_ref[k] = jnp.broadcast_to(top, total.shape)
    copies[4].wait()
    copies[5].wait()


def late_kernel(query_ref, shared_ref, w_ref, max_ref, total_ref, count_ref, prompt_ref, node_ref, out_ref):
    owners = shared_ref.shape[0]
    tokens = shared_ref.shape[1] // 2
    prompt_cols = prompt_ref.shape[0]
    node_cols = node_ref.shape[0] * node_ref.shape[1]
    shared_cols = owners * tokens
    rows = query_ref.shape[1] // GROUP
    half = rows // 2
    count = count_ref[...]
    reps = GROUP * rows // count.shape[0]
    pick = jnp.where(lax.broadcasted_iota(jnp.int32, (8, HEAD_DIM), 1) == 0, 1.0, 0.0).astype(jnp.bfloat16)

    for k in range(KV_HEADS):
        cols = slice(k * HEAD_DIM, (k + 1) * HEAD_DIM)
        keys = shared_ref[:, 0:tokens, cols].reshape(shared_cols, HEAD_DIM)
        values = shared_ref[:, tokens : 2 * tokens, cols].reshape(shared_cols, HEAD_DIM)
        marks = dot_nt(pick, keys)[0:1]
        mult = tall(jnp.where(marks < INVALID_KEY / 2, count, 0.0), reps)
        s = dot_nt(query_ref[k], keys)
        s = jnp.where(mult > 0.0, s, -jnp.inf)
        early_max = max_ref[k]
        block_max = jnp.maximum(jnp.max(fold(s, jnp.maximum), axis=1, keepdims=True), early_max)
        scale = jnp.exp(early_max - block_max)
        w = jnp.exp(s - block_max[:, 0:1]) * mult
        total = jnp.sum(fold(w, jnp.add), axis=1, keepdims=True) + total_ref[k] * scale
        acc = jnp.dot(w.astype(jnp.bfloat16), values, preferred_element_type=jnp.float32)
        wide = jnp.concatenate([scale, scale], axis=1)
        for start in range(0, prompt_cols, CHUNK):
            w = (w_ref[k, :, start : start + CHUNK] * wide).astype(jnp.bfloat16)
            acc = acc + jnp.dot(w, prompt_ref[start : start + CHUNK, cols], preferred_element_type=jnp.float32)
        w = (w_ref[k, :, prompt_cols:] * wide).astype(jnp.bfloat16)
        node_values = node_ref[:, :, cols].reshape(node_cols, HEAD_DIM)
        acc = acc + jnp.dot(w, node_values, preferred_element_type=jnp.float32)

        reach = jnp.maximum(jnp.max(fold(jnp.abs(acc), jnp.maximum), axis=1, keepdims=True), 1e-30)
        data = jnp.round(acc * (TOP / reach)).astype(jnp.int32).astype(jnp.int16)
        fixed = [
            jnp.round(value * point).astype(jnp.int32)
            for value, point in zip((block_max, jnp.log(total), jnp.log(reach)), POINTS)
        ]
        lane = lax.broadcasted_iota(jnp.int32, (GROUP * rows, LANES), 1)
        stats = jnp.zeros((GROUP * rows, LANES), jnp.int32)
        for i, value in enumerate(fixed):
            stats = jnp.where(lane == 2 * i, value >> 16, stats)
            stats = jnp.where(lane == 2 * i + 1, (value & 0xFFFF) - 0x8000, stats)
        lane = lane[:half]
        for h in range(GROUP):
            first = h * rows
            for part in range(2):
                lanes = slice(part * HEAD_DIM, (part + 1) * HEAD_DIM)
                out_ref[k * GROUP + h, :, lanes] = data[first + part * half : first + (part + 1) * half]
            low, high = stats[first : first + half], stats[first + half : first + rows]
            both = jnp.where(lane < LANES // 2, low, pltpu.roll(high, LANES // 2, 1))
            out_ref[k * GROUP + h, :, 2 * HEAD_DIM :] = both.astype(jnp.int16)


def merge_kernel(parts_ref, out_ref):
    blocks, half, _ = parts_ref.shape
    leaf_count = out_ref.shape[0]
    stats = [parts_ref[b, :, 2 * HEAD_DIM :].astype(jnp.int32) for b in range(blocks)]
    for part in range(2):
        first = part * LANES // 2

        def value(b, i):
            high = stats[b][:, first + 2 * i : first + 2 * i + 1]
            low = stats[b][:, first + 2 * i + 1 : first + 2 * i + 2] + 0x8000
            return ((high << 16) + low).astype(jnp.float32) * (1.0 / POINTS[i])

        tops = [value(b, 0) for b in range(blocks)]
        row_max = functools.reduce(jnp.maximum, tops)
        denominator = jnp.zeros((half, 1), jnp.float32)
        numerator = jnp.zeros((half, HEAD_DIM), jnp.float32)
        for b in range(blocks):
            shift = tops[b] - row_max
            denominator = denominator + jnp.exp(shift + value(b, 1))
            data = parts_ref[b, :, part * HEAD_DIM : (part + 1) * HEAD_DIM].astype(jnp.int32).astype(jnp.float32)
            numerator = numerator + jnp.exp(shift + value(b, 2)) * data
        merged = (numerator / (denominator * TOP)).astype(jnp.bfloat16)
        for i in range(half // leaf_count):
            out_ref[:, part * half // leaf_count + i, :] = merged[i * leaf_count : (i + 1) * leaf_count]


def gather_shared(own, owners, early):
    along_z = [list(range(x, x + Z)) for x in range(0, owners, Z)]
    along_x = [list(range(z, owners, Z)) for z in range(Z)]
    plane = lax.all_to_all(own, "leaf", 0, 0, tiled=True, axis_index_groups=along_z)
    plane = pl.pallas_call(
        copies_kernel,
        out_shape=jax.ShapeDtypeStruct((owners // Z,) + plane.shape, plane.dtype),
        in_specs=[VMEM, VMEM],
        out_specs=VMEM,
        compiler_params=params(8),
    )(plane, early)
    shared = lax.all_to_all(plane, "leaf", 0, 0, tiled=True, axis_index_groups=along_x)
    return shared.reshape((owners,) + own.shape[1:])


def shards(queries, prompt_kv, node_kv, node_lengths, ancestors):
    leaf_count, steps, feat_width = queries.shape
    node_slots, tokens = node_kv.shape[1:3]
    prompt_cols = prompt_kv.shape[1]
    width = KV_HEADS * HEAD_DIM
    rows = steps * leaf_count
    owners = lax.axis_size("leaf")

    own = pl.pallas_call(
        post_kernel,
        out_shape=jax.ShapeDtypeStruct((Z, 2 * tokens, width), jnp.bfloat16),
        in_specs=[HBM, HBM],
        out_specs=VMEM,
        scratch_shapes=[
            pltpu.VMEM((2, tokens, width), jnp.bfloat16),
            pltpu.SMEM((node_slots,), jnp.int32),
            pltpu.SemaphoreType.DMA((2,)),
        ],
        compiler_params=params(8),
    )(*in_hbm(node_lengths, node_kv))
    query_rows = queries.transpose(1, 0, 2).reshape(rows, feat_width)
    cols = prompt_cols + node_slots * tokens
    row_shape = jax.ShapeDtypeStruct((KV_HEADS, GROUP * rows, LANES), jnp.float32)
    weights, early_max, early_total, query, count, prompt_values, node_values = pl.pallas_call(
        functools.partial(early_kernel, steps),
        out_shape=(
            jax.ShapeDtypeStruct((KV_HEADS, GROUP * rows, cols), jnp.float32),
            row_shape,
            row_shape,
            jax.ShapeDtypeStruct((KV_HEADS, GROUP * rows, HEAD_DIM), jnp.bfloat16),
            jax.ShapeDtypeStruct((leaf_count, owners * tokens), jnp.float32),
            jax.ShapeDtypeStruct((prompt_cols, width), jnp.bfloat16),
            jax.ShapeDtypeStruct((node_slots, tokens, width), jnp.bfloat16),
        ),
        in_specs=[HBM, HBM, HBM, HBM, VMEM],
        out_specs=(VMEM,) * 7,
        scratch_shapes=[
            pltpu.SMEM((node_slots,), jnp.int32),
            pltpu.VMEM(ancestors.shape, jnp.int32),
            pltpu.VMEM((prompt_cols, width), jnp.bfloat16),
            pltpu.VMEM((node_slots, tokens, width), jnp.bfloat16),
            pltpu.SemaphoreType.DMA((6,)),
        ],
        compiler_params=params(16),
        cost_estimate=pl.CostEstimate(flops=500_000_000, bytes_accessed=6_000_000, transcendentals=800_000),
    )(*in_hbm(node_lengths, ancestors, prompt_kv, node_kv), query_rows)

    shared = gather_shared(own, owners, count)
    parts = pl.pallas_call(
        late_kernel,
        out_shape=jax.ShapeDtypeStruct((HEADS, rows // 2, 2 * HEAD_DIM + LANES), jnp.int16),
        in_specs=[VMEM] * 8,
        out_specs=VMEM,
        compiler_params=params(16),
    )(query, shared, weights, early_max, early_total, count, prompt_values, node_values)

    parts = lax.all_to_all(parts, "seq", 0, 0, tiled=True)
    return pl.pallas_call(
        merge_kernel,
        out_shape=jax.ShapeDtypeStruct((leaf_count, steps, HEAD_DIM), jnp.bfloat16),
        in_specs=[VMEM],
        out_specs=VMEM,
        compiler_params=params(8),
    )(parts)


def solution(mesh):
    placed = (
        P("leaf", None, None),
        P(None, "seq", None),
        P(None, "leaf", "seq", None),
        P("leaf"),
        P("leaf", None),
    )
    return jax.shard_map(
        shards, mesh=mesh, in_specs=placed, out_specs=P("leaf", None, "seq"), check_vma=False
    )
```

```python
import functools

import jax
import jax.numpy as jnp
from jax import lax
from jax.experimental import pallas as pl
from jax.experimental.pallas import tpu as pltpu
from jax.sharding import PartitionSpec as P

HEADS = 16
KV_HEADS = 2
HEAD_DIM = 256
GROUP = HEADS // KV_HEADS
CHUNK = 256
LANES = 128
Z = 8
INVALID_KEY = 256.0
TOP = 32767.0
POINTS = (2.0**18, 2.0**26, 2.0**23)

VMEM = pl.BlockSpec(memory_space=pltpu.VMEM)
HBM = pl.BlockSpec(memory_space=pltpu.HBM)


def in_hbm(*arrays):
    return [pltpu.with_memory_space_constraint(array, pltpu.HBM) for array in arrays]


def params(mib):
    return pltpu.CompilerParams(vmem_limit_bytes=mib * 1024 * 1024)


def fold(x, combine):
    parts = [x[:, i : i + LANES] for i in range(0, x.shape[1], LANES)]
    return functools.reduce(combine, parts)


def tall(x, reps):
    return jnp.concatenate([x] * reps, axis=0)


def node_counts(anc, ids, levels):
    counts = jnp.zeros((anc.shape[0], ids.shape[1]), jnp.float32)
    for level in levels:
        counts = counts + jnp.where(anc[:, level : level + 1] == ids, 1.0, 0.0)
    return counts


def group_query(q_ref, k):
    heads = range(k * GROUP, (k + 1) * GROUP)
    query = jnp.concatenate([q_ref[:, h * HEAD_DIM : (h + 1) * HEAD_DIM] for h in heads], axis=0)
    return query * jnp.bfloat16(1.0 / 16.0)


def dot_nt(a, b):
    return lax.dot_general(a, b, (((1,), (1,)), ((), ())), preferred_element_type=jnp.float32)


def fetch(pairs, sems):
    copies = [pltpu.make_async_copy(src, dst, sems.at[i]) for i, (src, dst) in enumerate(pairs)]
    for copy in copies:
        copy.start()
    return copies


def post_kernel(lengths_hbm, node_hbm, out_ref, node_ref, lengths_ref, sems):
    node_slots = lengths_hbm.shape[0]
    tokens = node_ref.shape[1]
    for copy in fetch([(node_hbm.at[:, node_slots - 1], node_ref), (lengths_hbm, lengths_ref)], sems):
        copy.wait()
    present = lax.axis_index("seq") * tokens < lengths_ref[node_slots - 1]
    keys = jnp.where(present, node_ref[0], jnp.bfloat16(INVALID_KEY))
    values = node_ref[1]
    for copy in range(out_ref.shape[0]):
        out_ref[copy, 0:tokens] = keys
        out_ref[copy, tokens : 2 * tokens] = values


def copies_kernel(plane_ref, early_ref, out_ref):
    del early_ref
    for copy in range(out_ref.shape[0]):
        out_ref[copy] = plane_ref[...]


def early_kernel(
    steps,
    lengths_hbm,
    anc_hbm,
    prompt_hbm,
    node_hbm,
    q_ref,
    w_hbm,
    max_ref,
    total_ref,
    query_ref,
    count_ref,
    prompt_values_ref,
    node_values_ref,
    lengths_ref,
    anc_ref,
    prompt_ref,
    node_ref,
    w_ref,
    sems,
    w_sems,
):
    copies = fetch(
        [
            (lengths_hbm, lengths_ref),
            (anc_hbm, anc_ref),
            (node_hbm.at[0], node_ref),
            (prompt_hbm.at[0], prompt_ref),
            (node_hbm.at[1], node_values_ref),
            (prompt_hbm.at[1], prompt_values_ref),
        ],
        sems,
    )
    leaf_count, level_count = anc_ref.shape
    node_slots, tokens, width = node_ref.shape
    node_cols = node_slots * tokens
    prompt_cols = prompt_ref.shape[0]
    shared_cols = count_ref.shape[1]
    for k in range(KV_HEADS):
        query_ref[k] = group_query(q_ref, k)
    copies[0].wait()
    copies[1].wait()
    anc = anc_ref[...]

    lane = lax.broadcasted_iota(jnp.int32, (1, shared_cols), 1)
    owner = lane // tokens
    count = node_counts(anc, owner * node_slots + node_slots - 1, range(level_count - 1))
    count_ref[...] = jnp.where(owner == lax.axis_index("leaf"), 0.0, count)

    lane = lax.broadcasted_iota(jnp.int32, (1, node_cols), 1)
    slot = lane // tokens
    position = lax.axis_index("seq") * tokens + lane % tokens
    length = jnp.zeros((1, node_cols), jnp.int32)
    for n in range(node_slots):
        length = jnp.where(slot == n, lengths_ref[n], length)
    ids = lax.axis_index("leaf") * node_slots + slot
    upper = node_counts(anc, ids, range(level_count - 1))
    own = node_counts(anc, ids, [level_count - 1])
    mult = []
    for step in range(steps):
        causal = jnp.where(position <= length - steps + step, 1.0, 0.0)
        mult.append(jnp.where(position < length, upper + own * causal, 0.0))
    mult = tall(jnp.concatenate(mult, axis=0), GROUP)
    copies[2].wait()
    copies[3].wait()

    for k in range(KV_HEADS):
        cols = slice(k * HEAD_DIM, (k + 1) * HEAD_DIM)
        query = query_ref[k]
        top = None
        for start in range(0, prompt_cols, CHUNK):
            s = dot_nt(query, prompt_ref[start : start + CHUNK, cols])
            w_ref[k, start // CHUNK] = s
            part = fold(s, jnp.maximum)
            top = part if top is None else jnp.maximum(top, part)
        s = dot_nt(query, node_ref[:, :, cols].reshape(node_cols, HEAD_DIM))
        s = jnp.where(mult > 0.0, s, -jnp.inf)
        w_ref[k, prompt_cols // CHUNK] = s
        top = jnp.max(jnp.maximum(top, fold(s, jnp.maximum)), axis=1, keepdims=True)
        total = jnp.zeros((s.shape[0], LANES), jnp.float32)
        for start in range(0, prompt_cols, CHUNK):
            c = start // CHUNK
            w = jnp.exp(w_ref[k, c] - top)
            w_ref[k, c] = w
            copies += fetch([(w_ref.at[k, c], w_hbm.at[k, c])], w_sems.at[k, pl.ds(c, 1)])
            total = total + fold(w, jnp.add)
        c = prompt_cols // CHUNK
        w = jnp.exp(w_ref[k, c] - top) * mult
        w_ref[k, c] = w
        copies += fetch([(w_ref.at[k, c], w_hbm.at[k, c])], w_sems.at[k, pl.ds(c, 1)])
        total = total + fold(w, jnp.add)
        total_ref[k] = jnp.broadcast_to(jnp.sum(total, axis=1, keepdims=True), total.shape)
        max_ref[k] = jnp.broadcast_to(top, total.shape)
    for copy in copies[4:]:
        copy.wait()


def late_kernel(query_ref, shared_ref, w_ref, max_ref, total_ref, count_ref, prompt_ref, node_ref, out_ref):
    owners = shared_ref.shape[0]
    tokens = shared_ref.shape[1] // 2
    prompt_cols = prompt_ref.shape[0]
    node_cols = node_ref.shape[0] * node_ref.shape[1]
    shared_cols = owners * tokens
    rows = query_ref.shape[1] // GROUP
    half = rows // 2
    count = count_ref[...]
    reps = GROUP * rows // count.shape[0]
    pick = jnp.where(lax.broadcasted_iota(jnp.int32, (8, HEAD_DIM), 1) == 0, 1.0, 0.0).astype(jnp.bfloat16)

    for k in range(KV_HEADS):
        cols = slice(k * HEAD_DIM, (k + 1) * HEAD_DIM)
        keys = shared_ref[:, 0:tokens, cols].reshape(shared_cols, HEAD_DIM)
        values = shared_ref[:, tokens : 2 * tokens, cols].reshape(shared_cols, HEAD_DIM)
        marks = dot_nt(pick, keys)[0:1]
        mult = tall(jnp.where(marks < INVALID_KEY / 2, count, 0.0), reps)
        s = dot_nt(query_ref[k], keys)
        s = jnp.where(mult > 0.0, s, -jnp.inf)
        early_max = max_ref[k]
        block_max = jnp.maximum(jnp.max(fold(s, jnp.maximum), axis=1, keepdims=True), early_max)
        scale = jnp.exp(early_max - block_max)
        w = jnp.exp(s - block_max[:, 0:1]) * mult
        total = jnp.sum(fold(w, jnp.add), axis=1, keepdims=True) + total_ref[k] * scale
        acc = jnp.dot(w.astype(jnp.bfloat16), values, preferred_element_type=jnp.float32)
        wide = jnp.concatenate([scale, scale], axis=1)
        for start in range(0, prompt_cols, CHUNK):
            w = (w_ref[k, start // CHUNK] * wide).astype(jnp.bfloat16)
            acc = acc + jnp.dot(w, prompt_ref[start : start + CHUNK, cols], preferred_element_type=jnp.float32)
        w = (w_ref[k, prompt_cols // CHUNK] * wide).astype(jnp.bfloat16)
        node_values = node_ref[:, :, cols].reshape(node_cols, HEAD_DIM)
        acc = acc + jnp.dot(w, node_values, preferred_element_type=jnp.float32)

        reach = jnp.maximum(jnp.max(fold(jnp.abs(acc), jnp.maximum), axis=1, keepdims=True), 1e-30)
        data = jnp.round(acc * (TOP / reach)).astype(jnp.int32).astype(jnp.int16)
        fixed = [
            jnp.round(value * point).astype(jnp.int32)
            for value, point in zip((block_max, jnp.log(total), jnp.log(reach)), POINTS)
        ]
        lane = lax.broadcasted_iota(jnp.int32, (GROUP * rows, LANES), 1)
        stats = jnp.zeros((GROUP * rows, LANES), jnp.int32)
        for i, value in enumerate(fixed):
            stats = jnp.where(lane == 2 * i, value >> 16, stats)
            stats = jnp.where(lane == 2 * i + 1, (value & 0xFFFF) - 0x8000, stats)
        lane = lane[:half]
        for h in range(GROUP):
            first = h * rows
            for part in range(2):
                lanes = slice(part * HEAD_DIM, (part + 1) * HEAD_DIM)
                out_ref[k * GROUP + h, :, lanes] = data[first + part * half : first + (part + 1) * half]
            low, high = stats[first : first + half], stats[first + half : first + rows]
            both = jnp.where(lane < LANES // 2, low, pltpu.roll(high, LANES // 2, 1))
            out_ref[k * GROUP + h, :, 2 * HEAD_DIM :] = both.astype(jnp.int16)


def merge_kernel(parts_ref, out_ref):
    blocks, half, _ = parts_ref.shape
    leaf_count = out_ref.shape[0]
    stats = [parts_ref[b, :, 2 * HEAD_DIM :].astype(jnp.int32) for b in range(blocks)]
    for part in range(2):
        first = part * LANES // 2

        def value(b, i):
            high = stats[b][:, first + 2 * i : first + 2 * i + 1]
            low = stats[b][:, first + 2 * i + 1 : first + 2 * i + 2] + 0x8000
            return ((high << 16) + low).astype(jnp.float32) * (1.0 / POINTS[i])

        tops = [value(b, 0) for b in range(blocks)]
        row_max = functools.reduce(jnp.maximum, tops)
        denominator = jnp.zeros((half, 1), jnp.float32)
        numerator = jnp.zeros((half, HEAD_DIM), jnp.float32)
        for b in range(blocks):
            shift = tops[b] - row_max
            denominator = denominator + jnp.exp(shift + value(b, 1))
            data = parts_ref[b, :, part * HEAD_DIM : (part + 1) * HEAD_DIM].astype(jnp.int32).astype(jnp.float32)
            numerator = numerator + jnp.exp(shift + value(b, 2)) * data
        merged = (numerator / (denominator * TOP)).astype(jnp.bfloat16)
        for i in range(half // leaf_count):
            out_ref[:, part * half // leaf_count + i, :] = merged[i * leaf_count : (i + 1) * leaf_count]


def gather_shared(own, owners, early):
    along_z = [list(range(x, x + Z)) for x in range(0, owners, Z)]
    along_x = [list(range(z, owners, Z)) for z in range(Z)]
    plane = lax.all_to_all(own, "leaf", 0, 0, tiled=True, axis_index_groups=along_z)
    plane = pl.pallas_call(
        copies_kernel,
        out_shape=jax.ShapeDtypeStruct((owners // Z,) + plane.shape, plane.dtype),
        in_specs=[VMEM, VMEM],
        out_specs=VMEM,
        compiler_params=params(8),
    )(plane, early)
    shared = lax.all_to_all(plane, "leaf", 0, 0, tiled=True, axis_index_groups=along_x)
    return shared.reshape((owners,) + own.shape[1:])


def shards(queries, prompt_kv, node_kv, node_lengths, ancestors):
    leaf_count, steps, feat_width = queries.shape
    node_slots, tokens = node_kv.shape[1:3]
    prompt_cols = prompt_kv.shape[1]
    width = KV_HEADS * HEAD_DIM
    rows = steps * leaf_count
    owners = lax.axis_size("leaf")

    own = pl.pallas_call(
        post_kernel,
        out_shape=jax.ShapeDtypeStruct((Z, 2 * tokens, width), jnp.bfloat16),
        in_specs=[HBM, HBM],
        out_specs=VMEM,
        scratch_shapes=[
            pltpu.VMEM((2, tokens, width), jnp.bfloat16),
            pltpu.SMEM((node_slots,), jnp.int32),
            pltpu.SemaphoreType.DMA((2,)),
        ],
        compiler_params=params(8),
    )(*in_hbm(node_lengths, node_kv))
    query_rows = queries.transpose(1, 0, 2).reshape(rows, feat_width)
    assert prompt_cols % CHUNK == 0 and node_slots * tokens == CHUNK
    weights_shape = (KV_HEADS, prompt_cols // CHUNK + 1, GROUP * rows, CHUNK)
    row_shape = jax.ShapeDtypeStruct((KV_HEADS, GROUP * rows, LANES), jnp.float32)
    weights, early_max, early_total, query, count, prompt_values, node_values = pl.pallas_call(
        functools.partial(early_kernel, steps),
        out_shape=(
            pltpu.HBM(weights_shape, jnp.float32),
            row_shape,
            row_shape,
            jax.ShapeDtypeStruct((KV_HEADS, GROUP * rows, HEAD_DIM), jnp.bfloat16),
            jax.ShapeDtypeStruct((leaf_count, owners * tokens), jnp.float32),
            jax.ShapeDtypeStruct((prompt_cols, width), jnp.bfloat16),
            jax.ShapeDtypeStruct((node_slots, tokens, width), jnp.bfloat16),
        ),
        in_specs=[HBM, HBM, HBM, HBM, VMEM],
        out_specs=(HBM,) + (VMEM,) * 6,
        scratch_shapes=[
            pltpu.SMEM((node_slots,), jnp.int32),
            pltpu.VMEM(ancestors.shape, jnp.int32),
            pltpu.VMEM((prompt_cols, width), jnp.bfloat16),
            pltpu.VMEM((node_slots, tokens, width), jnp.bfloat16),
            pltpu.VMEM(weights_shape, jnp.float32),
            pltpu.SemaphoreType.DMA((6,)),
            pltpu.SemaphoreType.DMA(weights_shape[:2]),
        ],
        compiler_params=params(16),
        cost_estimate=pl.CostEstimate(flops=500_000_000, bytes_accessed=6_000_000, transcendentals=800_000),
    )(*in_hbm(node_lengths, ancestors, prompt_kv, node_kv), query_rows)

    shared = gather_shared(own, owners, count)
    parts = pl.pallas_call(
        late_kernel,
        out_shape=jax.ShapeDtypeStruct((HEADS, rows // 2, 2 * HEAD_DIM + LANES), jnp.int16),
        in_specs=[VMEM] * 8,
        out_specs=VMEM,
        compiler_params=params(16),
    )(query, shared, weights, early_max, early_total, count, prompt_values, node_values)

    parts = lax.all_to_all(parts, "seq", 0, 0, tiled=True)
    return pl.pallas_call(
        merge_kernel,
        out_shape=jax.ShapeDtypeStruct((leaf_count, steps, HEAD_DIM), jnp.bfloat16),
        in_specs=[VMEM],
        out_specs=VMEM,
        compiler_params=params(8),
    )(parts)


def solution(mesh):
    placed = (
        P("leaf", None, None),
        P(None, "seq", None),
        P(None, "leaf", "seq", None),
        P("leaf"),
        P("leaf", None),
    )
    return jax.shard_map(
        shards, mesh=mesh, in_specs=placed, out_specs=P("leaf", None, "seq"), check_vma=False
    )
```

```python
import functools

import jax
import jax.numpy as jnp
from jax import lax
from jax.experimental import pallas as pl
from jax.experimental.pallas import tpu as pltpu
from jax.sharding import PartitionSpec as P

HEADS = 16
KV_HEADS = 2
HEAD_DIM = 256
GROUP = HEADS // KV_HEADS
CHUNK = 256
LANES = 128
Z = 8
INVALID_KEY = 256.0
TOP = 32767.0
POINTS = (2.0**18, 2.0**26, 2.0**23)

VMEM = pl.BlockSpec(memory_space=pltpu.VMEM)
HBM = pl.BlockSpec(memory_space=pltpu.HBM)


def in_hbm(*arrays):
    return [pltpu.with_memory_space_constraint(array, pltpu.HBM) for array in arrays]


def params(mib):
    return pltpu.CompilerParams(vmem_limit_bytes=mib * 1024 * 1024)


def fold(x, combine):
    parts = [x[:, i : i + LANES] for i in range(0, x.shape[1], LANES)]
    return functools.reduce(combine, parts)


def tall(x, reps):
    return jnp.concatenate([x] * reps, axis=0)


def node_counts(anc, ids, levels):
    counts = jnp.zeros((anc.shape[0], ids.shape[1]), jnp.float32)
    for level in levels:
        counts = counts + jnp.where(anc[:, level : level + 1] == ids, 1.0, 0.0)
    return counts


def group_query(q_ref, k):
    heads = range(k * GROUP, (k + 1) * GROUP)
    query = jnp.concatenate([q_ref[:, h * HEAD_DIM : (h + 1) * HEAD_DIM] for h in heads], axis=0)
    return query * jnp.bfloat16(1.0 / 16.0)


def dot_nt(a, b):
    return lax.dot_general(a, b, (((1,), (1,)), ((), ())), preferred_element_type=jnp.float32)


def fetch(pairs, sems):
    copies = [pltpu.make_async_copy(src, dst, sems.at[i]) for i, (src, dst) in enumerate(pairs)]
    for copy in copies:
        copy.start()
    return copies


def post_kernel(lengths_hbm, node_hbm, out_ref, node_ref, lengths_ref, sems):
    node_slots = lengths_hbm.shape[0]
    tokens = node_ref.shape[1]
    for copy in fetch([(node_hbm.at[:, node_slots - 1], node_ref), (lengths_hbm, lengths_ref)], sems):
        copy.wait()
    present = lax.axis_index("seq") * tokens < lengths_ref[node_slots - 1]
    keys = jnp.where(present, node_ref[0], jnp.bfloat16(INVALID_KEY))
    values = node_ref[1]
    for copy in range(out_ref.shape[0]):
        out_ref[copy, 0:tokens] = keys
        out_ref[copy, tokens : 2 * tokens] = values


def copies_kernel(plane_ref, early_ref, out_ref):
    del early_ref
    for copy in range(out_ref.shape[0]):
        out_ref[copy] = plane_ref[...]


def early_kernel(
    steps,
    lengths_hbm,
    anc_hbm,
    prompt_hbm,
    node_hbm,
    q_ref,
    w_ref,
    max_ref,
    total_ref,
    query_ref,
    count_ref,
    prompt_values_ref,
    node_values_ref,
    lengths_ref,
    anc_ref,
    prompt_ref,
    node_ref,
    sems,
):
    copies = fetch(
        [
            (lengths_hbm, lengths_ref),
            (anc_hbm, anc_ref),
            (node_hbm.at[0], node_ref),
            (prompt_hbm.at[0], prompt_ref),
            (node_hbm.at[1], node_values_ref),
            (prompt_hbm.at[1], prompt_values_ref),
        ],
        sems,
    )
    leaf_count, level_count = anc_ref.shape
    node_slots, tokens, width = node_ref.shape
    node_cols = node_slots * tokens
    prompt_cols = prompt_ref.shape[0]
    shared_cols = count_ref.shape[1]
    for k in range(KV_HEADS):
        query_ref[k] = group_query(q_ref, k)
    copies[0].wait()
    copies[1].wait()
    anc = anc_ref[...]

    lane = lax.broadcasted_iota(jnp.int32, (1, shared_cols), 1)
    owner = lane // tokens
    count = node_counts(anc, owner * node_slots + node_slots - 1, range(level_count - 1))
    count_ref[...] = jnp.where(owner == lax.axis_index("leaf"), 0.0, count)

    lane = lax.broadcasted_iota(jnp.int32, (1, node_cols), 1)
    slot = lane // tokens
    position = lax.axis_index("seq") * tokens + lane % tokens
    length = jnp.zeros((1, node_cols), jnp.int32)
    for n in range(node_slots):
        length = jnp.where(slot == n, lengths_ref[n], length)
    ids = lax.axis_index("leaf") * node_slots + slot
    upper = node_counts(anc, ids, range(level_count - 1))
    own = node_counts(anc, ids, [level_count - 1])
    mult = []
    for step in range(steps):
        causal = jnp.where(position <= length - steps + step, 1.0, 0.0)
        mult.append(jnp.where(position < length, upper + own * causal, 0.0))
    mult = tall(jnp.concatenate(mult, axis=0), GROUP)
    copies[2].wait()
    copies[3].wait()

    for k in range(KV_HEADS):
        cols = slice(k * HEAD_DIM, (k + 1) * HEAD_DIM)
        query = query_ref[k]
        top = None
        for start in range(0, prompt_cols, CHUNK):
            s = dot_nt(query, prompt_ref[start : start + CHUNK, cols])
            w_ref[k, :, start : start + CHUNK] = s
            part = fold(s, jnp.maximum)
            top = part if top is None else jnp.maximum(top, part)
        s = dot_nt(query, node_ref[:, :, cols].reshape(node_cols, HEAD_DIM))
        s = jnp.where(mult > 0.0, s, -jnp.inf)
        w_ref[k, :, prompt_cols:] = s
        top = jnp.max(jnp.maximum(top, fold(s, jnp.maximum)), axis=1, keepdims=True)
        total = jnp.zeros((s.shape[0], LANES), jnp.float32)
        for start in range(0, prompt_cols, CHUNK):
            w = jnp.exp(w_ref[k, :, start : start + CHUNK] - top)
            w_ref[k, :, start : start + CHUNK] = w
            total = total + fold(w, jnp.add)
        w = jnp.exp(w_ref[k, :, prompt_cols:] - top) * mult
        w_ref[k, :, prompt_cols:] = w
        total = total + fold(w, jnp.add)
        total_ref[k] = jnp.broadcast_to(jnp.sum(total, axis=1, keepdims=True), total.shape)
        max_ref[k] = jnp.broadcast_to(top, total.shape)
    copies[4].wait()
    copies[5].wait()


def late_kernel(query_ref, shared_ref, w_ref, max_ref, total_ref, count_ref, prompt_ref, node_ref, own_ref, out_ref):
    owners = shared_ref.shape[0]
    tokens = shared_ref.shape[1] // 2
    prompt_cols = prompt_ref.shape[0]
    node_cols = node_ref.shape[0] * node_ref.shape[1]
    shared_cols = owners * tokens
    rows = query_ref.shape[1] // GROUP
    half = rows // 2
    count = count_ref[...]
    reps = GROUP * rows // count.shape[0]
    pick = jnp.where(lax.broadcasted_iota(jnp.int32, (8, HEAD_DIM), 1) == 0, 1.0, 0.0).astype(jnp.bfloat16)

    for k in range(KV_HEADS):
        cols = slice(k * HEAD_DIM, (k + 1) * HEAD_DIM)
        keys = shared_ref[:, 0:tokens, cols].reshape(shared_cols, HEAD_DIM)
        values = shared_ref[:, tokens : 2 * tokens, cols].reshape(shared_cols, HEAD_DIM)
        marks = dot_nt(pick, keys)[0:1]
        mult = tall(jnp.where(marks < INVALID_KEY / 2, count, 0.0), reps)
        s = dot_nt(query_ref[k], keys)
        s = jnp.where(mult > 0.0, s, -jnp.inf)
        early_max = max_ref[k]
        block_max = jnp.maximum(jnp.max(fold(s, jnp.maximum), axis=1, keepdims=True), early_max)
        scale = jnp.exp(early_max - block_max)
        w = jnp.exp(s - block_max[:, 0:1]) * mult
        total = jnp.sum(fold(w, jnp.add), axis=1, keepdims=True) + total_ref[k] * scale
        acc = jnp.dot(w.astype(jnp.bfloat16), values, preferred_element_type=jnp.float32)
        wide = jnp.concatenate([scale, scale], axis=1)
        for start in range(0, prompt_cols, CHUNK):
            w = (w_ref[k, :, start : start + CHUNK] * wide).astype(jnp.bfloat16)
            acc = acc + jnp.dot(w, prompt_ref[start : start + CHUNK, cols], preferred_element_type=jnp.float32)
        w = (w_ref[k, :, prompt_cols:] * wide).astype(jnp.bfloat16)
        node_values = node_ref[:, :, cols].reshape(node_cols, HEAD_DIM)
        acc = acc + jnp.dot(w, node_values, preferred_element_type=jnp.float32)

        core = lax.rem(lax.axis_index("seq"), 2)
        total = jnp.broadcast_to(total, block_max.shape)
        for pair in range(GROUP // 2):
            kept, sent = [], []
            for x in (acc, block_max, total):
                even = x[2 * pair * rows : (2 * pair + 1) * rows]
                odd = x[(2 * pair + 1) * rows : (2 * pair + 2) * rows]
                kept.append(jnp.where(core == 0, even, odd))
                sent.append(jnp.where(core == 0, odd, even))
            slot = k * (GROUP // 2) + pair
            lane = lax.broadcasted_iota(jnp.int32, (half, LANES), 1)
            stats = [jnp.where(lane % (LANES // 2) == 0, kept[1][i : i + half], kept[2][i : i + half]) for i in (0, half)]
            own_ref[slot, :, 2 * HEAD_DIM :] = jnp.where(lane < LANES // 2, stats[0], stats[1])
            own_ref[slot, :, 0:HEAD_DIM] = kept[0][:half]
            own_ref[slot, :, HEAD_DIM : 2 * HEAD_DIM] = kept[0][half:]
            data, fixed = to_wire(*sent)
            out_ref[slot, :, 0:HEAD_DIM] = data[:half]
            out_ref[slot, :, HEAD_DIM : 2 * HEAD_DIM] = data[half:]
            out_ref[slot, :, 2 * HEAD_DIM :] = jnp.where(lane < LANES // 2, fixed[:half], fixed[half:]).astype(jnp.int16)


def to_wire(acc, block_max, total):
    reach = jnp.maximum(jnp.max(fold(jnp.abs(acc), jnp.maximum), axis=1, keepdims=True), 1e-30)
    data = jnp.round(acc * (TOP / reach)).astype(jnp.int32).astype(jnp.int16)
    lane = lax.broadcasted_iota(jnp.int32, block_max.shape, 1) % (LANES // 2)
    log_total = jnp.log(total) * POINTS[1]
    log_reach = jnp.log(reach) * POINTS[2]
    value = jnp.where(lane < 2, block_max * POINTS[0], jnp.where(lane < 4, log_total, log_reach))
    value = jnp.round(value).astype(jnp.int32)
    return data, jnp.where(lane % 2 == 0, value >> 16, (value & 0xFFFF) - 0x8000)


def from_wire(stats, first, i):
    high = stats[:, first + 2 * i : first + 2 * i + 1]
    low = stats[:, first + 2 * i + 1 : first + 2 * i + 2] + 0x8000
    return ((high << 16) + low).astype(jnp.float32) * (1.0 / POINTS[i])


def pair_kernel(own_ref, other_ref, out_ref):
    slots, half, lanes = own_ref.shape
    rows = slots * half
    own_stats = own_ref[:, :, 2 * HEAD_DIM :].reshape(rows, LANES)
    other_stats = other_ref[:, :, 2 * HEAD_DIM :].reshape(rows, LANES).astype(jnp.int32)
    fixed = []
    for part in range(2):
        first = part * LANES // 2
        span = slice(part * HEAD_DIM, (part + 1) * HEAD_DIM)
        own_max, own_total = own_stats[:, first : first + 1], own_stats[:, first + 1 : first + 2]
        other_max = from_wire(other_stats, first, 0)
        top = jnp.maximum(own_max, other_max)
        own_scale = jnp.exp(own_max - top)
        shift = other_max - top
        total = own_total * own_scale + jnp.exp(shift + from_wire(other_stats, first, 1))
        other = other_ref[:, :, span].reshape(rows, HEAD_DIM).astype(jnp.int32).astype(jnp.float32)
        acc = own_ref[:, :, span].reshape(rows, HEAD_DIM) * own_scale
        acc = acc + other * (jnp.exp(shift + from_wire(other_stats, first, 2)) * (1.0 / TOP))
        shape = (rows, LANES)
        data, stats = to_wire(acc, jnp.broadcast_to(top, shape), jnp.broadcast_to(total, shape))
        out_ref[:, :, span] = data.reshape(slots, half, HEAD_DIM)
        fixed.append(stats)
    lane = lax.broadcasted_iota(jnp.int32, (rows, LANES), 1)
    stats = jnp.where(lane < LANES // 2, fixed[0], fixed[1]).astype(jnp.int16)
    out_ref[:, :, 2 * HEAD_DIM :] = stats.reshape(slots, half, LANES)


def merge_kernel(parts_ref, out_ref):
    blocks, half, _ = parts_ref.shape
    leaf_count = out_ref.shape[0]
    stats = [parts_ref[b, :, 2 * HEAD_DIM :].astype(jnp.int32) for b in range(blocks)]
    for part in range(2):
        first = part * LANES // 2
        tops = [from_wire(stats[b], first, 0) for b in range(blocks)]
        row_max = functools.reduce(jnp.maximum, tops)
        denominator = jnp.zeros((half, 1), jnp.float32)
        numerator = jnp.zeros((half, HEAD_DIM), jnp.float32)
        for b in range(blocks):
            shift = tops[b] - row_max
            denominator = denominator + jnp.exp(shift + from_wire(stats[b], first, 1))
            data = parts_ref[b, :, part * HEAD_DIM : (part + 1) * HEAD_DIM].astype(jnp.int32).astype(jnp.float32)
            numerator = numerator + jnp.exp(shift + from_wire(stats[b], first, 2)) * data
        merged = (numerator / (denominator * TOP)).astype(jnp.bfloat16)
        for i in range(half // leaf_count):
            out_ref[:, part * half // leaf_count + i, :] = merged[i * leaf_count : (i + 1) * leaf_count]


def gather_shared(own, owners, early):
    along_z = [list(range(x, x + Z)) for x in range(0, owners, Z)]
    along_x = [list(range(z, owners, Z)) for z in range(Z)]
    plane = lax.all_to_all(own, "leaf", 0, 0, tiled=True, axis_index_groups=along_z)
    plane = pl.pallas_call(
        copies_kernel,
        out_shape=jax.ShapeDtypeStruct((owners // Z,) + plane.shape, plane.dtype),
        in_specs=[VMEM, VMEM],
        out_specs=VMEM,
        compiler_params=params(8),
    )(plane, early)
    shared = lax.all_to_all(plane, "leaf", 0, 0, tiled=True, axis_index_groups=along_x)
    return shared.reshape((owners,) + own.shape[1:])


def shards(queries, prompt_kv, node_kv, node_lengths, ancestors):
    leaf_count, steps, feat_width = queries.shape
    node_slots, tokens = node_kv.shape[1:3]
    prompt_cols = prompt_kv.shape[1]
    width = KV_HEADS * HEAD_DIM
    rows = steps * leaf_count
    owners = lax.axis_size("leaf")

    own = pl.pallas_call(
        post_kernel,
        out_shape=jax.ShapeDtypeStruct((Z, 2 * tokens, width), jnp.bfloat16),
        in_specs=[HBM, HBM],
        out_specs=VMEM,
        scratch_shapes=[
            pltpu.VMEM((2, tokens, width), jnp.bfloat16),
            pltpu.SMEM((node_slots,), jnp.int32),
            pltpu.SemaphoreType.DMA((2,)),
        ],
        compiler_params=params(8),
    )(*in_hbm(node_lengths, node_kv))
    query_rows = queries.transpose(1, 0, 2).reshape(rows, feat_width)
    cols = prompt_cols + node_slots * tokens
    row_shape = jax.ShapeDtypeStruct((KV_HEADS, GROUP * rows, LANES), jnp.float32)
    weights, early_max, early_total, query, count, prompt_values, node_values = pl.pallas_call(
        functools.partial(early_kernel, steps),
        out_shape=(
            jax.ShapeDtypeStruct((KV_HEADS, GROUP * rows, cols), jnp.float32),
            row_shape,
            row_shape,
            jax.ShapeDtypeStruct((KV_HEADS, GROUP * rows, HEAD_DIM), jnp.bfloat16),
            jax.ShapeDtypeStruct((leaf_count, owners * tokens), jnp.float32),
            jax.ShapeDtypeStruct((prompt_cols, width), jnp.bfloat16),
            jax.ShapeDtypeStruct((node_slots, tokens, width), jnp.bfloat16),
        ),
        in_specs=[HBM, HBM, HBM, HBM, VMEM],
        out_specs=(VMEM,) * 7,
        scratch_shapes=[
            pltpu.SMEM((node_slots,), jnp.int32),
            pltpu.VMEM(ancestors.shape, jnp.int32),
            pltpu.VMEM((prompt_cols, width), jnp.bfloat16),
            pltpu.VMEM((node_slots, tokens, width), jnp.bfloat16),
            pltpu.SemaphoreType.DMA((6,)),
        ],
        compiler_params=params(16),
        cost_estimate=pl.CostEstimate(flops=500_000_000, bytes_accessed=6_000_000, transcendentals=800_000),
    )(*in_hbm(node_lengths, ancestors, prompt_kv, node_kv), query_rows)

    shared = gather_shared(own, owners, count)
    seqs = lax.axis_size("seq")
    wire = jax.ShapeDtypeStruct((HEADS // 2, rows // 2, 2 * HEAD_DIM + LANES), jnp.int16)
    kept, sent = pl.pallas_call(
        late_kernel,
        out_shape=(jax.ShapeDtypeStruct(wire.shape, jnp.float32), wire),
        in_specs=[VMEM] * 8,
        out_specs=(VMEM, VMEM),
        compiler_params=params(16),
    )(query, shared, weights, early_max, early_total, count, prompt_values, node_values)

    got = lax.ppermute(sent, "seq", [(i, i ^ 1) for i in range(seqs)])
    parts = pl.pallas_call(
        pair_kernel,
        out_shape=wire,
        in_specs=[VMEM, VMEM],
        out_specs=VMEM,
        compiler_params=params(8),
    )(kept, got)
    chips = [list(range(c, seqs, 2)) for c in range(2)]
    parts = lax.all_to_all(parts, "seq", 0, 0, tiled=True, axis_index_groups=chips)
    return pl.pallas_call(
        merge_kernel,
        out_shape=jax.ShapeDtypeStruct((leaf_count, steps, HEAD_DIM), jnp.bfloat16),
        in_specs=[VMEM],
        out_specs=VMEM,
        compiler_params=params(8),
    )(parts)


def solution(mesh):
    placed = (
        P("leaf", None, None),
        P(None, "seq", None),
        P(None, "leaf", "seq", None),
        P("leaf"),
        P("leaf", None),
    )
    return jax.shard_map(
        shards, mesh=mesh, in_specs=placed, out_specs=P("leaf", None, "seq"), check_vma=False
    )
```

```python
import functools

import jax
import jax.numpy as jnp
from jax import lax
from jax.experimental import pallas as pl
from jax.experimental.pallas import tpu as pltpu
from jax.sharding import PartitionSpec as P

HEADS = 16
KV_HEADS = 2
HEAD_DIM = 256
GROUP = HEADS // KV_HEADS
CHUNK = 256
LANES = 128
Z = 8
INVALID_KEY = 256.0
TOP = 32767.0
POINTS = (2.0**18, 2.0**26, 2.0**23)

VMEM = pl.BlockSpec(memory_space=pltpu.VMEM)
HBM = pl.BlockSpec(memory_space=pltpu.HBM)


def in_hbm(*arrays):
    return [pltpu.with_memory_space_constraint(array, pltpu.HBM) for array in arrays]


def params(mib):
    return pltpu.CompilerParams(vmem_limit_bytes=mib * 1024 * 1024)


def fold(x, combine):
    parts = [x[:, i : i + LANES] for i in range(0, x.shape[1], LANES)]
    return functools.reduce(combine, parts)


def tall(x, reps):
    return jnp.concatenate([x] * reps, axis=0)


def node_counts(anc, ids, levels):
    counts = jnp.zeros((anc.shape[0], ids.shape[1]), jnp.float32)
    for level in levels:
        counts = counts + jnp.where(anc[:, level : level + 1] == ids, 1.0, 0.0)
    return counts


def group_query(q_ref, k):
    heads = range(k * GROUP, (k + 1) * GROUP)
    query = jnp.concatenate([q_ref[:, h * HEAD_DIM : (h + 1) * HEAD_DIM] for h in heads], axis=0)
    return query * jnp.bfloat16(1.0 / 16.0)


def dot_nt(a, b):
    return lax.dot_general(a, b, (((1,), (1,)), ((), ())), preferred_element_type=jnp.float32)


def fetch(pairs, sems):
    copies = [pltpu.make_async_copy(src, dst, sems.at[i]) for i, (src, dst) in enumerate(pairs)]
    for copy in copies:
        copy.start()
    return copies


def post_kernel(lengths_hbm, node_hbm, out_ref, node_ref, lengths_ref, sems):
    node_slots = lengths_hbm.shape[0]
    tokens = node_ref.shape[1]
    for copy in fetch([(node_hbm.at[:, node_slots - 1], node_ref), (lengths_hbm, lengths_ref)], sems):
        copy.wait()
    present = lax.axis_index("seq") * tokens < lengths_ref[node_slots - 1]
    keys = jnp.where(present, node_ref[0], jnp.bfloat16(INVALID_KEY))
    values = node_ref[1]
    for copy in range(out_ref.shape[0]):
        out_ref[copy, 0:tokens] = keys
        out_ref[copy, tokens : 2 * tokens] = values


def early_kernel(
    steps,
    lengths_hbm,
    anc_hbm,
    prompt_hbm,
    node_hbm,
    q_ref,
    w_ref,
    max_ref,
    total_ref,
    query_ref,
    count_ref,
    prompt_values_ref,
    node_values_ref,
    lengths_ref,
    anc_ref,
    prompt_ref,
    node_ref,
    sems,
):
    copies = fetch(
        [
            (lengths_hbm, lengths_ref),
            (anc_hbm, anc_ref),
            (node_hbm.at[0], node_ref),
            (prompt_hbm.at[0], prompt_ref),
            (node_hbm.at[1], node_values_ref),
            (prompt_hbm.at[1], prompt_values_ref),
        ],
        sems,
    )
    leaf_count, level_count = anc_ref.shape
    node_slots, tokens, width = node_ref.shape
    node_cols = node_slots * tokens
    prompt_cols = prompt_ref.shape[0]
    shared_cols = count_ref.shape[1]
    planes = shared_cols // (tokens * Z)
    for k in range(KV_HEADS):
        query_ref[k] = group_query(q_ref, k)
    copies[0].wait()
    copies[1].wait()
    anc = anc_ref[...]

    lane = lax.broadcasted_iota(jnp.int32, (1, shared_cols), 1)
    device = lax.axis_index("leaf")
    plane, along_z = lane // (tokens * Z), lane // tokens % Z
    owner = lax.rem(device // Z - plane + planes, planes) * Z + along_z
    count = node_counts(anc, owner * node_slots + node_slots - 1, range(level_count - 1))
    count_ref[...] = jnp.where(owner == device, 0.0, count)

    lane = lax.broadcasted_iota(jnp.int32, (1, node_cols), 1)
    slot = lane // tokens
    position = lax.axis_index("seq") * tokens + lane % tokens
    length = jnp.zeros((1, node_cols), jnp.int32)
    for n in range(node_slots):
        length = jnp.where(slot == n, lengths_ref[n], length)
    ids = lax.axis_index("leaf") * node_slots + slot
    upper = node_counts(anc, ids, range(level_count - 1))
    own = node_counts(anc, ids, [level_count - 1])
    mult = []
    for step in range(steps):
        causal = jnp.where(position <= length - steps + step, 1.0, 0.0)
        mult.append(jnp.where(position < length, upper + own * causal, 0.0))
    mult = tall(jnp.concatenate(mult, axis=0), GROUP)
    copies[2].wait()
    copies[3].wait()

    for k in range(KV_HEADS):
        cols = slice(k * HEAD_DIM, (k + 1) * HEAD_DIM)
        query = query_ref[k]
        top = None
        for start in range(0, prompt_cols, CHUNK):
            s = dot_nt(query, prompt_ref[start : start + CHUNK, cols])
            w_ref[k, :, start : start + CHUNK] = s
            part = fold(s, jnp.maximum)
            top = part if top is None else jnp.maximum(top, part)
        s = dot_nt(query, node_ref[:, :, cols].reshape(node_cols, HEAD_DIM))
        s = jnp.where(mult > 0.0, s, -jnp.inf)
        w_ref[k, :, prompt_cols:] = s
        top = jnp.max(jnp.maximum(top, fold(s, jnp.maximum)), axis=1, keepdims=True)
        total = jnp.zeros((s.shape[0], LANES), jnp.float32)
        for start in range(0, prompt_cols, CHUNK):
            w = jnp.exp(w_ref[k, :, start : start + CHUNK] - top)
            w_ref[k, :, start : start + CHUNK] = w
            total = total + fold(w, jnp.add)
        w = jnp.exp(w_ref[k, :, prompt_cols:] - top) * mult
        w_ref[k, :, prompt_cols:] = w
        total = total + fold(w, jnp.add)
        total_ref[k] = jnp.broadcast_to(jnp.sum(total, axis=1, keepdims=True), total.shape)
        max_ref[k] = jnp.broadcast_to(top, total.shape)
    copies[4].wait()
    copies[5].wait()


def late_kernel(planes, *refs):
    shared_refs = refs[:planes]
    query_ref, w_ref, max_ref, total_ref, count_ref, prompt_ref, node_ref, own_ref, out_ref = refs[planes:]
    tokens = shared_refs[0].shape[1] // 2
    prompt_cols = prompt_ref.shape[0]
    node_cols = node_ref.shape[0] * node_ref.shape[1]
    rows = query_ref.shape[1] // GROUP
    half = rows // 2

    def shared_rows(first, cols):
        return jnp.concatenate(
            [ref[:, first : first + tokens, cols].reshape(Z * tokens, HEAD_DIM) for ref in shared_refs], axis=0
        )

    count = count_ref[...]
    reps = GROUP * rows // count.shape[0]
    pick = jnp.where(lax.broadcasted_iota(jnp.int32, (8, HEAD_DIM), 1) == 0, 1.0, 0.0).astype(jnp.bfloat16)

    for k in range(KV_HEADS):
        cols = slice(k * HEAD_DIM, (k + 1) * HEAD_DIM)
        keys = shared_rows(0, cols)
        values = shared_rows(tokens, cols)
        marks = dot_nt(pick, keys)[0:1]
        mult = tall(jnp.where(marks < INVALID_KEY / 2, count, 0.0), reps)
        s = dot_nt(query_ref[k], keys)
        s = jnp.where(mult > 0.0, s, -jnp.inf)
        early_max = max_ref[k]
        block_max = jnp.maximum(jnp.max(fold(s, jnp.maximum), axis=1, keepdims=True), early_max)
        scale = jnp.exp(early_max - block_max)
        w = jnp.exp(s - block_max[:, 0:1]) * mult
        total = jnp.sum(fold(w, jnp.add), axis=1, keepdims=True) + total_ref[k] * scale
        acc = jnp.dot(w.astype(jnp.bfloat16), values, preferred_element_type=jnp.float32)
        wide = jnp.concatenate([scale, scale], axis=1)
        for start in range(0, prompt_cols, CHUNK):
            w = (w_ref[k, :, start : start + CHUNK] * wide).astype(jnp.bfloat16)
            acc = acc + jnp.dot(w, prompt_ref[start : start + CHUNK, cols], preferred_element_type=jnp.float32)
        w = (w_ref[k, :, prompt_cols:] * wide).astype(jnp.bfloat16)
        node_values = node_ref[:, :, cols].reshape(node_cols, HEAD_DIM)
        acc = acc + jnp.dot(w, node_values, preferred_element_type=jnp.float32)

        core = lax.rem(lax.axis_index("seq"), 2)
        total = jnp.broadcast_to(total, block_max.shape)
        for pair in range(GROUP // 2):
            kept, sent = [], []
            for x in (acc, block_max, total):
                even = x[2 * pair * rows : (2 * pair + 1) * rows]
                odd = x[(2 * pair + 1) * rows : (2 * pair + 2) * rows]
                kept.append(jnp.where(core == 0, even, odd))
                sent.append(jnp.where(core == 0, odd, even))
            slot = k * (GROUP // 2) + pair
            lane = lax.broadcasted_iota(jnp.int32, (half, LANES), 1)
            stats = [jnp.where(lane % (LANES // 2) == 0, kept[1][i : i + half], kept[2][i : i + half]) for i in (0, half)]
            own_ref[slot, :, 2 * HEAD_DIM :] = jnp.where(lane < LANES // 2, stats[0], stats[1])
            own_ref[slot, :, 0:HEAD_DIM] = kept[0][:half]
            own_ref[slot, :, HEAD_DIM : 2 * HEAD_DIM] = kept[0][half:]
            data, fixed = to_wire(*sent)
            out_ref[slot, :, 0:HEAD_DIM] = data[:half]
            out_ref[slot, :, HEAD_DIM : 2 * HEAD_DIM] = data[half:]
            out_ref[slot, :, 2 * HEAD_DIM :] = jnp.where(lane < LANES // 2, fixed[:half], fixed[half:]).astype(jnp.int16)


def to_wire(acc, block_max, total):
    reach = jnp.maximum(jnp.max(fold(jnp.abs(acc), jnp.maximum), axis=1, keepdims=True), 1e-30)
    data = jnp.round(acc * (TOP / reach)).astype(jnp.int32).astype(jnp.int16)
    lane = lax.broadcasted_iota(jnp.int32, block_max.shape, 1) % (LANES // 2)
    log_total = jnp.log(total) * POINTS[1]
    log_reach = jnp.log(reach) * POINTS[2]
    value = jnp.where(lane < 2, block_max * POINTS[0], jnp.where(lane < 4, log_total, log_reach))
    value = jnp.round(value).astype(jnp.int32)
    return data, jnp.where(lane % 2 == 0, value >> 16, (value & 0xFFFF) - 0x8000)


def from_wire(stats, first, i):
    high = stats[:, first + 2 * i : first + 2 * i + 1]
    low = stats[:, first + 2 * i + 1 : first + 2 * i + 2] + 0x8000
    return ((high << 16) + low).astype(jnp.float32) * (1.0 / POINTS[i])


def pair_kernel(own_ref, other_ref, out_ref):
    slots, half, lanes = own_ref.shape
    rows = slots * half
    own_stats = own_ref[:, :, 2 * HEAD_DIM :].reshape(rows, LANES)
    other_stats = other_ref[:, :, 2 * HEAD_DIM :].reshape(rows, LANES).astype(jnp.int32)
    fixed = []
    for part in range(2):
        first = part * LANES // 2
        span = slice(part * HEAD_DIM, (part + 1) * HEAD_DIM)
        own_max, own_total = own_stats[:, first : first + 1], own_stats[:, first + 1 : first + 2]
        other_max = from_wire(other_stats, first, 0)
        top = jnp.maximum(own_max, other_max)
        own_scale = jnp.exp(own_max - top)
        shift = other_max - top
        total = own_total * own_scale + jnp.exp(shift + from_wire(other_stats, first, 1))
        other = other_ref[:, :, span].reshape(rows, HEAD_DIM).astype(jnp.int32).astype(jnp.float32)
        acc = own_ref[:, :, span].reshape(rows, HEAD_DIM) * own_scale
        acc = acc + other * (jnp.exp(shift + from_wire(other_stats, first, 2)) * (1.0 / TOP))
        shape = (rows, LANES)
        data, stats = to_wire(acc, jnp.broadcast_to(top, shape), jnp.broadcast_to(total, shape))
        out_ref[:, :, span] = data.reshape(slots, half, HEAD_DIM)
        fixed.append(stats)
    lane = lax.broadcasted_iota(jnp.int32, (rows, LANES), 1)
    stats = jnp.where(lane < LANES // 2, fixed[0], fixed[1]).astype(jnp.int16)
    out_ref[:, :, 2 * HEAD_DIM :] = stats.reshape(slots, half, LANES)


def merge_kernel(parts_ref, out_ref):
    blocks, half, _ = parts_ref.shape
    leaf_count = out_ref.shape[0]
    stats = [parts_ref[b, :, 2 * HEAD_DIM :].astype(jnp.int32) for b in range(blocks)]
    for part in range(2):
        first = part * LANES // 2
        tops = [from_wire(stats[b], first, 0) for b in range(blocks)]
        row_max = functools.reduce(jnp.maximum, tops)
        denominator = jnp.zeros((half, 1), jnp.float32)
        numerator = jnp.zeros((half, HEAD_DIM), jnp.float32)
        for b in range(blocks):
            shift = tops[b] - row_max
            denominator = denominator + jnp.exp(shift + from_wire(stats[b], first, 1))
            data = parts_ref[b, :, part * HEAD_DIM : (part + 1) * HEAD_DIM].astype(jnp.int32).astype(jnp.float32)
            numerator = numerator + jnp.exp(shift + from_wire(stats[b], first, 2)) * data
        merged = (numerator / (denominator * TOP)).astype(jnp.bfloat16)
        for i in range(half // leaf_count):
            out_ref[:, part * half // leaf_count + i, :] = merged[i * leaf_count : (i + 1) * leaf_count]


def gather_shared(own, owners):
    along_z = [list(range(x, x + Z)) for x in range(0, owners, Z)]
    plane = lax.all_to_all(own, "leaf", 0, 0, tiled=True, axis_index_groups=along_z)
    planes = owners // Z
    got = {0: plane}
    for k in sorted(range(1, planes), key=lambda k: (min(k, planes - k), k)):
        got[k] = lax.ppermute(plane, "leaf", [(i, (i + k * Z) % owners) for i in range(owners)])
    return [got[k] for k in range(planes)]


def shards(queries, prompt_kv, node_kv, node_lengths, ancestors):
    leaf_count, steps, feat_width = queries.shape
    node_slots, tokens = node_kv.shape[1:3]
    prompt_cols = prompt_kv.shape[1]
    width = KV_HEADS * HEAD_DIM
    rows = steps * leaf_count
    owners = lax.axis_size("leaf")

    own = pl.pallas_call(
        post_kernel,
        out_shape=jax.ShapeDtypeStruct((Z, 2 * tokens, width), jnp.bfloat16),
        in_specs=[HBM, HBM],
        out_specs=VMEM,
        scratch_shapes=[
            pltpu.VMEM((2, tokens, width), jnp.bfloat16),
            pltpu.SMEM((node_slots,), jnp.int32),
            pltpu.SemaphoreType.DMA((2,)),
        ],
        compiler_params=params(8),
    )(*in_hbm(node_lengths, node_kv))
    query_rows = queries.transpose(1, 0, 2).reshape(rows, feat_width)
    cols = prompt_cols + node_slots * tokens
    row_shape = jax.ShapeDtypeStruct((KV_HEADS, GROUP * rows, LANES), jnp.float32)
    weights, early_max, early_total, query, count, prompt_values, node_values = pl.pallas_call(
        functools.partial(early_kernel, steps),
        out_shape=(
            jax.ShapeDtypeStruct((KV_HEADS, GROUP * rows, cols), jnp.float32),
            row_shape,
            row_shape,
            jax.ShapeDtypeStruct((KV_HEADS, GROUP * rows, HEAD_DIM), jnp.bfloat16),
            jax.ShapeDtypeStruct((leaf_count, owners * tokens), jnp.float32),
            jax.ShapeDtypeStruct((prompt_cols, width), jnp.bfloat16),
            jax.ShapeDtypeStruct((node_slots, tokens, width), jnp.bfloat16),
        ),
        in_specs=[HBM, HBM, HBM, HBM, VMEM],
        out_specs=(VMEM,) * 7,
        scratch_shapes=[
            pltpu.SMEM((node_slots,), jnp.int32),
            pltpu.VMEM(ancestors.shape, jnp.int32),
            pltpu.VMEM((prompt_cols, width), jnp.bfloat16),
            pltpu.VMEM((node_slots, tokens, width), jnp.bfloat16),
            pltpu.SemaphoreType.DMA((6,)),
        ],
        compiler_params=params(16),
        cost_estimate=pl.CostEstimate(flops=500_000_000, bytes_accessed=6_000_000, transcendentals=800_000),
    )(*in_hbm(node_lengths, ancestors, prompt_kv, node_kv), query_rows)

    shared = gather_shared(own, owners)
    seqs = lax.axis_size("seq")
    wire = jax.ShapeDtypeStruct((HEADS // 2, rows // 2, 2 * HEAD_DIM + LANES), jnp.int16)
    kept, sent = pl.pallas_call(
        functools.partial(late_kernel, len(shared)),
        out_shape=(jax.ShapeDtypeStruct(wire.shape, jnp.float32), wire),
        in_specs=[VMEM] * (len(shared) + 7),
        out_specs=(VMEM, VMEM),
        compiler_params=params(16),
    )(*shared, query, weights, early_max, early_total, count, prompt_values, node_values)

    got = lax.ppermute(sent, "seq", [(i, i ^ 1) for i in range(seqs)])
    parts = pl.pallas_call(
        pair_kernel,
        out_shape=wire,
        in_specs=[VMEM, VMEM],
        out_specs=VMEM,
        compiler_params=params(8),
    )(kept, got)
    chips = [list(range(c, seqs, 2)) for c in range(2)]
    parts = lax.all_to_all(parts, "seq", 0, 0, tiled=True, axis_index_groups=chips)
    return pl.pallas_call(
        merge_kernel,
        out_shape=jax.ShapeDtypeStruct((leaf_count, steps, HEAD_DIM), jnp.bfloat16),
        in_specs=[VMEM],
        out_specs=VMEM,
        compiler_params=params(8),
    )(parts)


def solution(mesh):
    placed = (
        P("leaf", None, None),
        P(None, "seq", None),
        P(None, "leaf", "seq", None),
        P("leaf"),
        P("leaf", None),
    )
    return jax.shard_map(
        shards, mesh=mesh, in_specs=placed, out_specs=P("leaf", None, "seq"), check_vma=False
    )
```

```python
import functools

import jax
import jax.numpy as jnp
from jax import lax
from jax.experimental import pallas as pl
from jax.experimental.pallas import tpu as pltpu
from jax.sharding import PartitionSpec as P

HEADS = 16
KV_HEADS = 2
HEAD_DIM = 256
GROUP = HEADS // KV_HEADS
CHUNK = 256
LANES = 128
Z = 8
STRIDE = 2
INVALID_KEY = 256.0
TOP = 32767.0
POINTS = (2.0**18, 2.0**26, 2.0**23)

VMEM = pl.BlockSpec(memory_space=pltpu.VMEM)
HBM = pl.BlockSpec(memory_space=pltpu.HBM)


def in_hbm(*arrays):
    return [pltpu.with_memory_space_constraint(array, pltpu.HBM) for array in arrays]


def params(mib):
    return pltpu.CompilerParams(vmem_limit_bytes=mib * 1024 * 1024)


def fold(x, combine):
    parts = [x[:, i : i + LANES] for i in range(0, x.shape[1], LANES)]
    return functools.reduce(combine, parts)


def tall(x, reps):
    return jnp.concatenate([x] * reps, axis=0)


def node_counts(anc, ids, levels):
    counts = jnp.zeros((anc.shape[0], ids.shape[1]), jnp.float32)
    for level in levels:
        counts = counts + jnp.where(anc[:, level : level + 1] == ids, 1.0, 0.0)
    return counts


def group_query(q_ref, k):
    heads = range(k * GROUP, (k + 1) * GROUP)
    query = jnp.concatenate([q_ref[:, h * HEAD_DIM : (h + 1) * HEAD_DIM] for h in heads], axis=0)
    return query * jnp.bfloat16(1.0 / 16.0)


def dot_nt(a, b):
    return lax.dot_general(a, b, (((1,), (1,)), ((), ())), preferred_element_type=jnp.float32)


def fetch(pairs, sems):
    copies = [pltpu.make_async_copy(src, dst, sems.at[i]) for i, (src, dst) in enumerate(pairs)]
    for copy in copies:
        copy.start()
    return copies


def post_kernel(lengths_hbm, node_hbm, out_ref, node_ref, lengths_ref, sems):
    node_slots = lengths_hbm.shape[0]
    tokens = node_ref.shape[1]
    for copy in fetch([(node_hbm.at[:, node_slots - 1], node_ref), (lengths_hbm, lengths_ref)], sems):
        copy.wait()
    present = lax.axis_index("seq") * tokens < lengths_ref[node_slots - 1]
    keys = jnp.where(present, node_ref[0], jnp.bfloat16(INVALID_KEY))
    values = node_ref[1]
    for copy in range(out_ref.shape[0]):
        out_ref[copy, 0:tokens] = keys
        out_ref[copy, tokens : 2 * tokens] = values


def copies_kernel(plane_ref, early_ref, out_ref):
    del early_ref
    for copy in range(out_ref.shape[0]):
        out_ref[copy] = plane_ref[...]


def early_kernel(
    steps,
    lengths_hbm,
    anc_hbm,
    prompt_hbm,
    node_hbm,
    q_ref,
    w_ref,
    half_ref,
    count_ref,
    lengths_ref,
    anc_ref,
    prompt_ref,
    node_ref,
    sems,
):
    copies = fetch(
        [
            (lengths_hbm, lengths_ref),
            (anc_hbm, anc_ref),
            (node_hbm.at[0], node_ref),
            (prompt_hbm.at[0], prompt_ref),
            (prompt_hbm.at[1], half_ref.at[pl.ds(0, prompt_ref.shape[0])]),
        ]
        + [
            (node_hbm.at[1, n], half_ref.at[pl.ds(prompt_ref.shape[0] + n * node_ref.shape[1], node_ref.shape[1])])
            for n in range(node_ref.shape[0])
        ],
        sems,
    )
    leaf_count, level_count = anc_ref.shape
    node_slots, tokens, width = node_ref.shape
    node_cols = node_slots * tokens
    prompt_cols = prompt_ref.shape[0]
    shared_cols = count_ref.shape[1]
    for k in range(KV_HEADS):
        half_ref[prompt_cols + node_cols :, k * HEAD_DIM : (k + 1) * HEAD_DIM] = group_query(q_ref, k)
    copies[0].wait()
    copies[1].wait()
    anc = anc_ref[...]

    lane = lax.broadcasted_iota(jnp.int32, (1, shared_cols), 1)
    block = lane // tokens
    owner = block // Z * Z + block % (Z // STRIDE) * STRIDE + block // (Z // STRIDE) % STRIDE
    count = node_counts(anc, owner * node_slots + node_slots - 1, range(level_count - 1))
    count_ref[...] = jnp.where(owner == lax.axis_index("leaf"), 0.0, count)

    lane = lax.broadcasted_iota(jnp.int32, (1, node_cols), 1)
    slot = lane // tokens
    position = lax.axis_index("seq") * tokens + lane % tokens
    length = jnp.zeros((1, node_cols), jnp.int32)
    for n in range(node_slots):
        length = jnp.where(slot == n, lengths_ref[n], length)
    ids = lax.axis_index("leaf") * node_slots + slot
    upper = node_counts(anc, ids, range(level_count - 1))
    own = node_counts(anc, ids, [level_count - 1])
    mult = []
    for step in range(steps):
        causal = jnp.where(position <= length - steps + step, 1.0, 0.0)
        mult.append(jnp.where(position < length, upper + own * causal, 0.0))
    mult = tall(jnp.concatenate(mult, axis=0), GROUP)
    copies[2].wait()
    copies[3].wait()

    for k in range(KV_HEADS):
        cols = slice(k * HEAD_DIM, (k + 1) * HEAD_DIM)
        query = half_ref[prompt_cols + node_cols :, cols]
        top = None
        for start in range(0, prompt_cols, CHUNK):
            s = dot_nt(query, prompt_ref[start : start + CHUNK, cols])
            w_ref[k, start // CHUNK] = s
            part = fold(s, jnp.maximum)
            top = part if top is None else jnp.maximum(top, part)
        s = dot_nt(query, node_ref[:, :, cols].reshape(node_cols, HEAD_DIM))
        s = jnp.where(mult > 0.0, s, -jnp.inf)
        w_ref[k, prompt_cols // CHUNK] = s
        top = jnp.max(jnp.maximum(top, fold(s, jnp.maximum)), axis=1, keepdims=True)
        total = jnp.zeros((s.shape[0], LANES), jnp.float32)
        for start in range(0, prompt_cols, CHUNK):
            w = jnp.exp(w_ref[k, start // CHUNK] - top)
            w_ref[k, start // CHUNK] = w
            total = total + fold(w, jnp.add)
        w = jnp.exp(w_ref[k, prompt_cols // CHUNK] - top) * mult
        w_ref[k, prompt_cols // CHUNK] = w
        total = total + fold(w, jnp.add)
        w_ref[k, prompt_cols // CHUNK + 1, :, LANES:] = jnp.broadcast_to(jnp.sum(total, axis=1, keepdims=True), total.shape)
        w_ref[k, prompt_cols // CHUNK + 1, :, :LANES] = jnp.broadcast_to(top, total.shape)
    for copy in copies[4:]:
        copy.wait()


def late_kernel(shared_ref, w_ref, half_ref, count_ref, own_ref, out_ref):
    owners = shared_ref.shape[0]
    tokens = shared_ref.shape[1] // 2
    shared_cols = owners * tokens
    rows = w_ref.shape[2] // GROUP
    half = rows // 2
    chunks = w_ref.shape[1] - 1
    early_cols = chunks * CHUNK
    count = count_ref[...]
    reps = GROUP * rows // count.shape[0]
    pick = jnp.where(lax.broadcasted_iota(jnp.int32, (8, HEAD_DIM), 1) == 0, 1.0, 0.0).astype(jnp.bfloat16)

    for k in range(KV_HEADS):
        cols = slice(k * HEAD_DIM, (k + 1) * HEAD_DIM)
        keys = shared_ref[:, 0:tokens, cols].reshape(shared_cols, HEAD_DIM)
        values = shared_ref[:, tokens : 2 * tokens, cols].reshape(shared_cols, HEAD_DIM)
        marks = dot_nt(pick, keys)[0:1]
        mult = tall(jnp.where(marks < INVALID_KEY / 2, count, 0.0), reps)
        s = dot_nt(half_ref[early_cols:, cols], keys)
        s = jnp.where(mult > 0.0, s, -jnp.inf)
        early_max = w_ref[k, chunks, :, :LANES]
        block_max = jnp.maximum(jnp.max(fold(s, jnp.maximum), axis=1, keepdims=True), early_max)
        scale = jnp.exp(early_max - block_max)
        w = jnp.exp(s - block_max[:, 0:1]) * mult
        total = jnp.sum(fold(w, jnp.add), axis=1, keepdims=True) + w_ref[k, chunks, :, LANES:] * scale
        acc = jnp.dot(w.astype(jnp.bfloat16), values, preferred_element_type=jnp.float32)
        wide = jnp.concatenate([scale, scale], axis=1)
        for c in range(chunks):
            w = (w_ref[k, c] * wide).astype(jnp.bfloat16)
            acc = acc + jnp.dot(w, half_ref[c * CHUNK : (c + 1) * CHUNK, cols], preferred_element_type=jnp.float32)

        core = lax.rem(lax.axis_index("seq"), 2)
        total = jnp.broadcast_to(total, block_max.shape)
        for pair in range(GROUP // 2):
            kept, sent = [], []
            for x in (acc, block_max, total):
                even = x[2 * pair * rows : (2 * pair + 1) * rows]
                odd = x[(2 * pair + 1) * rows : (2 * pair + 2) * rows]
                kept.append(jnp.where(core == 0, even, odd))
                sent.append(jnp.where(core == 0, odd, even))
            slot = k * (GROUP // 2) + pair
            lane = lax.broadcasted_iota(jnp.int32, (half, LANES), 1)
            stats = [jnp.where(lane % (LANES // 2) == 0, kept[1][i : i + half], kept[2][i : i + half]) for i in (0, half)]
            own_ref[slot, :, 2 * HEAD_DIM :] = jnp.where(lane < LANES // 2, stats[0], stats[1])
            own_ref[slot, :, 0:HEAD_DIM] = kept[0][:half]
            own_ref[slot, :, HEAD_DIM : 2 * HEAD_DIM] = kept[0][half:]
            data, fixed = to_wire(*sent)
            out_ref[slot, :, 0:HEAD_DIM] = data[:half]
            out_ref[slot, :, HEAD_DIM : 2 * HEAD_DIM] = data[half:]
            out_ref[slot, :, 2 * HEAD_DIM :] = jnp.where(lane < LANES // 2, fixed[:half], fixed[half:]).astype(jnp.int16)


def to_wire(acc, block_max, total):
    reach = jnp.maximum(jnp.max(fold(jnp.abs(acc), jnp.maximum), axis=1, keepdims=True), 1e-30)
    data = jnp.round(acc * (TOP / reach)).astype(jnp.int32).astype(jnp.int16)
    lane = lax.broadcasted_iota(jnp.int32, block_max.shape, 1) % (LANES // 2)
    log_total = jnp.log(total) * POINTS[1]
    log_reach = jnp.log(reach) * POINTS[2]
    value = jnp.where(lane < 2, block_max * POINTS[0], jnp.where(lane < 4, log_total, log_reach))
    value = jnp.round(value).astype(jnp.int32)
    return data, jnp.where(lane % 2 == 0, value >> 16, (value & 0xFFFF) - 0x8000)


def from_wire(stats, first, i):
    high = stats[:, first + 2 * i : first + 2 * i + 1]
    low = stats[:, first + 2 * i + 1 : first + 2 * i + 2] + 0x8000
    return ((high << 16) + low).astype(jnp.float32) * (1.0 / POINTS[i])


def pair_kernel(own_ref, other_ref, out_ref):
    slots, half, lanes = own_ref.shape
    rows = slots * half
    own_stats = own_ref[:, :, 2 * HEAD_DIM :].reshape(rows, LANES)
    other_stats = other_ref[:, :, 2 * HEAD_DIM :].reshape(rows, LANES).astype(jnp.int32)
    fixed = []
    for part in range(2):
        first = part * LANES // 2
        span = slice(part * HEAD_DIM, (part + 1) * HEAD_DIM)
        own_max, own_total = own_stats[:, first : first + 1], own_stats[:, first + 1 : first + 2]
        other_max = from_wire(other_stats, first, 0)
        top = jnp.maximum(own_max, other_max)
        own_scale = jnp.exp(own_max - top)
        shift = other_max - top
        total = own_total * own_scale + jnp.exp(shift + from_wire(other_stats, first, 1))
        other = other_ref[:, :, span].reshape(rows, HEAD_DIM).astype(jnp.int32).astype(jnp.float32)
        acc = own_ref[:, :, span].reshape(rows, HEAD_DIM) * own_scale
        acc = acc + other * (jnp.exp(shift + from_wire(other_stats, first, 2)) * (1.0 / TOP))
        shape = (rows, LANES)
        data, stats = to_wire(acc, jnp.broadcast_to(top, shape), jnp.broadcast_to(total, shape))
        out_ref[:, :, span] = data.reshape(slots, half, HEAD_DIM)
        fixed.append(stats)
    lane = lax.broadcasted_iota(jnp.int32, (rows, LANES), 1)
    stats = jnp.where(lane < LANES // 2, fixed[0], fixed[1]).astype(jnp.int16)
    out_ref[:, :, 2 * HEAD_DIM :] = stats.reshape(slots, half, LANES)


def merge_kernel(parts_ref, out_ref):
    blocks, half, _ = parts_ref.shape
    leaf_count = out_ref.shape[0]
    stats = [parts_ref[b, :, 2 * HEAD_DIM :].astype(jnp.int32) for b in range(blocks)]
    for part in range(2):
        first = part * LANES // 2
        tops = [from_wire(stats[b], first, 0) for b in range(blocks)]
        row_max = functools.reduce(jnp.maximum, tops)
        denominator = jnp.zeros((half, 1), jnp.float32)
        numerator = jnp.zeros((half, HEAD_DIM), jnp.float32)
        for b in range(blocks):
            shift = tops[b] - row_max
            denominator = denominator + jnp.exp(shift + from_wire(stats[b], first, 1))
            data = parts_ref[b, :, part * HEAD_DIM : (part + 1) * HEAD_DIM].astype(jnp.int32).astype(jnp.float32)
            numerator = numerator + jnp.exp(shift + from_wire(stats[b], first, 2)) * data
        merged = (numerator / (denominator * TOP)).astype(jnp.bfloat16)
        for i in range(half // leaf_count):
            out_ref[:, part * half // leaf_count + i, :] = merged[i * leaf_count : (i + 1) * leaf_count]


def gather_shared(own, owners, early):
    first = [[x + z + k for k in range(0, Z, STRIDE)] for x in range(0, owners, Z) for z in range(STRIDE)]
    second = [[x + z + k for x in range(0, owners, Z) for k in range(STRIDE)] for z in range(0, Z, STRIDE)]
    part = lax.all_to_all(own, "leaf", 0, 0, tiled=True, axis_index_groups=first)
    parts = pl.pallas_call(
        copies_kernel,
        out_shape=jax.ShapeDtypeStruct((len(second[0]),) + part.shape, part.dtype),
        in_specs=[VMEM, VMEM],
        out_specs=VMEM,
        compiler_params=params(8),
    )(part, early)
    shared = lax.all_to_all(parts, "leaf", 0, 0, tiled=True, axis_index_groups=second)
    return shared.reshape((owners,) + own.shape[1:])


def shards(queries, prompt_kv, node_kv, node_lengths, ancestors):
    leaf_count, steps, feat_width = queries.shape
    node_slots, tokens = node_kv.shape[1:3]
    prompt_cols = prompt_kv.shape[1]
    width = KV_HEADS * HEAD_DIM
    rows = steps * leaf_count
    owners = lax.axis_size("leaf")

    own = pl.pallas_call(
        post_kernel,
        out_shape=pltpu.VMEM((Z // STRIDE, 2 * tokens, width), jnp.bfloat16),
        in_specs=[HBM, HBM],
        out_specs=VMEM,
        scratch_shapes=[
            pltpu.VMEM((2, tokens, width), jnp.bfloat16),
            pltpu.SMEM((node_slots,), jnp.int32),
            pltpu.SemaphoreType.DMA((2,)),
        ],
        compiler_params=params(8),
    )(*in_hbm(node_lengths, node_kv))
    query_rows = queries.transpose(1, 0, 2).reshape(rows, feat_width)
    early_cols = prompt_cols + node_slots * tokens
    assert prompt_cols % CHUNK == 0 and node_slots * tokens == CHUNK and GROUP * rows == CHUNK
    early, halves, count = pl.pallas_call(
        functools.partial(early_kernel, steps),
        out_shape=(
            jax.ShapeDtypeStruct((KV_HEADS, early_cols // CHUNK + 1, CHUNK, CHUNK), jnp.float32),
            jax.ShapeDtypeStruct((early_cols + GROUP * rows, width), jnp.bfloat16),
            jax.ShapeDtypeStruct((leaf_count, owners * tokens), jnp.float32),
        ),
        in_specs=[HBM, HBM, HBM, HBM, VMEM],
        out_specs=(VMEM,) * 3,
        scratch_shapes=[
            pltpu.SMEM((node_slots,), jnp.int32),
            pltpu.VMEM(ancestors.shape, jnp.int32),
            pltpu.VMEM((prompt_cols, width), jnp.bfloat16),
            pltpu.VMEM((node_slots, tokens, width), jnp.bfloat16),
            pltpu.SemaphoreType.DMA((5 + node_slots,)),
        ],
        compiler_params=params(16),
        cost_estimate=pl.CostEstimate(flops=500_000_000, bytes_accessed=6_000_000, transcendentals=800_000),
    )(*in_hbm(node_lengths, ancestors, prompt_kv, node_kv), query_rows)

    shared = gather_shared(own, owners, count)
    seqs = lax.axis_size("seq")
    wire = jax.ShapeDtypeStruct((HEADS // 2, rows // 2, 2 * HEAD_DIM + LANES), jnp.int16)
    kept, sent = pl.pallas_call(
        late_kernel,
        out_shape=(jax.ShapeDtypeStruct(wire.shape, jnp.float32), wire),
        in_specs=[VMEM] * 4,
        out_specs=(VMEM, VMEM),
        compiler_params=params(16),
    )(shared, early, halves, count)

    got = lax.ppermute(sent, "seq", [(i, i ^ 1) for i in range(seqs)])
    parts = pl.pallas_call(
        pair_kernel,
        out_shape=wire,
        in_specs=[VMEM, VMEM],
        out_specs=VMEM,
        compiler_params=params(8),
    )(kept, got)
    chips = [list(range(c, seqs, 2)) for c in range(2)]
    parts = lax.all_to_all(parts, "seq", 0, 0, tiled=True, axis_index_groups=chips)
    return pl.pallas_call(
        merge_kernel,
        out_shape=jax.ShapeDtypeStruct((leaf_count, steps, HEAD_DIM), jnp.bfloat16),
        in_specs=[VMEM],
        out_specs=VMEM,
        compiler_params=params(8),
    )(parts)


def solution(mesh):
    placed = (
        P("leaf", None, None),
        P(None, "seq", None),
        P(None, "leaf", "seq", None),
        P("leaf"),
        P("leaf", None),
    )
    return jax.shard_map(
        shards, mesh=mesh, in_specs=placed, out_specs=P("leaf", None, "seq"), check_vma=False
    )
```

```python
import functools

import jax
import jax.numpy as jnp
from jax import lax
from jax.experimental import pallas as pl
from jax.experimental.pallas import tpu as pltpu
from jax.sharding import PartitionSpec as P

HEADS = 16
KV_HEADS = 2
HEAD_DIM = 256
GROUP = HEADS // KV_HEADS
CHUNK = 256
LANES = 128
Z = 8
STRIDE = 2
INVALID_KEY = 256.0
TOP = 32767.0
POINTS = (2.0**18, 2.0**26, 2.0**23)

VMEM = pl.BlockSpec(memory_space=pltpu.VMEM)
HBM = pl.BlockSpec(memory_space=pltpu.HBM)


def in_hbm(*arrays):
    return [pltpu.with_memory_space_constraint(array, pltpu.HBM) for array in arrays]


def params(mib):
    return pltpu.CompilerParams(vmem_limit_bytes=mib * 1024 * 1024)


def fold(x, combine):
    parts = [x[:, i : i + LANES] for i in range(0, x.shape[1], LANES)]
    return functools.reduce(combine, parts)


def tall(x, reps):
    return jnp.concatenate([x] * reps, axis=0)


def node_counts(anc, ids, levels):
    counts = jnp.zeros((anc.shape[0], ids.shape[1]), jnp.float32)
    for level in levels:
        counts = counts + jnp.where(anc[:, level : level + 1] == ids, 1.0, 0.0)
    return counts


def group_query(q_ref, k):
    heads = range(k * GROUP, (k + 1) * GROUP)
    query = jnp.concatenate([q_ref[:, h * HEAD_DIM : (h + 1) * HEAD_DIM] for h in heads], axis=0)
    return query * jnp.bfloat16(1.0 / 16.0)


def dot_nt(a, b):
    return lax.dot_general(a, b, (((1,), (1,)), ((), ())), preferred_element_type=jnp.float32)


def fetch(pairs, sems):
    copies = [pltpu.make_async_copy(src, dst, sems.at[i]) for i, (src, dst) in enumerate(pairs)]
    for copy in copies:
        copy.start()
    return copies


def post_kernel(lengths_hbm, node_hbm, out_ref, node_ref, lengths_ref, sems):
    node_slots = lengths_hbm.shape[0]
    tokens = node_ref.shape[1]
    for copy in fetch([(node_hbm.at[:, node_slots - 1], node_ref), (lengths_hbm, lengths_ref)], sems):
        copy.wait()
    present = lax.axis_index("seq") * tokens < lengths_ref[node_slots - 1]
    keys = jnp.where(present, node_ref[0], jnp.bfloat16(INVALID_KEY))
    values = node_ref[1]
    for copy in range(out_ref.shape[0]):
        out_ref[copy, 0:tokens] = keys
        out_ref[copy, tokens : 2 * tokens] = values


def copies_kernel(plane_ref, early_ref, out_ref):
    del early_ref
    for copy in range(out_ref.shape[0]):
        out_ref[copy] = plane_ref[...]


def early_kernel(
    steps,
    lengths_hbm,
    anc_hbm,
    prompt_hbm,
    node_hbm,
    q_ref,
    w_ref,
    row_ref,
    half_ref,
    count_ref,
    lengths_ref,
    anc_ref,
    prompt_ref,
    node_ref,
    sems,
):
    copies = fetch(
        [
            (lengths_hbm, lengths_ref),
            (anc_hbm, anc_ref),
            (node_hbm.at[0], node_ref),
            (prompt_hbm.at[0], prompt_ref),
            (prompt_hbm.at[1], half_ref.at[pl.ds(0, prompt_ref.shape[0])]),
        ]
        + [
            (node_hbm.at[1, n], half_ref.at[pl.ds(prompt_ref.shape[0] + n * node_ref.shape[1], node_ref.shape[1])])
            for n in range(node_ref.shape[0])
        ],
        sems,
    )
    leaf_count, level_count = anc_ref.shape
    node_slots, tokens, width = node_ref.shape
    node_cols = node_slots * tokens
    prompt_cols = prompt_ref.shape[0]
    shared_cols = count_ref.shape[1]
    for k in range(KV_HEADS):
        half_ref[prompt_cols + node_cols :, k * HEAD_DIM : (k + 1) * HEAD_DIM] = group_query(q_ref, k)
    copies[0].wait()
    copies[1].wait()
    anc = anc_ref[...]

    lane = lax.broadcasted_iota(jnp.int32, (1, shared_cols), 1)
    block = lane // tokens
    owner = block // Z * Z + block % (Z // STRIDE) * STRIDE + block // (Z // STRIDE) % STRIDE
    count = node_counts(anc, owner * node_slots + node_slots - 1, range(level_count - 1))
    count_ref[...] = jnp.where(owner == lax.axis_index("leaf"), 0.0, count)

    lane = lax.broadcasted_iota(jnp.int32, (1, node_cols), 1)
    slot = lane // tokens
    position = lax.axis_index("seq") * tokens + lane % tokens
    length = jnp.zeros((1, node_cols), jnp.int32)
    for n in range(node_slots):
        length = jnp.where(slot == n, lengths_ref[n], length)
    ids = lax.axis_index("leaf") * node_slots + slot
    upper = node_counts(anc, ids, range(level_count - 1))
    own = node_counts(anc, ids, [level_count - 1])
    mult = []
    for step in range(steps):
        causal = jnp.where(position <= length - steps + step, 1.0, 0.0)
        mult.append(jnp.where(position < length, upper + own * causal, 0.0))
    mult = tall(jnp.concatenate(mult, axis=0), GROUP)
    copies[2].wait()
    copies[3].wait()

    for k in range(KV_HEADS):
        cols = slice(k * HEAD_DIM, (k + 1) * HEAD_DIM)
        query = half_ref[prompt_cols + node_cols :, cols]
        top = None
        for start in range(0, prompt_cols, CHUNK):
            s = dot_nt(query, prompt_ref[start : start + CHUNK, cols])
            w_ref[k, start // CHUNK] = s
            part = fold(s, jnp.maximum)
            top = part if top is None else jnp.maximum(top, part)
        s = dot_nt(query, node_ref[:, :, cols].reshape(node_cols, HEAD_DIM))
        s = jnp.where(mult > 0.0, s, -jnp.inf)
        w_ref[k, prompt_cols // CHUNK] = s
        top = jnp.max(jnp.maximum(top, fold(s, jnp.maximum)), axis=1, keepdims=True)
        total = jnp.zeros((s.shape[0], LANES), jnp.float32)
        for start in range(0, prompt_cols, CHUNK):
            w = jnp.exp(w_ref[k, start // CHUNK] - top)
            w_ref[k, start // CHUNK] = w
            total = total + fold(w, jnp.add)
        w = jnp.exp(w_ref[k, prompt_cols // CHUNK] - top) * mult
        w_ref[k, prompt_cols // CHUNK] = w
        total = total + fold(w, jnp.add)
        row_ref[k, :, LANES:] = jnp.broadcast_to(jnp.sum(total, axis=1, keepdims=True), total.shape)
        row_ref[k, :, :LANES] = jnp.broadcast_to(top, total.shape)
    for copy in copies[4:]:
        copy.wait()


def late_kernel(shared_ref, w_ref, row_ref, half_ref, count_ref, own_ref, out_ref):
    owners = shared_ref.shape[0]
    tokens = shared_ref.shape[1] // 2
    shared_cols = owners * tokens
    rows = w_ref.shape[2] // GROUP
    half = rows // 2
    chunks = w_ref.shape[1]
    early_cols = chunks * CHUNK
    count = count_ref[...]
    reps = GROUP * rows // count.shape[0]
    pick = jnp.where(lax.broadcasted_iota(jnp.int32, (8, HEAD_DIM), 1) == 0, 1.0, 0.0).astype(jnp.bfloat16)

    for k in range(KV_HEADS):
        cols = slice(k * HEAD_DIM, (k + 1) * HEAD_DIM)
        keys = shared_ref[:, 0:tokens, cols].reshape(shared_cols, HEAD_DIM)
        values = shared_ref[:, tokens : 2 * tokens, cols].reshape(shared_cols, HEAD_DIM)
        marks = dot_nt(pick, keys)[0:1]
        mult = tall(jnp.where(marks < INVALID_KEY / 2, count, 0.0), reps)
        s = dot_nt(half_ref[early_cols:, cols], keys)
        s = jnp.where(mult > 0.0, s, -jnp.inf)
        early_max = row_ref[k, :, :LANES]
        block_max = jnp.maximum(jnp.max(fold(s, jnp.maximum), axis=1, keepdims=True), early_max)
        scale = jnp.exp(early_max - block_max)
        w = jnp.exp(s - block_max[:, 0:1]) * mult
        total = jnp.sum(fold(w, jnp.add), axis=1, keepdims=True) + row_ref[k, :, LANES:] * scale
        acc = jnp.dot(w.astype(jnp.bfloat16), values, preferred_element_type=jnp.float32)
        wide = jnp.concatenate([scale, scale], axis=1)
        for c in range(chunks):
            w = (w_ref[k, c] * wide).astype(jnp.bfloat16)
            acc = acc + jnp.dot(w, half_ref[c * CHUNK : (c + 1) * CHUNK, cols], preferred_element_type=jnp.float32)

        core = lax.rem(lax.axis_index("seq"), 2)
        total = jnp.broadcast_to(total, block_max.shape)
        for pair in range(GROUP // 2):
            kept, sent = [], []
            for x in (acc, block_max, total):
                even = x[2 * pair * rows : (2 * pair + 1) * rows]
                odd = x[(2 * pair + 1) * rows : (2 * pair + 2) * rows]
                kept.append(jnp.where(core == 0, even, odd))
                sent.append(jnp.where(core == 0, odd, even))
            slot = k * (GROUP // 2) + pair
            lane = lax.broadcasted_iota(jnp.int32, (half, LANES), 1)
            stats = [jnp.where(lane % (LANES // 2) == 0, kept[1][i : i + half], kept[2][i : i + half]) for i in (0, half)]
            own_ref[slot, :, 2 * HEAD_DIM :] = jnp.where(lane < LANES // 2, stats[0], stats[1])
            own_ref[slot, :, 0:HEAD_DIM] = kept[0][:half]
            own_ref[slot, :, HEAD_DIM : 2 * HEAD_DIM] = kept[0][half:]
            data, fixed = to_wire(*sent)
            out_ref[slot, :, 0:HEAD_DIM] = data[:half]
            out_ref[slot, :, HEAD_DIM : 2 * HEAD_DIM] = data[half:]
            out_ref[slot, :, 2 * HEAD_DIM :] = jnp.where(lane < LANES // 2, fixed[:half], fixed[half:]).astype(jnp.int16)


def to_wire(acc, block_max, total):
    reach = jnp.maximum(jnp.max(fold(jnp.abs(acc), jnp.maximum), axis=1, keepdims=True), 1e-30)
    data = jnp.round(acc * (TOP / reach)).astype(jnp.int32).astype(jnp.int16)
    lane = lax.broadcasted_iota(jnp.int32, block_max.shape, 1) % (LANES // 2)
    log_total = jnp.log(total) * POINTS[1]
    log_reach = jnp.log(reach) * POINTS[2]
    value = jnp.where(lane < 2, block_max * POINTS[0], jnp.where(lane < 4, log_total, log_reach))
    value = jnp.round(value).astype(jnp.int32)
    return data, jnp.where(lane % 2 == 0, value >> 16, (value & 0xFFFF) - 0x8000)


def from_wire(stats, first, i):
    high = stats[:, first + 2 * i : first + 2 * i + 1]
    low = stats[:, first + 2 * i + 1 : first + 2 * i + 2] + 0x8000
    return ((high << 16) + low).astype(jnp.float32) * (1.0 / POINTS[i])


def pair_kernel(own_ref, other_ref, out_ref):
    slots, half, lanes = own_ref.shape
    rows = slots * half
    own_stats = own_ref[:, :, 2 * HEAD_DIM :].reshape(rows, LANES)
    other_stats = other_ref[:, :, 2 * HEAD_DIM :].reshape(rows, LANES).astype(jnp.int32)
    fixed = []
    for part in range(2):
        first = part * LANES // 2
        span = slice(part * HEAD_DIM, (part + 1) * HEAD_DIM)
        own_max, own_total = own_stats[:, first : first + 1], own_stats[:, first + 1 : first + 2]
        other_max = from_wire(other_stats, first, 0)
        top = jnp.maximum(own_max, other_max)
        own_scale = jnp.exp(own_max - top)
        shift = other_max - top
        total = own_total * own_scale + jnp.exp(shift + from_wire(other_stats, first, 1))
        other = other_ref[:, :, span].reshape(rows, HEAD_DIM).astype(jnp.int32).astype(jnp.float32)
        acc = own_ref[:, :, span].reshape(rows, HEAD_DIM) * own_scale
        acc = acc + other * (jnp.exp(shift + from_wire(other_stats, first, 2)) * (1.0 / TOP))
        shape = (rows, LANES)
        data, stats = to_wire(acc, jnp.broadcast_to(top, shape), jnp.broadcast_to(total, shape))
        out_ref[:, :, span] = data.reshape(slots, half, HEAD_DIM)
        fixed.append(stats)
    lane = lax.broadcasted_iota(jnp.int32, (rows, LANES), 1)
    stats = jnp.where(lane < LANES // 2, fixed[0], fixed[1]).astype(jnp.int16)
    out_ref[:, :, 2 * HEAD_DIM :] = stats.reshape(slots, half, LANES)


def merge_kernel(parts_ref, out_ref):
    blocks, half, _ = parts_ref.shape
    leaf_count = out_ref.shape[0]
    stats = [parts_ref[b, :, 2 * HEAD_DIM :].astype(jnp.int32) for b in range(blocks)]
    for part in range(2):
        first = part * LANES // 2
        tops = [from_wire(stats[b], first, 0) for b in range(blocks)]
        row_max = functools.reduce(jnp.maximum, tops)
        denominator = jnp.zeros((half, 1), jnp.float32)
        numerator = jnp.zeros((half, HEAD_DIM), jnp.float32)
        for b in range(blocks):
            shift = tops[b] - row_max
            denominator = denominator + jnp.exp(shift + from_wire(stats[b], first, 1))
            data = parts_ref[b, :, part * HEAD_DIM : (part + 1) * HEAD_DIM].astype(jnp.int32).astype(jnp.float32)
            numerator = numerator + jnp.exp(shift + from_wire(stats[b], first, 2)) * data
        merged = (numerator / (denominator * TOP)).astype(jnp.bfloat16)
        for i in range(half // leaf_count):
            out_ref[:, part * half // leaf_count + i, :] = merged[i * leaf_count : (i + 1) * leaf_count]


def gather_shared(own, owners, early):
    first = [[x + z + k for k in range(0, Z, STRIDE)] for x in range(0, owners, Z) for z in range(STRIDE)]
    second = [[x + z + k for x in range(0, owners, Z) for k in range(STRIDE)] for z in range(0, Z, STRIDE)]
    part = lax.all_to_all(own, "leaf", 0, 0, tiled=True, axis_index_groups=first)
    parts = pl.pallas_call(
        copies_kernel,
        out_shape=jax.ShapeDtypeStruct((len(second[0]),) + part.shape, part.dtype),
        in_specs=[VMEM, VMEM],
        out_specs=VMEM,
        compiler_params=params(8),
    )(part, early)
    shared = lax.all_to_all(parts, "leaf", 0, 0, tiled=True, axis_index_groups=second)
    return shared.reshape((owners,) + own.shape[1:])


def shards(queries, prompt_kv, node_kv, node_lengths, ancestors):
    leaf_count, steps, feat_width = queries.shape
    node_slots, tokens = node_kv.shape[1:3]
    prompt_cols = prompt_kv.shape[1]
    width = KV_HEADS * HEAD_DIM
    rows = steps * leaf_count
    owners = lax.axis_size("leaf")

    own = pl.pallas_call(
        post_kernel,
        out_shape=jax.ShapeDtypeStruct((Z // STRIDE, 2 * tokens, width), jnp.bfloat16),
        in_specs=[HBM, HBM],
        out_specs=VMEM,
        scratch_shapes=[
            pltpu.VMEM((2, tokens, width), jnp.bfloat16),
            pltpu.SMEM((node_slots,), jnp.int32),
            pltpu.SemaphoreType.DMA((2,)),
        ],
        compiler_params=params(8),
    )(*in_hbm(node_lengths, node_kv))
    query_rows = queries.transpose(1, 0, 2).reshape(rows, feat_width)
    early_cols = prompt_cols + node_slots * tokens
    assert prompt_cols % CHUNK == 0 and node_slots * tokens == CHUNK and GROUP * rows == CHUNK
    early, early_rows, halves, count = pl.pallas_call(
        functools.partial(early_kernel, steps),
        out_shape=(
            jax.ShapeDtypeStruct((KV_HEADS, early_cols // CHUNK, CHUNK, CHUNK), jnp.float32),
            jax.ShapeDtypeStruct((KV_HEADS, GROUP * rows, 2 * LANES), jnp.float32),
            jax.ShapeDtypeStruct((early_cols + GROUP * rows, width), jnp.bfloat16),
            jax.ShapeDtypeStruct((leaf_count, owners * tokens), jnp.float32),
        ),
        in_specs=[HBM, HBM, HBM, HBM, VMEM],
        out_specs=(VMEM,) * 4,
        scratch_shapes=[
            pltpu.SMEM((node_slots,), jnp.int32),
            pltpu.VMEM(ancestors.shape, jnp.int32),
            pltpu.VMEM((prompt_cols, width), jnp.bfloat16),
            pltpu.VMEM((node_slots, tokens, width), jnp.bfloat16),
            pltpu.SemaphoreType.DMA((5 + node_slots,)),
        ],
        compiler_params=params(16),
        cost_estimate=pl.CostEstimate(flops=500_000_000, bytes_accessed=6_000_000, transcendentals=800_000),
    )(*in_hbm(node_lengths, ancestors, prompt_kv, node_kv), query_rows)

    shared = gather_shared(own, owners, count)
    seqs = lax.axis_size("seq")
    wire = jax.ShapeDtypeStruct((HEADS // 2, rows // 2, 2 * HEAD_DIM + LANES), jnp.int16)
    kept, sent = pl.pallas_call(
        late_kernel,
        out_shape=(jax.ShapeDtypeStruct(wire.shape, jnp.float32), wire),
        in_specs=[VMEM] * 5,
        out_specs=(VMEM, VMEM),
        compiler_params=params(16),
    )(shared, early, early_rows, halves, count)

    got = lax.ppermute(sent, "seq", [(i, i ^ 1) for i in range(seqs)])
    parts = pl.pallas_call(
        pair_kernel,
        out_shape=wire,
        in_specs=[VMEM, VMEM],
        out_specs=VMEM,
        compiler_params=params(8),
    )(kept, got)
    chips = [list(range(c, seqs, 2)) for c in range(2)]
    parts = lax.all_to_all(parts, "seq", 0, 0, tiled=True, axis_index_groups=chips)
    return pl.pallas_call(
        merge_kernel,
        out_shape=jax.ShapeDtypeStruct((leaf_count, steps, HEAD_DIM), jnp.bfloat16),
        in_specs=[VMEM],
        out_specs=VMEM,
        compiler_params=params(8),
    )(parts)


def solution(mesh):
    placed = (
        P("leaf", None, None),
        P(None, "seq", None),
        P(None, "leaf", "seq", None),
        P("leaf"),
        P("leaf", None),
    )
    return jax.shard_map(
        shards, mesh=mesh, in_specs=placed, out_specs=P("leaf", None, "seq"), check_vma=False
    )
```

```python
import functools

import jax
import jax.numpy as jnp
from jax import lax
from jax.experimental import pallas as pl
from jax.experimental.pallas import tpu as pltpu
from jax.sharding import PartitionSpec as P

HEADS = 16
KV_HEADS = 2
HEAD_DIM = 256
GROUP = HEADS // KV_HEADS
CHUNK = 256
LANES = 128
Z = 8
STRIDE = 2
FIRST_Z, FIRST_X, FIRST_CHIP = 2, 2, 6
INVALID_KEY = 256.0
TOP = 32767.0
POINTS = (2.0**18, 2.0**26, 2.0**23)

VMEM = pl.BlockSpec(memory_space=pltpu.VMEM)
HBM = pl.BlockSpec(memory_space=pltpu.HBM)


def in_hbm(*arrays):
    return [pltpu.with_memory_space_constraint(array, pltpu.HBM) for array in arrays]


def params(mib):
    return pltpu.CompilerParams(vmem_limit_bytes=mib * 1024 * 1024)


def fold(x, combine):
    parts = [x[:, i : i + LANES] for i in range(0, x.shape[1], LANES)]
    return functools.reduce(combine, parts)


def tall(x, reps):
    return jnp.concatenate([x] * reps, axis=0)


def node_counts(anc, ids, levels):
    counts = jnp.zeros((anc.shape[0], ids.shape[1]), jnp.float32)
    for level in levels:
        counts = counts + jnp.where(anc[:, level : level + 1] == ids, 1.0, 0.0)
    return counts


def group_query(q_ref, k):
    heads = range(k * GROUP, (k + 1) * GROUP)
    query = jnp.concatenate([q_ref[:, h * HEAD_DIM : (h + 1) * HEAD_DIM] for h in heads], axis=0)
    return query * jnp.bfloat16(1.0 / 16.0)


def dot_nt(a, b):
    return lax.dot_general(a, b, (((1,), (1,)), ((), ())), preferred_element_type=jnp.float32)


def fetch(pairs, sems):
    copies = [pltpu.make_async_copy(src, dst, sems.at[i]) for i, (src, dst) in enumerate(pairs)]
    for copy in copies:
        copy.start()
    return copies


def post_kernel(lengths_hbm, node_hbm, out_ref, node_ref, lengths_ref, sems):
    node_slots = lengths_hbm.shape[0]
    tokens = node_ref.shape[1]
    for copy in fetch([(node_hbm.at[:, node_slots - 1], node_ref), (lengths_hbm, lengths_ref)], sems):
        copy.wait()
    present = lax.axis_index("seq") * tokens < lengths_ref[node_slots - 1]
    keys = jnp.where(present, node_ref[0], jnp.bfloat16(INVALID_KEY))
    values = node_ref[1]
    for copy in range(out_ref.shape[0]):
        out_ref[copy, 0:tokens] = keys
        out_ref[copy, tokens : 2 * tokens] = values


def copies_kernel(plane_ref, early_ref, out_ref):
    del early_ref
    for copy in range(out_ref.shape[0]):
        out_ref[copy] = plane_ref[...]


def early_kernel(
    steps,
    lengths_hbm,
    anc_hbm,
    prompt_hbm,
    node_hbm,
    q_ref,
    w_ref,
    row_ref,
    half_ref,
    count_ref,
    lengths_ref,
    anc_ref,
    prompt_ref,
    node_ref,
    sems,
):
    copies = fetch(
        [
            (lengths_hbm, lengths_ref),
            (anc_hbm, anc_ref),
            (node_hbm.at[0], node_ref),
            (prompt_hbm.at[0], prompt_ref),
            (prompt_hbm.at[1], half_ref.at[pl.ds(0, prompt_ref.shape[0])]),
        ]
        + [
            (node_hbm.at[1, n], half_ref.at[pl.ds(prompt_ref.shape[0] + n * node_ref.shape[1], node_ref.shape[1])])
            for n in range(node_ref.shape[0])
        ],
        sems,
    )
    leaf_count, level_count = anc_ref.shape
    node_slots, tokens, width = node_ref.shape
    node_cols = node_slots * tokens
    prompt_cols = prompt_ref.shape[0]
    shared_cols = count_ref.shape[1]
    for k in range(KV_HEADS):
        half_ref[prompt_cols + node_cols :, k * HEAD_DIM : (k + 1) * HEAD_DIM] = group_query(q_ref, k)
    copies[0].wait()
    copies[1].wait()
    anc = anc_ref[...]

    lane = lax.broadcasted_iota(jnp.int32, (1, shared_cols), 1)
    owner = owner_of(lane // tokens, shared_cols // tokens)
    count = node_counts(anc, owner * node_slots + node_slots - 1, range(level_count - 1))
    count_ref[...] = jnp.where(owner == lax.axis_index("leaf"), 0.0, count)

    lane = lax.broadcasted_iota(jnp.int32, (1, node_cols), 1)
    slot = lane // tokens
    position = lax.axis_index("seq") * tokens + lane % tokens
    length = jnp.zeros((1, node_cols), jnp.int32)
    for n in range(node_slots):
        length = jnp.where(slot == n, lengths_ref[n], length)
    ids = lax.axis_index("leaf") * node_slots + slot
    upper = node_counts(anc, ids, range(level_count - 1))
    own = node_counts(anc, ids, [level_count - 1])
    mult = []
    for step in range(steps):
        causal = jnp.where(position <= length - steps + step, 1.0, 0.0)
        mult.append(jnp.where(position < length, upper + own * causal, 0.0))
    mult = tall(jnp.concatenate(mult, axis=0), GROUP)
    copies[2].wait()
    copies[3].wait()

    for k in range(KV_HEADS):
        cols = slice(k * HEAD_DIM, (k + 1) * HEAD_DIM)
        query = half_ref[prompt_cols + node_cols :, cols]
        top = None
        for start in range(0, prompt_cols, CHUNK):
            s = dot_nt(query, prompt_ref[start : start + CHUNK, cols])
            w_ref[k, start // CHUNK] = s
            part = fold(s, jnp.maximum)
            top = part if top is None else jnp.maximum(top, part)
        s = dot_nt(query, node_ref[:, :, cols].reshape(node_cols, HEAD_DIM))
        s = jnp.where(mult > 0.0, s, -jnp.inf)
        w_ref[k, prompt_cols // CHUNK] = s
        top = jnp.max(jnp.maximum(top, fold(s, jnp.maximum)), axis=1, keepdims=True)
        total = jnp.zeros((s.shape[0], LANES), jnp.float32)
        for start in range(0, prompt_cols, CHUNK):
            w = jnp.exp(w_ref[k, start // CHUNK] - top)
            w_ref[k, start // CHUNK] = w
            total = total + fold(w, jnp.add)
        w = jnp.exp(w_ref[k, prompt_cols // CHUNK] - top) * mult
        w_ref[k, prompt_cols // CHUNK] = w
        total = total + fold(w, jnp.add)
        row_ref[k, :, LANES:] = jnp.broadcast_to(jnp.sum(total, axis=1, keepdims=True), total.shape)
        row_ref[k, :, :LANES] = jnp.broadcast_to(top, total.shape)
    for copy in copies[4:]:
        copy.wait()


def late_kernel(shared_ref, w_ref, row_ref, half_ref, count_ref, own_ref, out_ref):
    owners = shared_ref.shape[0]
    tokens = shared_ref.shape[1] // 2
    shared_cols = owners * tokens
    rows = w_ref.shape[2] // GROUP
    half = rows // 2
    chunks = w_ref.shape[1]
    early_cols = chunks * CHUNK
    count = count_ref[...]
    reps = GROUP * rows // count.shape[0]
    pick = jnp.where(lax.broadcasted_iota(jnp.int32, (8, HEAD_DIM), 1) == 0, 1.0, 0.0).astype(jnp.bfloat16)

    for k in range(KV_HEADS):
        cols = slice(k * HEAD_DIM, (k + 1) * HEAD_DIM)
        keys = shared_ref[:, 0:tokens, cols].reshape(shared_cols, HEAD_DIM)
        values = shared_ref[:, tokens : 2 * tokens, cols].reshape(shared_cols, HEAD_DIM)
        marks = dot_nt(pick, keys)[0:1]
        mult = tall(jnp.where(marks < INVALID_KEY / 2, count, 0.0), reps)
        s = dot_nt(half_ref[early_cols:, cols], keys)
        s = jnp.where(mult > 0.0, s, -jnp.inf)
        early_max = row_ref[k, :, :LANES]
        block_max = jnp.maximum(jnp.max(fold(s, jnp.maximum), axis=1, keepdims=True), early_max)
        scale = jnp.exp(early_max - block_max)
        w = jnp.exp(s - block_max[:, 0:1]) * mult
        total = jnp.sum(fold(w, jnp.add), axis=1, keepdims=True) + row_ref[k, :, LANES:] * scale
        acc = jnp.dot(w.astype(jnp.bfloat16), values, preferred_element_type=jnp.float32)
        wide = jnp.concatenate([scale, scale], axis=1)
        for c in range(chunks):
            w = (w_ref[k, c] * wide).astype(jnp.bfloat16)
            acc = acc + jnp.dot(w, half_ref[c * CHUNK : (c + 1) * CHUNK, cols], preferred_element_type=jnp.float32)

        core = lax.rem(lax.axis_index("seq"), 2)
        total = jnp.broadcast_to(total, block_max.shape)
        for pair in range(GROUP // 2):
            kept, sent = [], []
            for x in (acc, block_max, total):
                even = x[2 * pair * rows : (2 * pair + 1) * rows]
                odd = x[(2 * pair + 1) * rows : (2 * pair + 2) * rows]
                kept.append(jnp.where(core == 0, even, odd))
                sent.append(jnp.where(core == 0, odd, even))
            slot = (k * (GROUP // 2) + pair - FIRST_CHIP) % (HEADS // 2)
            lane = lax.broadcasted_iota(jnp.int32, (half, LANES), 1)
            stats = [jnp.where(lane % (LANES // 2) == 0, kept[1][i : i + half], kept[2][i : i + half]) for i in (0, half)]
            own_ref[slot, :, 2 * HEAD_DIM :] = jnp.where(lane < LANES // 2, stats[0], stats[1])
            own_ref[slot, :, 0:HEAD_DIM] = kept[0][:half]
            own_ref[slot, :, HEAD_DIM : 2 * HEAD_DIM] = kept[0][half:]
            data, fixed = to_wire(*sent)
            out_ref[slot, :, 0:HEAD_DIM] = data[:half]
            out_ref[slot, :, HEAD_DIM : 2 * HEAD_DIM] = data[half:]
            out_ref[slot, :, 2 * HEAD_DIM :] = jnp.where(lane < LANES // 2, fixed[:half], fixed[half:]).astype(jnp.int16)


def to_wire(acc, block_max, total):
    reach = jnp.maximum(jnp.max(fold(jnp.abs(acc), jnp.maximum), axis=1, keepdims=True), 1e-30)
    data = jnp.round(acc * (TOP / reach)).astype(jnp.int32).astype(jnp.int16)
    lane = lax.broadcasted_iota(jnp.int32, block_max.shape, 1) % (LANES // 2)
    log_total = jnp.log(total) * POINTS[1]
    log_reach = jnp.log(reach) * POINTS[2]
    value = jnp.where(lane < 2, block_max * POINTS[0], jnp.where(lane < 4, log_total, log_reach))
    value = jnp.round(value).astype(jnp.int32)
    return data, jnp.where(lane % 2 == 0, value >> 16, (value & 0xFFFF) - 0x8000)


def from_wire(stats, first, i):
    high = stats[:, first + 2 * i : first + 2 * i + 1]
    low = stats[:, first + 2 * i + 1 : first + 2 * i + 2] + 0x8000
    return ((high << 16) + low).astype(jnp.float32) * (1.0 / POINTS[i])


def pair_kernel(own_ref, other_ref, out_ref):
    slots, half, lanes = own_ref.shape
    rows = slots * half
    own_stats = own_ref[:, :, 2 * HEAD_DIM :].reshape(rows, LANES)
    other_stats = other_ref[:, :, 2 * HEAD_DIM :].reshape(rows, LANES).astype(jnp.int32)
    fixed = []
    for part in range(2):
        first = part * LANES // 2
        span = slice(part * HEAD_DIM, (part + 1) * HEAD_DIM)
        own_max, own_total = own_stats[:, first : first + 1], own_stats[:, first + 1 : first + 2]
        other_max = from_wire(other_stats, first, 0)
        top = jnp.maximum(own_max, other_max)
        own_scale = jnp.exp(own_max - top)
        shift = other_max - top
        total = own_total * own_scale + jnp.exp(shift + from_wire(other_stats, first, 1))
        other = other_ref[:, :, span].reshape(rows, HEAD_DIM).astype(jnp.int32).astype(jnp.float32)
        acc = own_ref[:, :, span].reshape(rows, HEAD_DIM) * own_scale
        acc = acc + other * (jnp.exp(shift + from_wire(other_stats, first, 2)) * (1.0 / TOP))
        shape = (rows, LANES)
        data, stats = to_wire(acc, jnp.broadcast_to(top, shape), jnp.broadcast_to(total, shape))
        out_ref[:, :, span] = data.reshape(slots, half, HEAD_DIM)
        fixed.append(stats)
    lane = lax.broadcasted_iota(jnp.int32, (rows, LANES), 1)
    stats = jnp.where(lane < LANES // 2, fixed[0], fixed[1]).astype(jnp.int16)
    out_ref[:, :, 2 * HEAD_DIM :] = stats.reshape(slots, half, LANES)


def merge_kernel(parts_ref, out_ref):
    blocks, half, _ = parts_ref.shape
    leaf_count = out_ref.shape[0]
    stats = [parts_ref[b, :, 2 * HEAD_DIM :].astype(jnp.int32) for b in range(blocks)]
    for part in range(2):
        first = part * LANES // 2
        tops = [from_wire(stats[b], first, 0) for b in range(blocks)]
        row_max = functools.reduce(jnp.maximum, tops)
        denominator = jnp.zeros((half, 1), jnp.float32)
        numerator = jnp.zeros((half, HEAD_DIM), jnp.float32)
        for b in range(blocks):
            shift = tops[b] - row_max
            denominator = denominator + jnp.exp(shift + from_wire(stats[b], first, 1))
            data = parts_ref[b, :, part * HEAD_DIM : (part + 1) * HEAD_DIM].astype(jnp.int32).astype(jnp.float32)
            numerator = numerator + jnp.exp(shift + from_wire(stats[b], first, 2)) * data
        merged = (numerator / (denominator * TOP)).astype(jnp.bfloat16)
        for i in range(half // leaf_count):
            out_ref[:, part * half // leaf_count + i, :] = merged[i * leaf_count : (i + 1) * leaf_count]


def turned(items, start):
    items = list(items)
    return items[start:] + items[:start]


def gather_orders(owners):
    return turned(range(0, Z, STRIDE), FIRST_Z), turned(range(0, owners, Z), FIRST_X)


def owner_of(block, owners):
    along_z, along_x = gather_orders(owners)
    owner = block // (Z // STRIDE) % STRIDE
    for i, z in enumerate(along_z):
        owner = owner + jnp.where(block % (Z // STRIDE) == i, z, 0)
    for i, x in enumerate(along_x):
        owner = owner + jnp.where(block // Z == i, x, 0)
    return owner


def gather_shared(own, owners, early):
    along_z, along_x = gather_orders(owners)
    first = [[x + z + k for k in along_z] for x in range(0, owners, Z) for z in range(STRIDE)]
    second = [[x + z + k for x in along_x for k in range(STRIDE)] for z in range(0, Z, STRIDE)]
    part = lax.all_to_all(own, "leaf", 0, 0, tiled=True, axis_index_groups=first)
    parts = pl.pallas_call(
        copies_kernel,
        out_shape=jax.ShapeDtypeStruct((len(second[0]),) + part.shape, part.dtype),
        in_specs=[VMEM, VMEM],
        out_specs=VMEM,
        compiler_params=params(8),
    )(part, early)
    shared = lax.all_to_all(parts, "leaf", 0, 0, tiled=True, axis_index_groups=second)
    return shared.reshape((owners,) + own.shape[1:])


def shards(queries, prompt_kv, node_kv, node_lengths, ancestors):
    leaf_count, steps, feat_width = queries.shape
    node_slots, tokens = node_kv.shape[1:3]
    prompt_cols = prompt_kv.shape[1]
    width = KV_HEADS * HEAD_DIM
    rows = steps * leaf_count
    owners = lax.axis_size("leaf")

    own = pl.pallas_call(
        post_kernel,
        out_shape=jax.ShapeDtypeStruct((Z // STRIDE, 2 * tokens, width), jnp.bfloat16),
        in_specs=[HBM, HBM],
        out_specs=VMEM,
        scratch_shapes=[
            pltpu.VMEM((2, tokens, width), jnp.bfloat16),
            pltpu.SMEM((node_slots,), jnp.int32),
            pltpu.SemaphoreType.DMA((2,)),
        ],
        compiler_params=params(8),
    )(*in_hbm(node_lengths, node_kv))
    query_rows = queries.transpose(1, 0, 2).reshape(rows, feat_width)
    early_cols = prompt_cols + node_slots * tokens
    assert prompt_cols % CHUNK == 0 and node_slots * tokens == CHUNK and GROUP * rows == CHUNK
    early, early_rows, halves, count = pl.pallas_call(
        functools.partial(early_kernel, steps),
        out_shape=(
            jax.ShapeDtypeStruct((KV_HEADS, early_cols // CHUNK, CHUNK, CHUNK), jnp.float32),
            jax.ShapeDtypeStruct((KV_HEADS, GROUP * rows, 2 * LANES), jnp.float32),
            jax.ShapeDtypeStruct((early_cols + GROUP * rows, width), jnp.bfloat16),
            jax.ShapeDtypeStruct((leaf_count, owners * tokens), jnp.float32),
        ),
        in_specs=[HBM, HBM, HBM, HBM, VMEM],
        out_specs=(VMEM,) * 4,
        scratch_shapes=[
            pltpu.SMEM((node_slots,), jnp.int32),
            pltpu.VMEM(ancestors.shape, jnp.int32),
            pltpu.VMEM((prompt_cols, width), jnp.bfloat16),
            pltpu.VMEM((node_slots, tokens, width), jnp.bfloat16),
            pltpu.SemaphoreType.DMA((5 + node_slots,)),
        ],
        compiler_params=params(16),
        cost_estimate=pl.CostEstimate(flops=500_000_000, bytes_accessed=6_000_000, transcendentals=800_000),
    )(*in_hbm(node_lengths, ancestors, prompt_kv, node_kv), query_rows)

    shared = gather_shared(own, owners, count)
    seqs = lax.axis_size("seq")
    wire = jax.ShapeDtypeStruct((HEADS // 2, rows // 2, 2 * HEAD_DIM + LANES), jnp.int16)
    kept, sent = pl.pallas_call(
        late_kernel,
        out_shape=(jax.ShapeDtypeStruct(wire.shape, jnp.float32), wire),
        in_specs=[VMEM] * 5,
        out_specs=(VMEM, VMEM),
        compiler_params=params(16),
    )(shared, early, early_rows, halves, count)

    got = lax.ppermute(sent, "seq", [(i, i ^ 1) for i in range(seqs)])
    parts = pl.pallas_call(
        pair_kernel,
        out_shape=wire,
        in_specs=[VMEM, VMEM],
        out_specs=VMEM,
        compiler_params=params(8),
    )(kept, got)
    chips = [turned(range(c, seqs, 2), FIRST_CHIP) for c in range(2)]
    parts = lax.all_to_all(parts, "seq", 0, 0, tiled=True, axis_index_groups=chips)
    return pl.pallas_call(
        merge_kernel,
        out_shape=jax.ShapeDtypeStruct((leaf_count, steps, HEAD_DIM), jnp.bfloat16),
        in_specs=[VMEM],
        out_specs=VMEM,
        compiler_params=params(8),
    )(parts)


def solution(mesh):
    placed = (
        P("leaf", None, None),
        P(None, "seq", None),
        P(None, "leaf", "seq", None),
        P("leaf"),
        P("leaf", None),
    )
    return jax.shard_map(
        shards, mesh=mesh, in_specs=placed, out_specs=P("leaf", None, "seq"), check_vma=False
    )
```

```python
import functools

import jax
import jax.numpy as jnp
from jax import lax
from jax.experimental import pallas as pl
from jax.experimental.pallas import tpu as pltpu
from jax.sharding import PartitionSpec as P

HEADS = 16
KV_HEADS = 2
HEAD_DIM = 256
GROUP = HEADS // KV_HEADS
CHUNK = 256
LANES = 128
Z = 8
STRIDE = 2
FIRST_Z, FIRST_X, FIRST_CHIP = 2, 2, 6
WAITING_Z = 4
INVALID_KEY = 256.0
TOP = 32767.0
POINTS = (2.0**18, 2.0**26, 2.0**23)

VMEM = pl.BlockSpec(memory_space=pltpu.VMEM)
HBM = pl.BlockSpec(memory_space=pltpu.HBM)


def in_hbm(*arrays):
    return [pltpu.with_memory_space_constraint(array, pltpu.HBM) for array in arrays]


def params(mib):
    return pltpu.CompilerParams(vmem_limit_bytes=mib * 1024 * 1024)


def fold(x, combine):
    parts = [x[:, i : i + LANES] for i in range(0, x.shape[1], LANES)]
    return functools.reduce(combine, parts)


def tall(x, reps):
    return jnp.concatenate([x] * reps, axis=0)


def node_counts(anc, ids, levels):
    counts = jnp.zeros((anc.shape[0], ids.shape[1]), jnp.float32)
    for level in levels:
        counts = counts + jnp.where(anc[:, level : level + 1] == ids, 1.0, 0.0)
    return counts


def group_query(q_ref, k):
    heads = range(k * GROUP, (k + 1) * GROUP)
    pieces = [q_ref[:, step, h * HEAD_DIM : (h + 1) * HEAD_DIM] for h in heads for step in range(q_ref.shape[1])]
    return (jnp.concatenate(pieces, axis=0) * (1.0 / 16.0)).astype(jnp.bfloat16)


def dot_nt(a, b):
    return lax.dot_general(a, b, (((1,), (1,)), ((), ())), preferred_element_type=jnp.float32)


def fetch(pairs, sems):
    copies = [pltpu.make_async_copy(src, dst, sems.at[i]) for i, (src, dst) in enumerate(pairs)]
    for copy in copies:
        copy.start()
    return copies


def waits():
    return lax.rem(lax.axis_index("leaf"), Z) < WAITING_Z


def first_kernel(inputs, outputs, scratch):
    lengths_hbm, node_hbm = inputs[0], inputs[3]
    out_ref, (node_ref, lengths_ref, sems) = outputs[0], scratch[:3]
    node_slots = lengths_hbm.shape[0]
    tokens = node_ref.shape[1]
    for copy in fetch([(node_hbm.at[:, node_slots - 1], node_ref), (lengths_hbm, lengths_ref)], sems):
        copy.wait()
    present = lax.axis_index("seq") * tokens < lengths_ref[node_slots - 1]
    keys = jnp.where(present, node_ref[0], jnp.bfloat16(INVALID_KEY))
    values = node_ref[1]
    for copy in range(out_ref.shape[0]):
        out_ref[copy, 0:tokens] = keys
        out_ref[copy, tokens : 2 * tokens] = values

    @pl.when(waits())
    def _():
        early_work(*inputs, *outputs[1:], *scratch[3:])


def second_kernel(inputs, outputs, scratch):
    part_ref, out_ref = inputs[0], outputs[0]
    for copy in range(out_ref.shape[0]):
        out_ref[copy] = part_ref[...]

    @pl.when(jnp.logical_not(waits()))
    def _():
        early_work(*inputs[1:], *outputs[1:], *scratch)


def early_work(
    lengths_hbm,
    anc_hbm,
    prompt_hbm,
    node_hbm,
    q_hbm,
    w_ref,
    row_ref,
    half_ref,
    count_ref,
    lengths_ref,
    anc_ref,
    prompt_ref,
    node_ref,
    q_raw_ref,
    q_ref,
    sems,
):
    copies = fetch(
        [
            (lengths_hbm, lengths_ref),
            (anc_hbm, anc_ref),
            (q_hbm, q_raw_ref),
            (node_hbm.at[0], node_ref),
            (prompt_hbm.at[0], prompt_ref),
            (prompt_hbm.at[1], half_ref.at[pl.ds(0, prompt_ref.shape[0])]),
        ]
        + [
            (node_hbm.at[1, n], half_ref.at[pl.ds(prompt_ref.shape[0] + n * node_ref.shape[1], node_ref.shape[1])])
            for n in range(node_ref.shape[0])
        ],
        sems,
    )
    level_count = anc_ref.shape[1]
    steps = q_ref.shape[1]
    node_slots, tokens, width = node_ref.shape
    node_cols = node_slots * tokens
    prompt_cols = prompt_ref.shape[0]
    shared_cols = count_ref.shape[1]
    copies[2].wait()
    q_ref[...] = q_raw_ref[...].astype(jnp.float32)
    for k in range(KV_HEADS):
        half_ref[prompt_cols + node_cols :, k * HEAD_DIM : (k + 1) * HEAD_DIM] = group_query(q_ref, k)
    copies[0].wait()
    copies[1].wait()
    anc = anc_ref[...]

    lane = lax.broadcasted_iota(jnp.int32, (1, shared_cols), 1)
    owner = owner_of(lane // tokens, shared_cols // tokens)
    count = node_counts(anc, owner * node_slots + node_slots - 1, range(level_count - 1))
    count_ref[...] = jnp.where(owner == lax.axis_index("leaf"), 0.0, count)

    lane = lax.broadcasted_iota(jnp.int32, (1, node_cols), 1)
    slot = lane // tokens
    position = lax.axis_index("seq") * tokens + lane % tokens
    length = jnp.zeros((1, node_cols), jnp.int32)
    for n in range(node_slots):
        length = jnp.where(slot == n, lengths_ref[n], length)
    ids = lax.axis_index("leaf") * node_slots + slot
    upper = node_counts(anc, ids, range(level_count - 1))
    own = node_counts(anc, ids, [level_count - 1])
    mult = []
    for step in range(steps):
        causal = jnp.where(position <= length - steps + step, 1.0, 0.0)
        mult.append(jnp.where(position < length, upper + own * causal, 0.0))
    mult = tall(jnp.concatenate(mult, axis=0), GROUP)
    copies[3].wait()
    copies[4].wait()

    for k in range(KV_HEADS):
        cols = slice(k * HEAD_DIM, (k + 1) * HEAD_DIM)
        query = half_ref[prompt_cols + node_cols :, cols]
        top = None
        for start in range(0, prompt_cols, CHUNK):
            s = dot_nt(query, prompt_ref[start : start + CHUNK, cols])
            w_ref[k, start // CHUNK] = s
            part = fold(s, jnp.maximum)
            top = part if top is None else jnp.maximum(top, part)
        s = dot_nt(query, node_ref[:, :, cols].reshape(node_cols, HEAD_DIM))
        s = jnp.where(mult > 0.0, s, -jnp.inf)
        w_ref[k, prompt_cols // CHUNK] = s
        top = jnp.max(jnp.maximum(top, fold(s, jnp.maximum)), axis=1, keepdims=True)
        total = jnp.zeros((s.shape[0], LANES), jnp.float32)
        for start in range(0, prompt_cols, CHUNK):
            w = jnp.exp(w_ref[k, start // CHUNK] - top)
            w_ref[k, start // CHUNK] = w
            total = total + fold(w, jnp.add)
        w = jnp.exp(w_ref[k, prompt_cols // CHUNK] - top) * mult
        w_ref[k, prompt_cols // CHUNK] = w
        total = total + fold(w, jnp.add)
        row_ref[k, :, LANES:] = jnp.broadcast_to(jnp.sum(total, axis=1, keepdims=True), total.shape)
        row_ref[k, :, :LANES] = jnp.broadcast_to(top, total.shape)
    for copy in copies[5:]:
        copy.wait()


def late_kernel(shared_ref, *refs):
    sets, outputs = (refs[:4], refs[4:8]), refs[8:]

    @pl.when(waits())
    def _():
        late_work(shared_ref, *sets[0], *outputs)

    @pl.when(jnp.logical_not(waits()))
    def _():
        late_work(shared_ref, *sets[1], *outputs)


def late_work(shared_ref, w_ref, row_ref, half_ref, count_ref, own_ref, out_ref):
    owners = shared_ref.shape[0]
    tokens = shared_ref.shape[1] // 2
    shared_cols = owners * tokens
    rows = w_ref.shape[2] // GROUP
    half = rows // 2
    chunks = w_ref.shape[1]
    early_cols = chunks * CHUNK
    count = count_ref[...]
    reps = GROUP * rows // count.shape[0]
    pick = jnp.where(lax.broadcasted_iota(jnp.int32, (8, HEAD_DIM), 1) == 0, 1.0, 0.0).astype(jnp.bfloat16)

    for k in range(KV_HEADS):
        cols = slice(k * HEAD_DIM, (k + 1) * HEAD_DIM)
        keys = shared_ref[:, 0:tokens, cols].reshape(shared_cols, HEAD_DIM)
        values = shared_ref[:, tokens : 2 * tokens, cols].reshape(shared_cols, HEAD_DIM)
        marks = dot_nt(pick, keys)[0:1]
        mult = tall(jnp.where(marks < INVALID_KEY / 2, count, 0.0), reps)
        s = dot_nt(half_ref[early_cols:, cols], keys)
        s = jnp.where(mult > 0.0, s, -jnp.inf)
        early_max = row_ref[k, :, :LANES]
        block_max = jnp.maximum(jnp.max(fold(s, jnp.maximum), axis=1, keepdims=True), early_max)
        scale = jnp.exp(early_max - block_max)
        w = jnp.exp(s - block_max[:, 0:1]) * mult
        total = jnp.sum(fold(w, jnp.add), axis=1, keepdims=True) + row_ref[k, :, LANES:] * scale
        acc = jnp.dot(w.astype(jnp.bfloat16), values, preferred_element_type=jnp.float32)
        wide = jnp.concatenate([scale, scale], axis=1)
        for c in range(chunks):
            w = (w_ref[k, c] * wide).astype(jnp.bfloat16)
            acc = acc + jnp.dot(w, half_ref[c * CHUNK : (c + 1) * CHUNK, cols], preferred_element_type=jnp.float32)

        core = lax.rem(lax.axis_index("seq"), 2)
        total = jnp.broadcast_to(total, block_max.shape)
        for pair in range(GROUP // 2):
            kept, sent = [], []
            for x in (acc, block_max, total):
                even = x[2 * pair * rows : (2 * pair + 1) * rows]
                odd = x[(2 * pair + 1) * rows : (2 * pair + 2) * rows]
                kept.append(jnp.where(core == 0, even, odd))
                sent.append(jnp.where(core == 0, odd, even))
            slot = (k * (GROUP // 2) + pair - FIRST_CHIP) % (HEADS // 2)
            lane = lax.broadcasted_iota(jnp.int32, (half, LANES), 1)
            stats = [jnp.where(lane % (LANES // 2) == 0, kept[1][i : i + half], kept[2][i : i + half]) for i in (0, half)]
            own_ref[slot, :, 2 * HEAD_DIM :] = jnp.where(lane < LANES // 2, stats[0], stats[1])
            own_ref[slot, :, 0:HEAD_DIM] = kept[0][:half]
            own_ref[slot, :, HEAD_DIM : 2 * HEAD_DIM] = kept[0][half:]
            data, fixed = to_wire(*sent)
            out_ref[slot, :, 0:HEAD_DIM] = data[:half]
            out_ref[slot, :, HEAD_DIM : 2 * HEAD_DIM] = data[half:]
            out_ref[slot, :, 2 * HEAD_DIM :] = jnp.where(lane < LANES // 2, fixed[:half], fixed[half:]).astype(jnp.int16)


def to_wire(acc, block_max, total):
    reach = jnp.maximum(jnp.max(fold(jnp.abs(acc), jnp.maximum), axis=1, keepdims=True), 1e-30)
    data = jnp.round(acc * (TOP / reach)).astype(jnp.int32).astype(jnp.int16)
    lane = lax.broadcasted_iota(jnp.int32, block_max.shape, 1) % (LANES // 2)
    log_total = jnp.log(total) * POINTS[1]
    log_reach = jnp.log(reach) * POINTS[2]
    value = jnp.where(lane < 2, block_max * POINTS[0], jnp.where(lane < 4, log_total, log_reach))
    value = jnp.round(value).astype(jnp.int32)
    return data, jnp.where(lane % 2 == 0, value >> 16, (value & 0xFFFF) - 0x8000)


def from_wire(stats, first, i):
    high = stats[:, first + 2 * i : first + 2 * i + 1]
    low = stats[:, first + 2 * i + 1 : first + 2 * i + 2] + 0x8000
    return ((high << 16) + low).astype(jnp.float32) * (1.0 / POINTS[i])


def pair_kernel(own_ref, other_ref, out_ref):
    slots, half, lanes = own_ref.shape
    rows = slots * half
    own_stats = own_ref[:, :, 2 * HEAD_DIM :].reshape(rows, LANES)
    other_stats = other_ref[:, :, 2 * HEAD_DIM :].reshape(rows, LANES).astype(jnp.int32)
    fixed = []
    for part in range(2):
        first = part * LANES // 2
        span = slice(part * HEAD_DIM, (part + 1) * HEAD_DIM)
        own_max, own_total = own_stats[:, first : first + 1], own_stats[:, first + 1 : first + 2]
        other_max = from_wire(other_stats, first, 0)
        top = jnp.maximum(own_max, other_max)
        own_scale = jnp.exp(own_max - top)
        shift = other_max - top
        total = own_total * own_scale + jnp.exp(shift + from_wire(other_stats, first, 1))
        other = other_ref[:, :, span].reshape(rows, HEAD_DIM).astype(jnp.int32).astype(jnp.float32)
        acc = own_ref[:, :, span].reshape(rows, HEAD_DIM) * own_scale
        acc = acc + other * (jnp.exp(shift + from_wire(other_stats, first, 2)) * (1.0 / TOP))
        shape = (rows, LANES)
        data, stats = to_wire(acc, jnp.broadcast_to(top, shape), jnp.broadcast_to(total, shape))
        out_ref[:, :, span] = data.reshape(slots, half, HEAD_DIM)
        fixed.append(stats)
    lane = lax.broadcasted_iota(jnp.int32, (rows, LANES), 1)
    stats = jnp.where(lane < LANES // 2, fixed[0], fixed[1]).astype(jnp.int16)
    out_ref[:, :, 2 * HEAD_DIM :] = stats.reshape(slots, half, LANES)


def merge_kernel(parts_ref, out_ref):
    blocks, half, _ = parts_ref.shape
    leaf_count = out_ref.shape[0]
    stats = [parts_ref[b, :, 2 * HEAD_DIM :].astype(jnp.int32) for b in range(blocks)]
    for part in range(2):
        first = part * LANES // 2
        tops = [from_wire(stats[b], first, 0) for b in range(blocks)]
        row_max = functools.reduce(jnp.maximum, tops)
        denominator = jnp.zeros((half, 1), jnp.float32)
        numerator = jnp.zeros((half, HEAD_DIM), jnp.float32)
        for b in range(blocks):
            shift = tops[b] - row_max
            denominator = denominator + jnp.exp(shift + from_wire(stats[b], first, 1))
            data = parts_ref[b, :, part * HEAD_DIM : (part + 1) * HEAD_DIM].astype(jnp.int32).astype(jnp.float32)
            numerator = numerator + jnp.exp(shift + from_wire(stats[b], first, 2)) * data
        merged = (numerator / (denominator * TOP)).astype(jnp.bfloat16)
        for i in range(half // leaf_count):
            out_ref[:, part * half // leaf_count + i, :] = merged[i * leaf_count : (i + 1) * leaf_count]


def turned(items, start):
    items = list(items)
    return items[start:] + items[:start]


def gather_orders(owners):
    return turned(range(0, Z, STRIDE), FIRST_Z), turned(range(0, owners, Z), FIRST_X)


def owner_of(block, owners):
    along_z, along_x = gather_orders(owners)
    owner = block // (Z // STRIDE) % STRIDE
    for i, z in enumerate(along_z):
        owner = owner + jnp.where(block % (Z // STRIDE) == i, z, 0)
    for i, x in enumerate(along_x):
        owner = owner + jnp.where(block // Z == i, x, 0)
    return owner


def gather_groups(owners):
    along_z, along_x = gather_orders(owners)
    first = [[x + z + k for k in along_z] for x in range(0, owners, Z) for z in range(STRIDE)]
    second = [[x + z + k for x in along_x for k in range(STRIDE)] for z in range(0, Z, STRIDE)]
    return first, second


def shards(queries, prompt_kv, node_kv, node_lengths, ancestors):
    leaf_count, steps, feat_width = queries.shape
    node_slots, tokens = node_kv.shape[1:3]
    prompt_cols = prompt_kv.shape[1]
    width = KV_HEADS * HEAD_DIM
    rows = steps * leaf_count
    owners = lax.axis_size("leaf")

    first, second = gather_groups(owners)
    early_cols = prompt_cols + node_slots * tokens
    assert prompt_cols % CHUNK == 0 and node_slots * tokens == CHUNK and GROUP * rows == CHUNK
    arrays = in_hbm(node_lengths, ancestors, prompt_kv, node_kv, queries)
    early_shapes = (
        jax.ShapeDtypeStruct((KV_HEADS, early_cols // CHUNK, CHUNK, CHUNK), jnp.float32),
        jax.ShapeDtypeStruct((KV_HEADS, GROUP * rows, 2 * LANES), jnp.float32),
        jax.ShapeDtypeStruct((early_cols + GROUP * rows, width), jnp.bfloat16),
        jax.ShapeDtypeStruct((leaf_count, owners * tokens), jnp.float32),
    )
    early_scratch = [
        pltpu.SMEM((node_slots,), jnp.int32),
        pltpu.VMEM(ancestors.shape, jnp.int32),
        pltpu.VMEM((prompt_cols, width), jnp.bfloat16),
        pltpu.VMEM((node_slots, tokens, width), jnp.bfloat16),
        pltpu.VMEM(queries.shape, jnp.bfloat16),
        pltpu.VMEM(queries.shape, jnp.float32),
        pltpu.SemaphoreType.DMA((6 + node_slots,)),
    ]

    def stage_kernel(body, out_shape, scratch, *operands):
        ins, outs = len(operands), 1 + len(early_shapes)

        def kernel(*refs):
            body(refs[:ins], refs[ins : ins + outs], refs[ins + outs :])

        return pl.pallas_call(
            kernel,
            out_shape=(out_shape, *early_shapes),
            in_specs=[VMEM] * (ins - len(arrays)) + [HBM] * len(arrays),
            out_specs=(VMEM,) * outs,
            scratch_shapes=scratch,
            compiler_params=params(24),
        )(*operands)

    own, *before = stage_kernel(
        first_kernel,
        jax.ShapeDtypeStruct((len(first[0]), 2 * tokens, width), jnp.bfloat16),
        [
            pltpu.VMEM((2, tokens, width), jnp.bfloat16),
            pltpu.SMEM((node_slots,), jnp.int32),
            pltpu.SemaphoreType.DMA((2,)),
            *early_scratch,
        ],
        *arrays,
    )
    part = lax.all_to_all(own, "leaf", 0, 0, tiled=True, axis_index_groups=first)
    part_copies, *after = stage_kernel(
        second_kernel,
        jax.ShapeDtypeStruct((len(second[0]),) + part.shape, part.dtype),
        early_scratch,
        part,
        *arrays,
    )
    shared = lax.all_to_all(part_copies, "leaf", 0, 0, tiled=True, axis_index_groups=second)
    shared = shared.reshape(owners, 2 * tokens, width)

    seqs = lax.axis_size("seq")
    wire = jax.ShapeDtypeStruct((HEADS // 2, rows // 2, 2 * HEAD_DIM + LANES), jnp.int16)
    kept, sent = pl.pallas_call(
        late_kernel,
        out_shape=(jax.ShapeDtypeStruct(wire.shape, jnp.float32), wire),
        in_specs=[VMEM] * 9,
        out_specs=(VMEM, VMEM),
        compiler_params=params(16),
    )(shared, *before, *after)

    got = lax.ppermute(sent, "seq", [(i, i ^ 1) for i in range(seqs)])
    parts = pl.pallas_call(
        pair_kernel,
        out_shape=wire,
        in_specs=[VMEM, VMEM],
        out_specs=VMEM,
        compiler_params=params(8),
    )(kept, got)
    chips = [turned(range(c, seqs, 2), FIRST_CHIP) for c in range(2)]
    parts = lax.all_to_all(parts, "seq", 0, 0, tiled=True, axis_index_groups=chips)
    return pl.pallas_call(
        merge_kernel,
        out_shape=jax.ShapeDtypeStruct((leaf_count, steps, HEAD_DIM), jnp.bfloat16),
        in_specs=[VMEM],
        out_specs=VMEM,
        compiler_params=params(8),
    )(parts)


def solution(mesh):
    placed = (
        P("leaf", None, None),
        P(None, "seq", None),
        P(None, "leaf", "seq", None),
        P("leaf"),
        P("leaf", None),
    )
    return jax.shard_map(
        shards, mesh=mesh, in_specs=placed, out_specs=P("leaf", None, "seq"), check_vma=False
    )
```

```python
import functools

import jax
import jax.numpy as jnp
from jax import lax
from jax.experimental import pallas as pl
from jax.experimental.pallas import tpu as pltpu
from jax.sharding import PartitionSpec as P

HEADS = 16
KV_HEADS = 2
HEAD_DIM = 256
GROUP = HEADS // KV_HEADS
CHUNK = 256
LANES = 128
Z = 8
STRIDE = 2
FIRST_Z, FIRST_X, FIRST_CHIP = 2, 2, 6
WAITING_Z = 4
INVALID_KEY = 256.0
TOP = 32767.0
STATS = 32
POINTS = (2.0**18, 2.0**26, 2.0**23)

VMEM = pl.BlockSpec(memory_space=pltpu.VMEM)
HBM = pl.BlockSpec(memory_space=pltpu.HBM)


def in_hbm(*arrays):
    return [pltpu.with_memory_space_constraint(array, pltpu.HBM) for array in arrays]


def params(mib):
    return pltpu.CompilerParams(vmem_limit_bytes=mib * 1024 * 1024)


def fold(x, combine):
    parts = [x[:, i : i + LANES] for i in range(0, x.shape[1], LANES)]
    return functools.reduce(combine, parts)


def tall(x, reps):
    return jnp.concatenate([x] * reps, axis=0)


def node_counts(anc, ids, levels):
    counts = jnp.zeros((anc.shape[0], ids.shape[1]), jnp.float32)
    for level in levels:
        counts = counts + jnp.where(anc[:, level : level + 1] == ids, 1.0, 0.0)
    return counts


def group_query(q_ref, k):
    heads = range(k * GROUP, (k + 1) * GROUP)
    pieces = [q_ref[:, step, h * HEAD_DIM : (h + 1) * HEAD_DIM] for h in heads for step in range(q_ref.shape[1])]
    return (jnp.concatenate(pieces, axis=0) * (1.0 / 16.0)).astype(jnp.bfloat16)


def dot_nt(a, b):
    return lax.dot_general(a, b, (((1,), (1,)), ((), ())), preferred_element_type=jnp.float32)


def fetch(pairs, sems):
    copies = [pltpu.make_async_copy(src, dst, sems.at[i]) for i, (src, dst) in enumerate(pairs)]
    for copy in copies:
        copy.start()
    return copies


def waits():
    return lax.rem(lax.axis_index("leaf"), Z) < WAITING_Z


def first_kernel(inputs, outputs, scratch):
    lengths_hbm, node_hbm = inputs[0], inputs[3]
    out_ref, (node_ref, lengths_ref, sems) = outputs[0], scratch[:3]
    node_slots = lengths_hbm.shape[0]
    tokens = node_ref.shape[1]
    for copy in fetch([(node_hbm.at[:, node_slots - 1], node_ref), (lengths_hbm, lengths_ref)], sems):
        copy.wait()
    present = lax.axis_index("seq") * tokens < lengths_ref[node_slots - 1]
    keys = jnp.where(present, node_ref[0], jnp.bfloat16(INVALID_KEY))
    values = node_ref[1]
    for copy in range(out_ref.shape[0]):
        out_ref[copy, 0:tokens] = keys
        out_ref[copy, tokens : 2 * tokens] = values

    @pl.when(waits())
    def _():
        early_work(*inputs, *outputs[1:], *scratch[3:])


def second_kernel(inputs, outputs, scratch):
    part_ref, out_ref = inputs[0], outputs[0]
    for copy in range(out_ref.shape[0]):
        out_ref[copy] = part_ref[...]

    @pl.when(jnp.logical_not(waits()))
    def _():
        early_work(*inputs[1:], *outputs[1:], *scratch)


def early_work(
    lengths_hbm,
    anc_hbm,
    prompt_hbm,
    node_hbm,
    q_hbm,
    w_ref,
    row_ref,
    half_ref,
    count_ref,
    lengths_ref,
    anc_ref,
    prompt_ref,
    node_ref,
    q_raw_ref,
    q_ref,
    sems,
):
    copies = fetch(
        [
            (lengths_hbm, lengths_ref),
            (anc_hbm, anc_ref),
            (q_hbm, q_raw_ref),
            (node_hbm.at[0], node_ref),
            (prompt_hbm.at[0], prompt_ref),
            (prompt_hbm.at[1], half_ref.at[pl.ds(0, prompt_ref.shape[0])]),
        ]
        + [
            (node_hbm.at[1, n], half_ref.at[pl.ds(prompt_ref.shape[0] + n * node_ref.shape[1], node_ref.shape[1])])
            for n in range(node_ref.shape[0])
        ],
        sems,
    )
    level_count = anc_ref.shape[1]
    steps = q_ref.shape[1]
    node_slots, tokens, width = node_ref.shape
    node_cols = node_slots * tokens
    prompt_cols = prompt_ref.shape[0]
    shared_cols = count_ref.shape[1]
    copies[2].wait()
    q_ref[...] = q_raw_ref[...].astype(jnp.float32)
    for k in range(KV_HEADS):
        half_ref[prompt_cols + node_cols :, k * HEAD_DIM : (k + 1) * HEAD_DIM] = group_query(q_ref, k)
    copies[0].wait()
    copies[1].wait()
    anc = anc_ref[...]

    lane = lax.broadcasted_iota(jnp.int32, (1, shared_cols), 1)
    owner = owner_of(lane // tokens, shared_cols // tokens)
    count = node_counts(anc, owner * node_slots + node_slots - 1, range(level_count - 1))
    count_ref[...] = jnp.where(owner == lax.axis_index("leaf"), 0.0, count)

    lane = lax.broadcasted_iota(jnp.int32, (1, node_cols), 1)
    slot = lane // tokens
    position = lax.axis_index("seq") * tokens + lane % tokens
    length = jnp.zeros((1, node_cols), jnp.int32)
    for n in range(node_slots):
        length = jnp.where(slot == n, lengths_ref[n], length)
    ids = lax.axis_index("leaf") * node_slots + slot
    upper = node_counts(anc, ids, range(level_count - 1))
    own = node_counts(anc, ids, [level_count - 1])
    mult = []
    for step in range(steps):
        causal = jnp.where(position <= length - steps + step, 1.0, 0.0)
        mult.append(jnp.where(position < length, upper + own * causal, 0.0))
    mult = tall(jnp.concatenate(mult, axis=0), GROUP)
    copies[3].wait()
    copies[4].wait()

    for k in range(KV_HEADS):
        cols = slice(k * HEAD_DIM, (k + 1) * HEAD_DIM)
        query = half_ref[prompt_cols + node_cols :, cols]
        top = None
        for start in range(0, prompt_cols, CHUNK):
            s = dot_nt(query, prompt_ref[start : start + CHUNK, cols])
            w_ref[k, start // CHUNK] = s
            part = fold(s, jnp.maximum)
            top = part if top is None else jnp.maximum(top, part)
        s = dot_nt(query, node_ref[:, :, cols].reshape(node_cols, HEAD_DIM))
        s = jnp.where(mult > 0.0, s, -jnp.inf)
        w_ref[k, prompt_cols // CHUNK] = s
        top = jnp.max(jnp.maximum(top, fold(s, jnp.maximum)), axis=1, keepdims=True)
        total = jnp.zeros((s.shape[0], LANES), jnp.float32)
        for start in range(0, prompt_cols, CHUNK):
            w = jnp.exp(w_ref[k, start // CHUNK] - top)
            w_ref[k, start // CHUNK] = w
            total = total + fold(w, jnp.add)
        w = jnp.exp(w_ref[k, prompt_cols // CHUNK] - top) * mult
        w_ref[k, prompt_cols // CHUNK] = w
        total = total + fold(w, jnp.add)
        row_ref[k, :, LANES:] = jnp.broadcast_to(jnp.sum(total, axis=1, keepdims=True), total.shape)
        row_ref[k, :, :LANES] = jnp.broadcast_to(top, total.shape)
    for copy in copies[5:]:
        copy.wait()


def late_kernel(shared_ref, *refs):
    sets, outputs = (refs[:4], refs[4:8]), refs[8:]

    @pl.when(waits())
    def _():
        late_work(shared_ref, *sets[0], *outputs)

    @pl.when(jnp.logical_not(waits()))
    def _():
        late_work(shared_ref, *sets[1], *outputs)


def late_work(shared_ref, w_ref, row_ref, half_ref, count_ref, own_ref, out_ref):
    owners = shared_ref.shape[0]
    tokens = shared_ref.shape[1] // 2
    shared_cols = owners * tokens
    rows = w_ref.shape[2] // GROUP
    steps = rows // count_ref.shape[0]
    leaf_count = rows // steps
    chunks = w_ref.shape[1]
    early_cols = chunks * CHUNK
    count = count_ref[...]
    reps = GROUP * rows // count.shape[0]
    pick = jnp.where(lax.broadcasted_iota(jnp.int32, (8, HEAD_DIM), 1) == 0, 1.0, 0.0).astype(jnp.bfloat16)

    for k in range(KV_HEADS):
        cols = slice(k * HEAD_DIM, (k + 1) * HEAD_DIM)
        keys = shared_ref[:, 0:tokens, cols].reshape(shared_cols, HEAD_DIM)
        values = shared_ref[:, tokens : 2 * tokens, cols].reshape(shared_cols, HEAD_DIM)
        marks = dot_nt(pick, keys)[0:1]
        mult = tall(jnp.where(marks < INVALID_KEY / 2, count, 0.0), reps)
        s = dot_nt(half_ref[early_cols:, cols], keys)
        s = jnp.where(mult > 0.0, s, -jnp.inf)
        early_max = row_ref[k, :, :LANES]
        block_max = jnp.maximum(jnp.max(fold(s, jnp.maximum), axis=1, keepdims=True), early_max)
        scale = jnp.exp(early_max - block_max)
        w = jnp.exp(s - block_max[:, 0:1]) * mult
        total = jnp.sum(fold(w, jnp.add), axis=1, keepdims=True) + row_ref[k, :, LANES:] * scale
        acc = jnp.dot(w.astype(jnp.bfloat16), values, preferred_element_type=jnp.float32)
        wide = jnp.concatenate([scale, scale], axis=1)
        for c in range(chunks):
            w = (w_ref[k, c] * wide).astype(jnp.bfloat16)
            acc = acc + jnp.dot(w, half_ref[c * CHUNK : (c + 1) * CHUNK, cols], preferred_element_type=jnp.float32)

        core = lax.rem(lax.axis_index("seq"), 2)
        total = jnp.broadcast_to(total, block_max.shape)
        for pair in range(GROUP // 2):
            kept, sent = [], []
            for x in (acc, block_max, total):
                even = x[2 * pair * rows : (2 * pair + 1) * rows]
                odd = x[(2 * pair + 1) * rows : (2 * pair + 2) * rows]
                kept.append(jnp.where(core == 0, even, odd))
                sent.append(jnp.where(core == 0, odd, even))
            slot = (k * (GROUP // 2) + pair - FIRST_CHIP) % (HEADS // 2)
            lane = lax.broadcasted_iota(jnp.int32, (rows, LANES), 1)
            data, fixed = to_wire(*sent)
            put(own_ref, slot, steps, kept[0], jnp.where(lane % STATS == 0, kept[1], kept[2]))
            put(out_ref, slot, steps, data, fixed)


def put(ref, slot, steps, data, stats):
    leaf_count = data.shape[0] // steps
    group = lax.broadcasted_iota(jnp.int32, (leaf_count, LANES), 1) // STATS
    joint = stats[:leaf_count]
    for step in range(steps):
        rows = slice(step * leaf_count, (step + 1) * leaf_count)
        ref[slot, :, step * HEAD_DIM : (step + 1) * HEAD_DIM] = data[rows]
        joint = jnp.where(group == step, stats[rows], joint)
    ref[slot, :, steps * HEAD_DIM :] = joint.astype(ref.dtype)


def to_wire(acc, block_max, total):
    reach = jnp.maximum(jnp.max(fold(jnp.abs(acc), jnp.maximum), axis=1, keepdims=True), 1e-30)
    data = jnp.round(acc * (TOP / reach)).astype(jnp.int32).astype(jnp.int16)
    lane = lax.broadcasted_iota(jnp.int32, block_max.shape, 1) % STATS
    log_total = jnp.log(total) * POINTS[1]
    log_reach = jnp.log(reach) * POINTS[2]
    value = jnp.where(lane < 2, block_max * POINTS[0], jnp.where(lane < 4, log_total, log_reach))
    value = jnp.round(value).astype(jnp.int32)
    return data, jnp.where(lane % 2 == 0, value >> 16, (value & 0xFFFF) - 0x8000)


def from_wire(stats):
    lane = lax.broadcasted_iota(jnp.int32, stats.shape, 1) % STATS
    unit = jnp.where(lane < 2, 1.0 / POINTS[0], jnp.where(lane < 4, 1.0 / POINTS[1], 1.0 / POINTS[2]))
    return ((stats << 16) + (pltpu.roll(stats, LANES - 1, 1) + 0x8000)).astype(jnp.float32) * unit


def factors(values, top):
    lane = lax.broadcasted_iota(jnp.int32, values.shape, 1) % STATS
    shift = values - top
    return jnp.exp(values + jnp.where(lane == 2, pltpu.roll(shift, 2, 1), pltpu.roll(shift, 4, 1)))


def pair_kernel(own_ref, other_ref, out_ref):
    slots, leaf_count, lanes = own_ref.shape
    steps = lanes // HEAD_DIM
    rows = slots * leaf_count
    shape = (rows, LANES)
    own = own_ref[:, :, steps * HEAD_DIM :].reshape(shape)
    other = from_wire(other_ref[:, :, steps * HEAD_DIM :].astype(jnp.int32).reshape(shape))
    top = jnp.maximum(own, other)
    own_scale = jnp.exp(own - top)
    other_scale = factors(other, top)
    total = own * pltpu.roll(own_scale, 2, 1) + other_scale
    group = lax.broadcasted_iota(jnp.int32, shape, 1) // STATS
    joint = jnp.zeros(shape, jnp.int32)
    for step in range(steps):
        first = step * STATS
        span = slice(step * HEAD_DIM, (step + 1) * HEAD_DIM)
        data = other_ref[:, :, span].astype(jnp.int32).reshape(rows, HEAD_DIM).astype(jnp.float32)
        acc = own_ref[:, :, span].reshape(rows, HEAD_DIM) * own_scale[:, first : first + 1]
        acc = acc + data * (other_scale[:, first + 4 : first + 5] * (1.0 / TOP))
        data, stats = to_wire(
            acc,
            jnp.broadcast_to(top[:, first : first + 1], shape),
            jnp.broadcast_to(total[:, first + 2 : first + 3], shape),
        )
        out_ref[:, :, span] = data.reshape(slots, leaf_count, HEAD_DIM)
        joint = jnp.where(group == step, stats, joint)
    out_ref[:, :, steps * HEAD_DIM :] = joint.astype(jnp.int16).reshape(slots, leaf_count, LANES)


def merge_kernel(parts_ref, out_ref):
    blocks = parts_ref.shape[0]
    steps = out_ref.shape[1]
    values = [from_wire(parts_ref[b, :, steps * HEAD_DIM :].astype(jnp.int32)) for b in range(blocks)]
    row_max = functools.reduce(jnp.maximum, values)
    scales = [factors(value, row_max) for value in values]
    denominator = functools.reduce(jnp.add, scales) * TOP
    for step in range(steps):
        first = step * STATS
        numerator = jnp.zeros((out_ref.shape[0], HEAD_DIM), jnp.float32)
        for b in range(blocks):
            data = parts_ref[b, :, step * HEAD_DIM : (step + 1) * HEAD_DIM].astype(jnp.int32).astype(jnp.float32)
            numerator = numerator + scales[b][:, first + 4 : first + 5] * data
        out_ref[:, step, :] = (numerator / denominator[:, first + 2 : first + 3]).astype(jnp.bfloat16)


def turned(items, start):
    items = list(items)
    return items[start:] + items[:start]


def gather_orders(owners):
    return turned(range(0, Z, STRIDE), FIRST_Z), turned(range(0, owners, Z), FIRST_X)


def owner_of(block, owners):
    along_z, along_x = gather_orders(owners)
    owner = block // (Z // STRIDE) % STRIDE
    for i, z in enumerate(along_z):
        owner = owner + jnp.where(block % (Z // STRIDE) == i, z, 0)
    for i, x in enumerate(along_x):
        owner = owner + jnp.where(block // Z == i, x, 0)
    return owner


def gather_groups(owners):
    along_z, along_x = gather_orders(owners)
    first = [[x + z + k for k in along_z] for x in range(0, owners, Z) for z in range(STRIDE)]
    second = [[x + z + k for x in along_x for k in range(STRIDE)] for z in range(0, Z, STRIDE)]
    return first, second


def shards(queries, prompt_kv, node_kv, node_lengths, ancestors):
    leaf_count, steps, feat_width = queries.shape
    node_slots, tokens = node_kv.shape[1:3]
    prompt_cols = prompt_kv.shape[1]
    width = KV_HEADS * HEAD_DIM
    rows = steps * leaf_count
    owners = lax.axis_size("leaf")

    first, second = gather_groups(owners)
    early_cols = prompt_cols + node_slots * tokens
    assert prompt_cols % CHUNK == 0 and node_slots * tokens == CHUNK and GROUP * rows == CHUNK
    arrays = in_hbm(node_lengths, ancestors, prompt_kv, node_kv, queries)
    early_shapes = (
        jax.ShapeDtypeStruct((KV_HEADS, early_cols // CHUNK, CHUNK, CHUNK), jnp.float32),
        jax.ShapeDtypeStruct((KV_HEADS, GROUP * rows, 2 * LANES), jnp.float32),
        jax.ShapeDtypeStruct((early_cols + GROUP * rows, width), jnp.bfloat16),
        jax.ShapeDtypeStruct((leaf_count, owners * tokens), jnp.float32),
    )
    early_scratch = [
        pltpu.SMEM((node_slots,), jnp.int32),
        pltpu.VMEM(ancestors.shape, jnp.int32),
        pltpu.VMEM((prompt_cols, width), jnp.bfloat16),
        pltpu.VMEM((node_slots, tokens, width), jnp.bfloat16),
        pltpu.VMEM(queries.shape, jnp.bfloat16),
        pltpu.VMEM(queries.shape, jnp.float32),
        pltpu.SemaphoreType.DMA((6 + node_slots,)),
    ]

    def stage_kernel(body, out_shape, scratch, *operands):
        ins, outs = len(operands), 1 + len(early_shapes)

        def kernel(*refs):
            body(refs[:ins], refs[ins : ins + outs], refs[ins + outs :])

        return pl.pallas_call(
            kernel,
            out_shape=(out_shape, *early_shapes),
            in_specs=[VMEM] * (ins - len(arrays)) + [HBM] * len(arrays),
            out_specs=(VMEM,) * outs,
            scratch_shapes=scratch,
            compiler_params=params(24),
        )(*operands)

    own, *before = stage_kernel(
        first_kernel,
        jax.ShapeDtypeStruct((len(first[0]), 2 * tokens, width), jnp.bfloat16),
        [
            pltpu.VMEM((2, tokens, width), jnp.bfloat16),
            pltpu.SMEM((node_slots,), jnp.int32),
            pltpu.SemaphoreType.DMA((2,)),
            *early_scratch,
        ],
        *arrays,
    )
    part = lax.all_to_all(own, "leaf", 0, 0, tiled=True, axis_index_groups=first)
    part_copies, *after = stage_kernel(
        second_kernel,
        jax.ShapeDtypeStruct((len(second[0]),) + part.shape, part.dtype),
        early_scratch,
        part,
        *arrays,
    )
    shared = lax.all_to_all(part_copies, "leaf", 0, 0, tiled=True, axis_index_groups=second)
    shared = shared.reshape(owners, 2 * tokens, width)

    seqs = lax.axis_size("seq")
    assert steps * STATS == LANES
    wire = jax.ShapeDtypeStruct((HEADS // 2, leaf_count, steps * HEAD_DIM + LANES), jnp.int16)
    kept, sent = pl.pallas_call(
        late_kernel,
        out_shape=(jax.ShapeDtypeStruct(wire.shape, jnp.float32), wire),
        in_specs=[VMEM] * 9,
        out_specs=(VMEM, VMEM),
        compiler_params=params(16),
    )(shared, *before, *after)

    got = lax.ppermute(sent, "seq", [(i, i ^ 1) for i in range(seqs)])
    parts = pl.pallas_call(
        pair_kernel,
        out_shape=wire,
        in_specs=[VMEM, VMEM],
        out_specs=VMEM,
        compiler_params=params(8),
    )(kept, got)
    chips = [turned(range(c, seqs, 2), FIRST_CHIP) for c in range(2)]
    parts = lax.all_to_all(parts, "seq", 0, 0, tiled=True, axis_index_groups=chips)
    return pl.pallas_call(
        merge_kernel,
        out_shape=jax.ShapeDtypeStruct((leaf_count, steps, HEAD_DIM), jnp.bfloat16),
        in_specs=[VMEM],
        out_specs=VMEM,
        compiler_params=params(8),
    )(parts)


def solution(mesh):
    placed = (
        P("leaf", None, None),
        P(None, "seq", None),
        P(None, "leaf", "seq", None),
        P("leaf"),
        P("leaf", None),
    )
    return jax.shard_map(
        shards, mesh=mesh, in_specs=placed, out_specs=P("leaf", None, "seq"), check_vma=False
    )
```

```python
import functools

import jax
import jax.numpy as jnp
from jax import lax
from jax.experimental import pallas as pl
from jax.experimental.pallas import tpu as pltpu
from jax.sharding import PartitionSpec as P

HEADS = 16
KV_HEADS = 2
HEAD_DIM = 256
GROUP = HEADS // KV_HEADS
CHUNK = 256
LANES = 128
Z = 8
STRIDE = 2
FIRST_Z, FIRST_X, FIRST_MEMBER = 2, 2, 1
CHIPS = [4, 3, 2, 1, 0, 7, 6, 5]
WAITING_Z = 4
INVALID_KEY = 256.0
TOP = 32767.0
STATS = 32
POINTS = (2.0**18, 2.0**26, 2.0**23)

VMEM = pl.BlockSpec(memory_space=pltpu.VMEM)
HBM = pl.BlockSpec(memory_space=pltpu.HBM)


def in_hbm(*arrays):
    return [pltpu.with_memory_space_constraint(array, pltpu.HBM) for array in arrays]


def params(mib):
    return pltpu.CompilerParams(vmem_limit_bytes=mib * 1024 * 1024)


def fold(x, combine):
    parts = [x[:, i : i + LANES] for i in range(0, x.shape[1], LANES)]
    return functools.reduce(combine, parts)


def tall(x, reps):
    return jnp.concatenate([x] * reps, axis=0)


def node_counts(anc, ids, levels):
    counts = jnp.zeros((anc.shape[0], ids.shape[1]), jnp.float32)
    for level in levels:
        counts = counts + jnp.where(anc[:, level : level + 1] == ids, 1.0, 0.0)
    return counts


def group_query(q_ref, k):
    heads = range(k * GROUP, (k + 1) * GROUP)
    pieces = [q_ref[:, step, h * HEAD_DIM : (h + 1) * HEAD_DIM] for h in heads for step in range(q_ref.shape[1])]
    return (jnp.concatenate(pieces, axis=0) * (1.0 / 16.0)).astype(jnp.bfloat16)


def dot_nt(a, b):
    return lax.dot_general(a, b, (((1,), (1,)), ((), ())), preferred_element_type=jnp.float32)


def fetch(pairs, sems):
    copies = [pltpu.make_async_copy(src, dst, sems.at[i]) for i, (src, dst) in enumerate(pairs)]
    for copy in copies:
        copy.start()
    return copies


def waits():
    return lax.rem(lax.axis_index("leaf"), Z) < WAITING_Z


def first_kernel(inputs, outputs, scratch):
    lengths_hbm, node_hbm = inputs[0], inputs[3]
    out_ref, (node_ref, lengths_ref, sems) = outputs[0], scratch[:3]
    node_slots = lengths_hbm.shape[0]
    tokens = node_ref.shape[1]
    for copy in fetch([(node_hbm.at[:, node_slots - 1], node_ref), (lengths_hbm, lengths_ref)], sems):
        copy.wait()
    present = lax.axis_index("seq") * tokens < lengths_ref[node_slots - 1]
    keys = jnp.where(present, node_ref[0], jnp.bfloat16(INVALID_KEY))
    values = node_ref[1]
    for copy in range(out_ref.shape[0]):
        out_ref[copy, 0:tokens] = keys
        out_ref[copy, tokens : 2 * tokens] = values

    @pl.when(waits())
    def _():
        early_work(*inputs, *outputs[1:], *scratch[3:])


def second_kernel(inputs, outputs, scratch):
    part_ref, out_ref = inputs[0], outputs[0]
    for copy in range(out_ref.shape[0]):
        out_ref[copy] = part_ref[...]

    @pl.when(jnp.logical_not(waits()))
    def _():
        early_work(*inputs[1:], *outputs[1:], *scratch)


def early_work(
    lengths_hbm,
    anc_hbm,
    prompt_hbm,
    node_hbm,
    q_hbm,
    w_ref,
    row_ref,
    half_ref,
    count_ref,
    lengths_ref,
    anc_ref,
    prompt_ref,
    node_ref,
    q_raw_ref,
    q_ref,
    sems,
):
    copies = fetch(
        [
            (lengths_hbm, lengths_ref),
            (anc_hbm, anc_ref),
            (q_hbm, q_raw_ref),
            (node_hbm.at[0], node_ref),
            (prompt_hbm.at[0], prompt_ref),
            (prompt_hbm.at[1], half_ref.at[pl.ds(0, prompt_ref.shape[0])]),
        ]
        + [
            (node_hbm.at[1, n], half_ref.at[pl.ds(prompt_ref.shape[0] + n * node_ref.shape[1], node_ref.shape[1])])
            for n in range(node_ref.shape[0])
        ],
        sems,
    )
    level_count = anc_ref.shape[1]
    steps = q_ref.shape[1]
    node_slots, tokens, width = node_ref.shape
    node_cols = node_slots * tokens
    prompt_cols = prompt_ref.shape[0]
    shared_cols = count_ref.shape[1]
    copies[2].wait()
    q_ref[...] = q_raw_ref[...].astype(jnp.float32)
    for k in range(KV_HEADS):
        half_ref[prompt_cols + node_cols :, k * HEAD_DIM : (k + 1) * HEAD_DIM] = group_query(q_ref, k)
    copies[0].wait()
    copies[1].wait()
    anc = anc_ref[...]

    lane = lax.broadcasted_iota(jnp.int32, (1, shared_cols), 1)
    owner = owner_of(lane // tokens, shared_cols // tokens)
    count = node_counts(anc, owner * node_slots + node_slots - 1, range(level_count - 1))
    count_ref[...] = jnp.where(owner == lax.axis_index("leaf"), 0.0, count)

    lane = lax.broadcasted_iota(jnp.int32, (1, node_cols), 1)
    slot = lane // tokens
    position = lax.axis_index("seq") * tokens + lane % tokens
    length = jnp.zeros((1, node_cols), jnp.int32)
    for n in range(node_slots):
        length = jnp.where(slot == n, lengths_ref[n], length)
    ids = lax.axis_index("leaf") * node_slots + slot
    upper = node_counts(anc, ids, range(level_count - 1))
    own = node_counts(anc, ids, [level_count - 1])
    mult = []
    for step in range(steps):
        causal = jnp.where(position <= length - steps + step, 1.0, 0.0)
        mult.append(jnp.where(position < length, upper + own * causal, 0.0))
    mult = tall(jnp.concatenate(mult, axis=0), GROUP)
    copies[3].wait()
    copies[4].wait()

    for k in range(KV_HEADS):
        cols = slice(k * HEAD_DIM, (k + 1) * HEAD_DIM)
        query = half_ref[prompt_cols + node_cols :, cols]
        top = None
        for start in range(0, prompt_cols, CHUNK):
            s = dot_nt(query, prompt_ref[start : start + CHUNK, cols])
            w_ref[k, start // CHUNK] = s
            part = fold(s, jnp.maximum)
            top = part if top is None else jnp.maximum(top, part)
        s = dot_nt(query, node_ref[:, :, cols].reshape(node_cols, HEAD_DIM))
        s = jnp.where(mult > 0.0, s, -jnp.inf)
        w_ref[k, prompt_cols // CHUNK] = s
        top = jnp.max(jnp.maximum(top, fold(s, jnp.maximum)), axis=1, keepdims=True)
        total = jnp.zeros((s.shape[0], LANES), jnp.float32)
        for start in range(0, prompt_cols, CHUNK):
            w = jnp.exp(w_ref[k, start // CHUNK] - top)
            w_ref[k, start // CHUNK] = w
            total = total + fold(w, jnp.add)
        w = jnp.exp(w_ref[k, prompt_cols // CHUNK] - top) * mult
        w_ref[k, prompt_cols // CHUNK] = w
        total = total + fold(w, jnp.add)
        row_ref[k, :, LANES:] = jnp.broadcast_to(jnp.sum(total, axis=1, keepdims=True), total.shape)
        row_ref[k, :, :LANES] = jnp.broadcast_to(top, total.shape)
    for copy in copies[5:]:
        copy.wait()


def late_kernel(shared_ref, *refs):
    sets, outputs = (refs[:4], refs[4:8]), refs[8:]

    @pl.when(waits())
    def _():
        late_work(shared_ref, *sets[0], *outputs)

    @pl.when(jnp.logical_not(waits()))
    def _():
        late_work(shared_ref, *sets[1], *outputs)


def late_work(shared_ref, w_ref, row_ref, half_ref, count_ref, own_ref, out_ref):
    owners = shared_ref.shape[0]
    tokens = shared_ref.shape[1] // 2
    shared_cols = owners * tokens
    rows = w_ref.shape[2] // GROUP
    steps = rows // count_ref.shape[0]
    leaf_count = rows // steps
    chunks = w_ref.shape[1]
    early_cols = chunks * CHUNK
    count = count_ref[...]
    reps = GROUP * rows // count.shape[0]
    pick = jnp.where(lax.broadcasted_iota(jnp.int32, (8, HEAD_DIM), 1) == 0, 1.0, 0.0).astype(jnp.bfloat16)

    for k in range(KV_HEADS):
        cols = slice(k * HEAD_DIM, (k + 1) * HEAD_DIM)
        keys = shared_ref[:, 0:tokens, cols].reshape(shared_cols, HEAD_DIM)
        values = shared_ref[:, tokens : 2 * tokens, cols].reshape(shared_cols, HEAD_DIM)
        marks = dot_nt(pick, keys)[0:1]
        mult = tall(jnp.where(marks < INVALID_KEY / 2, count, 0.0), reps)
        s = dot_nt(half_ref[early_cols:, cols], keys)
        s = jnp.where(mult > 0.0, s, -jnp.inf)
        early_max = row_ref[k, :, :LANES]
        block_max = jnp.maximum(jnp.max(fold(s, jnp.maximum), axis=1, keepdims=True), early_max)
        scale = jnp.exp(early_max - block_max)
        w = jnp.exp(s - block_max[:, 0:1]) * mult
        total = jnp.sum(fold(w, jnp.add), axis=1, keepdims=True) + row_ref[k, :, LANES:] * scale
        acc = jnp.dot(w.astype(jnp.bfloat16), values, preferred_element_type=jnp.float32)
        wide = jnp.concatenate([scale, scale], axis=1)
        for c in range(chunks):
            w = (w_ref[k, c] * wide).astype(jnp.bfloat16)
            acc = acc + jnp.dot(w, half_ref[c * CHUNK : (c + 1) * CHUNK, cols], preferred_element_type=jnp.float32)

        core = lax.rem(lax.axis_index("seq"), 2)
        total = jnp.broadcast_to(total, block_max.shape)
        for pair in range(GROUP // 2):
            kept, sent = [], []
            for x in (acc, block_max, total):
                even = x[2 * pair * rows : (2 * pair + 1) * rows]
                odd = x[(2 * pair + 1) * rows : (2 * pair + 2) * rows]
                kept.append(jnp.where(core == 0, even, odd))
                sent.append(jnp.where(core == 0, odd, even))
            slot = CHIPS.index(k * (GROUP // 2) + pair)
            lane = lax.broadcasted_iota(jnp.int32, (rows, LANES), 1)
            data, fixed = to_wire(*sent)
            put(own_ref, slot, steps, kept[0], jnp.where(lane % STATS == 0, kept[1], kept[2]))
            put(out_ref, slot, steps, data, fixed)


def put(ref, slot, steps, data, stats):
    leaf_count = data.shape[0] // steps
    group = lax.broadcasted_iota(jnp.int32, (leaf_count, LANES), 1) // STATS
    joint = stats[:leaf_count]
    for step in range(steps):
        rows = slice(step * leaf_count, (step + 1) * leaf_count)
        ref[slot, :, step * HEAD_DIM : (step + 1) * HEAD_DIM] = data[rows]
        joint = jnp.where(group == step, stats[rows], joint)
    ref[slot, :, steps * HEAD_DIM :] = joint.astype(ref.dtype)


def to_wire(acc, block_max, total):
    reach = jnp.maximum(jnp.max(fold(jnp.abs(acc), jnp.maximum), axis=1, keepdims=True), 1e-30)
    data = jnp.round(acc * (TOP / reach)).astype(jnp.int32).astype(jnp.int16)
    lane = lax.broadcasted_iota(jnp.int32, block_max.shape, 1) % STATS
    log_total = jnp.log(total) * POINTS[1]
    log_reach = jnp.log(reach) * POINTS[2]
    value = jnp.where(lane < 2, block_max * POINTS[0], jnp.where(lane < 4, log_total, log_reach))
    value = jnp.round(value).astype(jnp.int32)
    return data, jnp.where(lane % 2 == 0, value >> 16, (value & 0xFFFF) - 0x8000)


def from_wire(stats):
    lane = lax.broadcasted_iota(jnp.int32, stats.shape, 1) % STATS
    unit = jnp.where(lane < 2, 1.0 / POINTS[0], jnp.where(lane < 4, 1.0 / POINTS[1], 1.0 / POINTS[2]))
    return ((stats << 16) + (pltpu.roll(stats, LANES - 1, 1) + 0x8000)).astype(jnp.float32) * unit


def factors(values, top):
    lane = lax.broadcasted_iota(jnp.int32, values.shape, 1) % STATS
    shift = values - top
    return jnp.exp(values + jnp.where(lane == 2, pltpu.roll(shift, 2, 1), pltpu.roll(shift, 4, 1)))


def pair_kernel(own_ref, other_ref, out_ref):
    slots, leaf_count, lanes = own_ref.shape
    steps = lanes // HEAD_DIM
    rows = slots * leaf_count
    shape = (rows, LANES)
    own = own_ref[:, :, steps * HEAD_DIM :].reshape(shape)
    other = from_wire(other_ref[:, :, steps * HEAD_DIM :].astype(jnp.int32).reshape(shape))
    top = jnp.maximum(own, other)
    own_scale = jnp.exp(own - top)
    other_scale = factors(other, top)
    total = own * pltpu.roll(own_scale, 2, 1) + other_scale
    group = lax.broadcasted_iota(jnp.int32, shape, 1) // STATS
    joint = jnp.zeros(shape, jnp.int32)
    for step in range(steps):
        first = step * STATS
        span = slice(step * HEAD_DIM, (step + 1) * HEAD_DIM)
        data = other_ref[:, :, span].astype(jnp.int32).reshape(rows, HEAD_DIM).astype(jnp.float32)
        acc = own_ref[:, :, span].reshape(rows, HEAD_DIM) * own_scale[:, first : first + 1]
        acc = acc + data * (other_scale[:, first + 4 : first + 5] * (1.0 / TOP))
        data, stats = to_wire(
            acc,
            jnp.broadcast_to(top[:, first : first + 1], shape),
            jnp.broadcast_to(total[:, first + 2 : first + 3], shape),
        )
        out_ref[:, :, span] = data.reshape(slots, leaf_count, HEAD_DIM)
        joint = jnp.where(group == step, stats, joint)
    out_ref[:, :, steps * HEAD_DIM :] = joint.astype(jnp.int16).reshape(slots, leaf_count, LANES)


def merge_kernel(parts_ref, out_ref):
    blocks = parts_ref.shape[0]
    steps = out_ref.shape[1]
    values = [from_wire(parts_ref[b, :, steps * HEAD_DIM :].astype(jnp.int32)) for b in range(blocks)]
    row_max = functools.reduce(jnp.maximum, values)
    scales = [factors(value, row_max) for value in values]
    denominator = functools.reduce(jnp.add, scales) * TOP
    for step in range(steps):
        first = step * STATS
        numerator = jnp.zeros((out_ref.shape[0], HEAD_DIM), jnp.float32)
        for b in range(blocks):
            data = parts_ref[b, :, step * HEAD_DIM : (step + 1) * HEAD_DIM].astype(jnp.int32).astype(jnp.float32)
            numerator = numerator + scales[b][:, first + 4 : first + 5] * data
        out_ref[:, step, :] = (numerator / denominator[:, first + 2 : first + 3]).astype(jnp.bfloat16)


def turned(items, start):
    items = list(items)
    return items[start:] + items[:start]


def gather_orders(owners):
    return turned(range(0, Z, STRIDE), FIRST_Z), turned(range(0, owners, Z), FIRST_X)


def owner_of(block, owners):
    along_z, along_x = gather_orders(owners)
    owner = 0
    for i, z in enumerate(along_z):
        owner = owner + jnp.where(block % (Z // STRIDE) == i, z, 0)
    members = turned([x + k for x in along_x for k in range(STRIDE)], FIRST_MEMBER)
    for i, m in enumerate(members):
        owner = owner + jnp.where(block // (Z // STRIDE) == i, m, 0)
    return owner


def gather_groups(owners):
    along_z, along_x = gather_orders(owners)
    first = [[x + z + k for k in along_z] for x in range(0, owners, Z) for z in range(STRIDE)]
    members = [x + k for x in along_x for k in range(STRIDE)]
    members = turned(members, FIRST_MEMBER)
    second = [[m + z for m in members] for z in range(0, Z, STRIDE)]
    return first, second


def shards(queries, prompt_kv, node_kv, node_lengths, ancestors):
    leaf_count, steps, feat_width = queries.shape
    node_slots, tokens = node_kv.shape[1:3]
    prompt_cols = prompt_kv.shape[1]
    width = KV_HEADS * HEAD_DIM
    rows = steps * leaf_count
    owners = lax.axis_size("leaf")

    first, second = gather_groups(owners)
    early_cols = prompt_cols + node_slots * tokens
    assert prompt_cols % CHUNK == 0 and node_slots * tokens == CHUNK and GROUP * rows == CHUNK
    arrays = in_hbm(node_lengths, ancestors, prompt_kv, node_kv, queries)
    early_shapes = (
        jax.ShapeDtypeStruct((KV_HEADS, early_cols // CHUNK, CHUNK, CHUNK), jnp.float32),
        jax.ShapeDtypeStruct((KV_HEADS, GROUP * rows, 2 * LANES), jnp.float32),
        jax.ShapeDtypeStruct((early_cols + GROUP * rows, width), jnp.bfloat16),
        jax.ShapeDtypeStruct((leaf_count, owners * tokens), jnp.float32),
    )
    early_scratch = [
        pltpu.SMEM((node_slots,), jnp.int32),
        pltpu.VMEM(ancestors.shape, jnp.int32),
        pltpu.VMEM((prompt_cols, width), jnp.bfloat16),
        pltpu.VMEM((node_slots, tokens, width), jnp.bfloat16),
        pltpu.VMEM(queries.shape, jnp.bfloat16),
        pltpu.VMEM(queries.shape, jnp.float32),
        pltpu.SemaphoreType.DMA((6 + node_slots,)),
    ]

    def stage_kernel(body, out_shape, scratch, *operands):
        ins, outs = len(operands), 1 + len(early_shapes)

        def kernel(*refs):
            body(refs[:ins], refs[ins : ins + outs], refs[ins + outs :])

        return pl.pallas_call(
            kernel,
            out_shape=(out_shape, *early_shapes),
            in_specs=[VMEM] * (ins - len(arrays)) + [HBM] * len(arrays),
            out_specs=(VMEM,) * outs,
            scratch_shapes=scratch,
            compiler_params=params(24),
        )(*operands)

    own, *before = stage_kernel(
        first_kernel,
        jax.ShapeDtypeStruct((len(first[0]), 2 * tokens, width), jnp.bfloat16),
        [
            pltpu.VMEM((2, tokens, width), jnp.bfloat16),
            pltpu.SMEM((node_slots,), jnp.int32),
            pltpu.SemaphoreType.DMA((2,)),
            *early_scratch,
        ],
        *arrays,
    )
    part = lax.all_to_all(own, "leaf", 0, 0, tiled=True, axis_index_groups=first)
    part_copies, *after = stage_kernel(
        second_kernel,
        jax.ShapeDtypeStruct((len(second[0]),) + part.shape, part.dtype),
        early_scratch,
        part,
        *arrays,
    )
    shared = lax.all_to_all(part_copies, "leaf", 0, 0, tiled=True, axis_index_groups=second)
    shared = shared.reshape(owners, 2 * tokens, width)

    seqs = lax.axis_size("seq")
    assert steps * STATS == LANES
    wire = jax.ShapeDtypeStruct((HEADS // 2, leaf_count, steps * HEAD_DIM + LANES), jnp.int16)
    kept, sent = pl.pallas_call(
        late_kernel,
        out_shape=(jax.ShapeDtypeStruct(wire.shape, jnp.float32), wire),
        in_specs=[VMEM] * 9,
        out_specs=(VMEM, VMEM),
        compiler_params=params(16),
    )(shared, *before, *after)

    got = lax.ppermute(sent, "seq", [(i, i ^ 1) for i in range(seqs)])
    parts = pl.pallas_call(
        pair_kernel,
        out_shape=wire,
        in_specs=[VMEM, VMEM],
        out_specs=VMEM,
        compiler_params=params(8),
    )(kept, got)
    chips = [[2 * y + c for y in CHIPS] for c in range(2)]
    parts = lax.all_to_all(parts, "seq", 0, 0, tiled=True, axis_index_groups=chips)
    return pl.pallas_call(
        merge_kernel,
        out_shape=jax.ShapeDtypeStruct((leaf_count, steps, HEAD_DIM), jnp.bfloat16),
        in_specs=[VMEM],
        out_specs=VMEM,
        compiler_params=params(8),
    )(parts)


def solution(mesh):
    placed = (
        P("leaf", None, None),
        P(None, "seq", None),
        P(None, "leaf", "seq", None),
        P("leaf"),
        P("leaf", None),
    )
    return jax.shard_map(
        shards, mesh=mesh, in_specs=placed, out_specs=P("leaf", None, "seq"), check_vma=False
    )
```

```python
import functools

import jax
import jax.numpy as jnp
from jax import lax
from jax.experimental import pallas as pl
from jax.experimental.pallas import tpu as pltpu
from jax.sharding import PartitionSpec as P

HEADS = 16
KV_HEADS = 2
HEAD_DIM = 256
GROUP = HEADS // KV_HEADS
CHUNK = 256
LANES = 128
Z = 8
STRIDE = 2
FIRST_Z, FIRST_X, FIRST_MEMBER = 2, 2, 1
CHIPS = [4, 3, 2, 1, 0, 7, 6, 5]
WAITING_Z = 4
INVALID_KEY = 256.0
TOP = 32767.0
STATS = 32
POINTS = (2.0**18, 2.0**26, 2.0**23)

VMEM = pl.BlockSpec(memory_space=pltpu.VMEM)
HBM = pl.BlockSpec(memory_space=pltpu.HBM)


def in_hbm(*arrays):
    return [pltpu.with_memory_space_constraint(array, pltpu.HBM) for array in arrays]


def params(mib):
    return pltpu.CompilerParams(vmem_limit_bytes=mib * 1024 * 1024)


def fold(x, combine):
    parts = [x[:, i : i + LANES] for i in range(0, x.shape[1], LANES)]
    return functools.reduce(combine, parts)


def tall(x, reps):
    return jnp.concatenate([x] * reps, axis=0)


def node_counts(anc, ids, levels):
    counts = jnp.zeros((anc.shape[0], ids.shape[1]), jnp.float32)
    for level in levels:
        counts = counts + jnp.where(anc[:, level : level + 1] == ids, 1.0, 0.0)
    return counts


def group_query(q_ref, k):
    heads = range(k * GROUP, (k + 1) * GROUP)
    pieces = [q_ref[:, step, h * HEAD_DIM : (h + 1) * HEAD_DIM] for h in heads for step in range(q_ref.shape[1])]
    return (jnp.concatenate(pieces, axis=0) * (1.0 / 16.0)).astype(jnp.bfloat16)


def dot_nt(a, b):
    return lax.dot_general(a, b, (((1,), (1,)), ((), ())), preferred_element_type=jnp.float32)


def fetch(pairs, sems):
    copies = [pltpu.make_async_copy(src, dst, sems.at[i]) for i, (src, dst) in enumerate(pairs)]
    for copy in copies:
        copy.start()
    return copies


def waits():
    return lax.rem(lax.axis_index("leaf"), Z) < WAITING_Z


def first_kernel(inputs, outputs, scratch):
    lengths_hbm, node_hbm = inputs[0], inputs[3]
    out_ref, (node_ref, lengths_ref, sems) = outputs[0], scratch[:3]
    node_slots = lengths_hbm.shape[0]
    tokens = node_ref.shape[1]
    for copy in fetch([(node_hbm.at[:, node_slots - 1], node_ref), (lengths_hbm, lengths_ref)], sems):
        copy.wait()
    present = lax.axis_index("seq") * tokens < lengths_ref[node_slots - 1]
    keys = jnp.where(present, node_ref[0], jnp.bfloat16(INVALID_KEY))
    values = node_ref[1]
    for copy in range(out_ref.shape[0]):
        out_ref[copy, 0:tokens] = keys
        out_ref[copy, tokens : 2 * tokens] = values

    @pl.when(waits())
    def _():
        early_work(*inputs, *outputs[1:], *scratch[3:])


def second_kernel(inputs, outputs, scratch):
    part_ref, out_ref = inputs[0], outputs[0]
    for copy in range(out_ref.shape[0]):
        out_ref[copy] = part_ref[...]

    @pl.when(jnp.logical_not(waits()))
    def _():
        early_work(*inputs[1:], *outputs[1:], *scratch)


def early_work(
    lengths_hbm,
    anc_hbm,
    prompt_hbm,
    node_hbm,
    q_hbm,
    w_ref,
    row_ref,
    half_ref,
    count_ref,
    lengths_ref,
    anc_ref,
    prompt_ref,
    node_ref,
    q_raw_ref,
    q_ref,
    sems,
):
    copies = fetch(
        [
            (lengths_hbm, lengths_ref),
            (anc_hbm, anc_ref),
            (q_hbm, q_raw_ref),
            (node_hbm.at[0], node_ref),
            (prompt_hbm.at[0], prompt_ref),
            (prompt_hbm.at[1], half_ref.at[pl.ds(0, prompt_ref.shape[0])]),
        ]
        + [
            (node_hbm.at[1, n], half_ref.at[pl.ds(prompt_ref.shape[0] + n * node_ref.shape[1], node_ref.shape[1])])
            for n in range(node_ref.shape[0])
        ],
        sems,
    )
    level_count = anc_ref.shape[1]
    steps = q_ref.shape[1]
    node_slots, tokens, width = node_ref.shape
    node_cols = node_slots * tokens
    prompt_cols = prompt_ref.shape[0]
    shared_cols = count_ref.shape[1]
    copies[2].wait()
    q_ref[...] = q_raw_ref[...].astype(jnp.float32)
    for k in range(KV_HEADS):
        half_ref[prompt_cols + node_cols :, k * HEAD_DIM : (k + 1) * HEAD_DIM] = group_query(q_ref, k)
    copies[0].wait()
    copies[1].wait()
    anc = anc_ref[...]

    lane = lax.broadcasted_iota(jnp.int32, (1, shared_cols), 1)
    owner = owner_of(lane // tokens, shared_cols // tokens)
    count = node_counts(anc, owner * node_slots + node_slots - 1, range(level_count - 1))
    count_ref[...] = jnp.where(owner == lax.axis_index("leaf"), 0.0, count)

    lane = lax.broadcasted_iota(jnp.int32, (1, node_cols), 1)
    slot = lane // tokens
    position = lax.axis_index("seq") * tokens + lane % tokens
    length = jnp.zeros((1, node_cols), jnp.int32)
    for n in range(node_slots):
        length = jnp.where(slot == n, lengths_ref[n], length)
    ids = lax.axis_index("leaf") * node_slots + slot
    upper = node_counts(anc, ids, range(level_count - 1))
    own = node_counts(anc, ids, [level_count - 1])
    mult = []
    for step in range(steps):
        causal = jnp.where(position <= length - steps + step, 1.0, 0.0)
        mult.append(jnp.where(position < length, upper + own * causal, 0.0))
    mult = tall(jnp.concatenate(mult, axis=0), GROUP)
    copies[3].wait()
    copies[4].wait()

    for k in range(KV_HEADS):
        cols = slice(k * HEAD_DIM, (k + 1) * HEAD_DIM)
        query = half_ref[prompt_cols + node_cols :, cols]
        top = None
        for start in range(0, prompt_cols, CHUNK):
            s = dot_nt(query, prompt_ref[start : start + CHUNK, cols])
            w_ref[k, start // CHUNK] = s
            part = fold(s, jnp.maximum)
            top = part if top is None else jnp.maximum(top, part)
        s = dot_nt(query, node_ref[:, :, cols].reshape(node_cols, HEAD_DIM))
        s = jnp.where(mult > 0.0, s, -jnp.inf)
        w_ref[k, prompt_cols // CHUNK] = s
        top = jnp.max(jnp.maximum(top, fold(s, jnp.maximum)), axis=1, keepdims=True)
        total = jnp.zeros((s.shape[0], LANES), jnp.float32)
        for start in range(0, prompt_cols, CHUNK):
            w = jnp.exp(w_ref[k, start // CHUNK] - top)
            w_ref[k, start // CHUNK] = w
            total = total + fold(w, jnp.add)
        w = jnp.exp(w_ref[k, prompt_cols // CHUNK] - top) * mult
        w_ref[k, prompt_cols // CHUNK] = w
        total = total + fold(w, jnp.add)
        row_ref[k, :, LANES:] = jnp.broadcast_to(jnp.sum(total, axis=1, keepdims=True), total.shape)
        row_ref[k, :, :LANES] = jnp.broadcast_to(top, total.shape)
    for copy in copies[5:]:
        copy.wait()


def late_kernel(shared_ref, *refs):
    sets, outputs = (refs[:4], refs[4:8]), refs[8:]

    @pl.when(waits())
    def _():
        late_work(shared_ref, *sets[0], *outputs)

    @pl.when(jnp.logical_not(waits()))
    def _():
        late_work(shared_ref, *sets[1], *outputs)


def late_work(shared_ref, w_ref, row_ref, half_ref, count_ref, own_ref, out_ref):
    owners = shared_ref.shape[0]
    tokens = shared_ref.shape[1] // 2
    shared_cols = owners * tokens
    rows = w_ref.shape[2] // GROUP
    steps = rows // count_ref.shape[0]
    leaf_count = rows // steps
    chunks = w_ref.shape[1]
    early_cols = chunks * CHUNK
    count = count_ref[...]
    reps = GROUP * rows // count.shape[0]
    pick = jnp.where(lax.broadcasted_iota(jnp.int32, (16, HEAD_DIM), 1) == 0, 1.0, 0.0).astype(jnp.bfloat16)

    for k in range(KV_HEADS):
        cols = slice(k * HEAD_DIM, (k + 1) * HEAD_DIM)
        keys = shared_ref[:, 0:tokens, cols].reshape(shared_cols, HEAD_DIM)
        values = shared_ref[:, tokens : 2 * tokens, cols].reshape(shared_cols, HEAD_DIM)
        query = half_ref[early_cols:, cols]
        both = dot_nt(jnp.concatenate([query, pick], axis=0), keys)
        s, marks = both[: query.shape[0]], both[query.shape[0] : query.shape[0] + 1]
        mult = tall(jnp.where(marks < INVALID_KEY / 2, count, 0.0), reps)
        s = jnp.where(mult > 0.0, s, -jnp.inf)
        early_max = row_ref[k, :, :LANES]
        block_max = jnp.maximum(jnp.max(fold(s, jnp.maximum), axis=1, keepdims=True), early_max)
        scale = jnp.exp(early_max - block_max)
        w = jnp.exp(s - block_max[:, 0:1]) * mult
        total = jnp.sum(fold(w, jnp.add), axis=1, keepdims=True) + row_ref[k, :, LANES:] * scale
        acc = jnp.dot(w.astype(jnp.bfloat16), values, preferred_element_type=jnp.float32)
        wide = jnp.concatenate([scale, scale], axis=1)
        for c in range(chunks):
            w = (w_ref[k, c] * wide).astype(jnp.bfloat16)
            acc = acc + jnp.dot(w, half_ref[c * CHUNK : (c + 1) * CHUNK, cols], preferred_element_type=jnp.float32)

        core = lax.rem(lax.axis_index("seq"), 2)
        total = jnp.broadcast_to(total, block_max.shape)
        for pair in range(GROUP // 2):
            kept, sent = [], []
            for x in (acc, block_max, total):
                even = x[2 * pair * rows : (2 * pair + 1) * rows]
                odd = x[(2 * pair + 1) * rows : (2 * pair + 2) * rows]
                kept.append(jnp.where(core == 0, even, odd))
                sent.append(jnp.where(core == 0, odd, even))
            slot = CHIPS.index(k * (GROUP // 2) + pair)
            lane = lax.broadcasted_iota(jnp.int32, (rows, LANES), 1)
            data, fixed = to_wire(*sent)
            put(own_ref, slot, steps, kept[0], jnp.where(lane % STATS == 0, kept[1], kept[2]))
            put(out_ref, slot, steps, data, fixed)


def put(ref, slot, steps, data, stats):
    leaf_count = data.shape[0] // steps
    group = lax.broadcasted_iota(jnp.int32, (leaf_count, LANES), 1) // STATS
    joint = stats[:leaf_count]
    for step in range(steps):
        rows = slice(step * leaf_count, (step + 1) * leaf_count)
        ref[slot, :, step * HEAD_DIM : (step + 1) * HEAD_DIM] = data[rows]
        joint = jnp.where(group == step, stats[rows], joint)
    ref[slot, :, steps * HEAD_DIM :] = joint.astype(ref.dtype)


def to_wire(acc, block_max, total):
    reach = jnp.maximum(jnp.max(fold(jnp.abs(acc), jnp.maximum), axis=1, keepdims=True), 1e-30)
    data = jnp.round(acc * (TOP / reach)).astype(jnp.int32).astype(jnp.int16)
    lane = lax.broadcasted_iota(jnp.int32, block_max.shape, 1) % STATS
    log_total = jnp.log(total) * POINTS[1]
    log_reach = jnp.log(reach) * POINTS[2]
    value = jnp.where(lane < 2, block_max * POINTS[0], jnp.where(lane < 4, log_total, log_reach))
    value = jnp.round(value).astype(jnp.int32)
    return data, jnp.where(lane % 2 == 0, value >> 16, (value & 0xFFFF) - 0x8000)


def from_wire(stats):
    lane = lax.broadcasted_iota(jnp.int32, stats.shape, 1) % STATS
    unit = jnp.where(lane < 2, 1.0 / POINTS[0], jnp.where(lane < 4, 1.0 / POINTS[1], 1.0 / POINTS[2]))
    return ((stats << 16) + (pltpu.roll(stats, LANES - 1, 1) + 0x8000)).astype(jnp.float32) * unit


def factors(values, top):
    lane = lax.broadcasted_iota(jnp.int32, values.shape, 1) % STATS
    shift = values - top
    return jnp.exp(values + jnp.where(lane == 2, pltpu.roll(shift, 2, 1), pltpu.roll(shift, 4, 1)))


def pair_kernel(own_ref, other_ref, out_ref):
    slots, leaf_count, lanes = own_ref.shape
    steps = lanes // HEAD_DIM
    rows = slots * leaf_count
    shape = (rows, LANES)
    own = own_ref[:, :, steps * HEAD_DIM :].reshape(shape)
    other = from_wire(other_ref[:, :, steps * HEAD_DIM :].astype(jnp.int32).reshape(shape))
    top = jnp.maximum(own, other)
    own_scale = jnp.exp(own - top)
    other_scale = factors(other, top)
    total = own * pltpu.roll(own_scale, 2, 1) + other_scale
    group = lax.broadcasted_iota(jnp.int32, shape, 1) // STATS
    joint = jnp.zeros(shape, jnp.int32)
    for step in range(steps):
        first = step * STATS
        span = slice(step * HEAD_DIM, (step + 1) * HEAD_DIM)
        data = other_ref[:, :, span].astype(jnp.int32).reshape(rows, HEAD_DIM).astype(jnp.float32)
        acc = own_ref[:, :, span].reshape(rows, HEAD_DIM) * own_scale[:, first : first + 1]
        acc = acc + data * (other_scale[:, first + 4 : first + 5] * (1.0 / TOP))
        data, stats = to_wire(
            acc,
            jnp.broadcast_to(top[:, first : first + 1], shape),
            jnp.broadcast_to(total[:, first + 2 : first + 3], shape),
        )
        out_ref[:, :, span] = data.reshape(slots, leaf_count, HEAD_DIM)
        joint = jnp.where(group == step, stats, joint)
    out_ref[:, :, steps * HEAD_DIM :] = joint.astype(jnp.int16).reshape(slots, leaf_count, LANES)


def merge_kernel(parts_ref, out_ref):
    blocks = parts_ref.shape[0]
    steps = out_ref.shape[1]
    values = [from_wire(parts_ref[b, :, steps * HEAD_DIM :].astype(jnp.int32)) for b in range(blocks)]
    row_max = functools.reduce(jnp.maximum, values)
    scales = [factors(value, row_max) for value in values]
    denominator = functools.reduce(jnp.add, scales) * TOP
    for step in range(steps):
        first = step * STATS
        numerator = jnp.zeros((out_ref.shape[0], HEAD_DIM), jnp.float32)
        for b in range(blocks):
            data = parts_ref[b, :, step * HEAD_DIM : (step + 1) * HEAD_DIM].astype(jnp.int32).astype(jnp.float32)
            numerator = numerator + scales[b][:, first + 4 : first + 5] * data
        out_ref[:, step, :] = (numerator / denominator[:, first + 2 : first + 3]).astype(jnp.bfloat16)


def turned(items, start):
    items = list(items)
    return items[start:] + items[:start]


def gather_orders(owners):
    return turned(range(0, Z, STRIDE), FIRST_Z), turned(range(0, owners, Z), FIRST_X)


def owner_of(block, owners):
    along_z, along_x = gather_orders(owners)
    owner = 0
    for i, z in enumerate(along_z):
        owner = owner + jnp.where(block % (Z // STRIDE) == i, z, 0)
    members = turned([x + k for x in along_x for k in range(STRIDE)], FIRST_MEMBER)
    for i, m in enumerate(members):
        owner = owner + jnp.where(block // (Z // STRIDE) == i, m, 0)
    return owner


def gather_groups(owners):
    along_z, along_x = gather_orders(owners)
    first = [[x + z + k for k in along_z] for x in range(0, owners, Z) for z in range(STRIDE)]
    members = [x + k for x in along_x for k in range(STRIDE)]
    members = turned(members, FIRST_MEMBER)
    second = [[m + z for m in members] for z in range(0, Z, STRIDE)]
    return first, second


def shards(queries, prompt_kv, node_kv, node_lengths, ancestors):
    leaf_count, steps, feat_width = queries.shape
    node_slots, tokens = node_kv.shape[1:3]
    prompt_cols = prompt_kv.shape[1]
    width = KV_HEADS * HEAD_DIM
    rows = steps * leaf_count
    owners = lax.axis_size("leaf")

    first, second = gather_groups(owners)
    early_cols = prompt_cols + node_slots * tokens
    assert prompt_cols % CHUNK == 0 and node_slots * tokens == CHUNK and GROUP * rows == CHUNK
    arrays = in_hbm(node_lengths, ancestors, prompt_kv, node_kv, queries)
    early_shapes = (
        jax.ShapeDtypeStruct((KV_HEADS, early_cols // CHUNK, CHUNK, CHUNK), jnp.float32),
        jax.ShapeDtypeStruct((KV_HEADS, GROUP * rows, 2 * LANES), jnp.float32),
        jax.ShapeDtypeStruct((early_cols + GROUP * rows, width), jnp.bfloat16),
        jax.ShapeDtypeStruct((leaf_count, owners * tokens), jnp.float32),
    )
    early_scratch = [
        pltpu.SMEM((node_slots,), jnp.int32),
        pltpu.VMEM(ancestors.shape, jnp.int32),
        pltpu.VMEM((prompt_cols, width), jnp.bfloat16),
        pltpu.VMEM((node_slots, tokens, width), jnp.bfloat16),
        pltpu.VMEM(queries.shape, jnp.bfloat16),
        pltpu.VMEM(queries.shape, jnp.float32),
        pltpu.SemaphoreType.DMA((6 + node_slots,)),
    ]

    def stage_kernel(body, out_shape, scratch, *operands):
        ins, outs = len(operands), 1 + len(early_shapes)

        def kernel(*refs):
            body(refs[:ins], refs[ins : ins + outs], refs[ins + outs :])

        return pl.pallas_call(
            kernel,
            out_shape=(out_shape, *early_shapes),
            in_specs=[VMEM] * (ins - len(arrays)) + [HBM] * len(arrays),
            out_specs=(VMEM,) * outs,
            scratch_shapes=scratch,
            compiler_params=params(24),
        )(*operands)

    own, *before = stage_kernel(
        first_kernel,
        jax.ShapeDtypeStruct((len(first[0]), 2 * tokens, width), jnp.bfloat16),
        [
            pltpu.VMEM((2, tokens, width), jnp.bfloat16),
            pltpu.SMEM((node_slots,), jnp.int32),
            pltpu.SemaphoreType.DMA((2,)),
            *early_scratch,
        ],
        *arrays,
    )
    part = lax.all_to_all(own, "leaf", 0, 0, tiled=True, axis_index_groups=first)
    part_copies, *after = stage_kernel(
        second_kernel,
        jax.ShapeDtypeStruct((len(second[0]),) + part.shape, part.dtype),
        early_scratch,
        part,
        *arrays,
    )
    shared = lax.all_to_all(part_copies, "leaf", 0, 0, tiled=True, axis_index_groups=second)
    shared = shared.reshape(owners, 2 * tokens, width)

    seqs = lax.axis_size("seq")
    assert steps * STATS == LANES
    wire = jax.ShapeDtypeStruct((HEADS // 2, leaf_count, steps * HEAD_DIM + LANES), jnp.int16)
    kept, sent = pl.pallas_call(
        late_kernel,
        out_shape=(jax.ShapeDtypeStruct(wire.shape, jnp.float32), wire),
        in_specs=[VMEM] * 9,
        out_specs=(VMEM, VMEM),
        compiler_params=params(16),
    )(shared, *before, *after)

    got = lax.ppermute(sent, "seq", [(i, i ^ 1) for i in range(seqs)])
    parts = pl.pallas_call(
        pair_kernel,
        out_shape=wire,
        in_specs=[VMEM, VMEM],
        out_specs=VMEM,
        compiler_params=params(8),
    )(kept, got)
    chips = [[2 * y + c for y in CHIPS] for c in range(2)]
    parts = lax.all_to_all(parts, "seq", 0, 0, tiled=True, axis_index_groups=chips)
    return pl.pallas_call(
        merge_kernel,
        out_shape=jax.ShapeDtypeStruct((leaf_count, steps, HEAD_DIM), jnp.bfloat16),
        in_specs=[VMEM],
        out_specs=VMEM,
        compiler_params=params(8),
    )(parts)


def solution(mesh):
    placed = (
        P("leaf", None, None),
        P(None, "seq", None),
        P(None, "leaf", "seq", None),
        P("leaf"),
        P("leaf", None),
    )
    return jax.shard_map(
        shards, mesh=mesh, in_specs=placed, out_specs=P("leaf", None, "seq"), check_vma=False
    )
```
